32 devices in a mesh: rows: 4 (over y, x), seq: 8 (over z, core).
Axes of the slice: x: 2, y: 2, z: 4, core: 2. Of those that a mesh axis runs over, the one named last changes fastest.
Arguments:
- inputs: bfloat16 [4, 2048, 1024], P('rows', 'seq'), may hold values from -6 to 6
- memory: bfloat16 [4, 4704, 1024], P('rows', 'seq'), may hold values from -6 to 6
- out_grad: bfloat16 [4, 2048, 1024], P('rows', 'seq'), may hold values from -6 to 6
- segment_ids: int32 [4, 2048], P('rows'), may hold values from 0 to 7, never falling along the last dimension, each value on 1 to 1920 neighbouring positions
- page_order: int32 [4, 8], P('rows'), may hold values from 0 to 7, each once within a row
- norm1_gain: bfloat16 [1024], replicated, may hold values from 0.5 to 1.5
- norm1_bias: bfloat16 [1024], replicated, may hold values from -1 to 1
- qkv_weight: bfloat16 [1024, 3072], replicated, may hold values from -0.1875 to 0.1875
- qv_bias: bfloat16 [2048], replicated, may hold values from -1.5 to 1.5
- self_out_weight: bfloat16 [1024, 1024], replicated, may hold values from -0.75 to 0.75
- self_out_bias: bfloat16 [1024], replicated, may hold values from -1.5 to 1.5
- norm2_gain: bfloat16 [1024], replicated, may hold values from 0.5 to 1.5
- norm2_bias: bfloat16 [1024], replicated, may hold values from -1 to 1
- cross_q_weight: bfloat16 [1024, 1024], replicated, may hold values from -0.1875 to 0.1875
- cross_q_bias: bfloat16 [1024], replicated, may hold values from -1.5 to 1.5
- cross_kv_weight: bfloat16 [1024, 2048], replicated, may hold values from -0.1875 to 0.1875
- cross_v_bias: bfloat16 [1024], replicated, may hold values from -1.5 to 1.5
- cross_out_weight: bfloat16 [1024, 1024], replicated, may hold values from -0.75 to 0.75
- cross_out_bias: bfloat16 [1024], replicated, may hold values from -1.5 to 1.5
- norm3_gain: bfloat16 [1024], replicated, may hold values from 0.5 to 1.5
- norm3_bias: bfloat16 [1024], replicated, may hold values from -1 to 1
- fc1_weight: bfloat16 [1024, 4096], replicated, may hold values from -0.1875 to 0.1875
- fc1_bias: bfloat16 [4096], replicated, may hold values from -1.5 to 1.5
- fc2_weight: bfloat16 [4096, 1024], replicated, may hold values from -0.09375 to 0.09375
- fc2_bias: bfloat16 [1024], replicated, may hold values from -1.5 to 1.5
Outputs:
- layer_out: bfloat16 [4, 2048, 1024], P('rows', 'seq')
- input_grad: float32 [4, 2048, 1024], P('rows', 'seq')
- memory_grad: float32 [4, 4704, 1024], P('rows', 'seq')
- norm1_gain_grad: float32 [1024], P('seq')
- norm1_bias_grad: float32 [1024], P('seq')
- qkv_weight_grad: float32 [1024, 3072], P('seq')
- qv_bias_grad: float32 [2048], P('seq')
- self_out_weight_grad: float32 [1024, 1024], P('seq')
- self_out_bias_grad: float32 [1024], P('seq')
- norm2_gain_grad: float32 [1024], P('seq')
- norm2_bias_grad: float32 [1024], P('seq')
- cross_q_weight_grad: float32 [1024, 1024], P('seq')
- cross_q_bias_grad: float32 [1024], P('seq')
- cross_kv_weight_grad: float32 [1024, 2048], P('seq')
- cross_v_bias_grad: float32 [1024], P('seq')
- cross_out_weight_grad: float32 [1024, 1024], P('seq')
- cross_out_bias_grad: float32 [1024], P('seq')
- norm3_gain_grad: float32 [1024], P('seq')
- norm3_bias_grad: float32 [1024], P('seq')
- fc1_weight_grad: float32 [1024, 4096], P('seq')
- fc1_bias_grad: float32 [4096], P('seq')
- fc2_weight_grad: float32 [4096, 1024], P('seq')
- fc2_bias_grad: float32 [1024], P('seq')
The draws below stay inside these ranges and needn't reach their ends.
Inputs may be any that keep to these rules, and one draw needn't show every extreme that they name: `segment_ids`: along each row the segment ids never fall, every page number appears, and one page holds exactly 1920 tokens. `page_order`: each row is a permutation of the page numbers.
All inputs are finite; a program needn't handle non-finite values.
Results may differ from the reference program's by a relative error of at most 0.024.
Values may be sent and summed in bfloat16 or wider, within the bound.
A program may use at most 256 MiB of HBM per device.

```python
import math
import jax
import jax.numpy as jnp
import numpy as np
from jax import lax

D = 1024
HEADS = 16
FF = 4096
TOK_DEV = 256
PAGES = 8
PAGE_TOK = 588
ROWS = 4
LEN = 2048
MEM = 4704


def levels(own_key, shape, split, low, high):
    level, own = 1.0, jax.random.fold_in(own_key, 6)
    for position, blocks in split:
        steps = jnp.exp(jax.random.uniform(jax.random.fold_in(own, position), (blocks,), jnp.float32, low / len(split), high / len(split)))
        level = level * jnp.repeat(steps, shape[position] // blocks).reshape([-1 if axis == position else 1 for axis in range(len(shape))])
    return level


def profile(amount, total, bound, slope):
    portions = [(1 << 20) // math.isqrt(rank ** slope) + 1 for rank in range(2, amount + 1)]
    rest, counts = total - bound - (amount - 1), [1] * (amount - 1)
    while rest > 0:
        candidates = [i for i in range(amount - 1) if counts[i] < bound]
        pool, budget = sum([portions[i] for i in candidates]), rest
        for i in candidates:
            more = min(bound - counts[i], max(1, budget * portions[i] // pool), rest)
            counts[i] = counts[i] + more
            rest = rest - more
    return np.array([bound] + counts)


def uneven_parts(stream_key, number_of, total, reach, skew):
    if number_of == 2:
        one = jax.random.randint(stream_key, (), max(1, total - reach), min(reach, total - 1) + 1)
        return jnp.stack([one, total - one])
    tallies = jnp.asarray(profile(number_of, total, reach, skew), jnp.int32)
    couples = (number_of - 1) // 2
    source_of, sink = tallies[1:1 + 2 * couples:2], tallies[2:2 + 2 * couples:2]
    room = jnp.minimum(source_of - 1, reach - sink)
    moved = jax.random.randint(jax.random.fold_in(stream_key, 1), (couples,), 0, 1 << 20) % (room + 1)
    tallies = tallies.at[1:1 + 2 * couples:2].set(source_of - moved).at[2:2 + 2 * couples:2].set(sink + moved)
    return tallies[jax.random.permutation(jax.random.fold_in(stream_key, 2), number_of)]


def centred(stream_key, dims, deviation, reach, split=(), kind=jnp.bfloat16):
    loudness = levels(stream_key, dims, split, -0.22, 0.18) if split else 1.0
    entries = jax.random.normal(stream_key, dims, jnp.float32) * deviation * loudness
    return jnp.minimum(jnp.maximum(entries, -reach), reach).astype(kind)


def setup_inputs(seed: int = 0) -> dict:
    streams_of = jax.random.split(jax.random.key(seed), 26)
    inputs = centred(streams_of[0], (ROWS, LEN, D), 1.0, 6.0, ((0, 4), (1, 8)))
    memory = centred(streams_of[1], (ROWS, MEM, D), 1.0, 6.0, ((0, 4), (1, 8)))
    out_grad = centred(streams_of[2], (ROWS, LEN, D), 1.0, 6.0, ((0, 4), (1, 8)))
    segment_ids = jax.vmap(lambda own: jnp.searchsorted(jnp.cumsum(uneven_parts(own, PAGES, LEN, LEN - TOK_DEV // 2, 0)), jnp.arange(LEN), side="right"))(jax.random.split(streams_of[3], ROWS)).reshape((ROWS, LEN)).astype(jnp.int32)
    page_order = jax.vmap(lambda own: jax.random.permutation(own, PAGES))(jax.random.split(streams_of[4], ROWS)).reshape((ROWS, PAGES)).astype(jnp.int32)
    norm1_gain = jnp.clip(1.0 + 0.1 * jax.random.normal(streams_of[5], (D,), jnp.float32), 0.5, 1.5).astype(jnp.bfloat16)
    norm1_bias = centred(streams_of[6], (D,), 0.2, 1.0)
    qkv_weight = centred(streams_of[7], (D, 3 * D), D ** -0.5, 0.1875)
    qv_bias = centred(streams_of[8], (2 * D,), 0.3, 1.5)
    self_out_weight = centred(streams_of[9], (D, D), (D // 16) ** -0.5, 0.75)
    self_out_bias = centred(streams_of[10], (D,), 0.3, 1.5)
    norm2_gain = jnp.clip(1.0 + 0.1 * jax.random.normal(streams_of[11], (D,), jnp.float32), 0.5, 1.5).astype(jnp.bfloat16)
    norm2_bias = centred(streams_of[12], (D,), 0.2, 1.0)
    cross_q_weight = centred(streams_of[13], (D, D), D ** -0.5, 0.1875)
    cross_q_bias = centred(streams_of[14], (D,), 0.3, 1.5)
    cross_kv_weight = centred(streams_of[15], (D, 2 * D), D ** -0.5, 0.1875)
    cross_v_bias = centred(streams_of[16], (D,), 0.3, 1.5)
    cross_out_weight = centred(streams_of[17], (D, D), (D // 16) ** -0.5, 0.75)
    cross_out_bias = centred(streams_of[18], (D,), 0.3, 1.5)
    norm3_gain = jnp.clip(1.0 + 0.1 * jax.random.normal(streams_of[19], (D,), jnp.float32), 0.5, 1.5).astype(jnp.bfloat16)
    norm3_bias = centred(streams_of[20], (D,), 0.2, 1.0)
    fc1_weight = centred(streams_of[21], (D, FF), D ** -0.5, 0.1875)
    fc1_bias = centred(streams_of[22], (FF,), 0.3, 1.5)
    fc2_weight = centred(streams_of[23], (FF, D), FF ** -0.5, 0.09375)
    fc2_bias = centred(streams_of[24], (D,), 0.3, 1.5)
    return dict(inputs=inputs, memory=memory, out_grad=out_grad, segment_ids=segment_ids, page_order=page_order, norm1_gain=norm1_gain, norm1_bias=norm1_bias, qkv_weight=qkv_weight, qv_bias=qv_bias, self_out_weight=self_out_weight, self_out_bias=self_out_bias, norm2_gain=norm2_gain, norm2_bias=norm2_bias, cross_q_weight=cross_q_weight, cross_q_bias=cross_q_bias, cross_kv_weight=cross_kv_weight, cross_v_bias=cross_v_bias, cross_out_weight=cross_out_weight, cross_out_bias=cross_out_bias, norm3_gain=norm3_gain, norm3_bias=norm3_bias, fc1_weight=fc1_weight, fc1_bias=fc1_bias, fc2_weight=fc2_weight, fc2_bias=fc2_bias)


NEGATIVE = -1e+30
SCALE = 0.125
EPSILON = 1e-05
HIGHEST = lax.Precision.HIGHEST

@jax.custom_vjp
def low(v):
    return lax.optimization_barrier(v.astype(jnp.bfloat16)).astype(jnp.float32)

@jax.custom_vjp
def low_back(v):
    return v

def low_keep(v):
    return (low(v), None)

def low_pass(kept, grad):
    return (grad,)

def back_keep(v):
    return (v, None)

def back_low(kept, grad):
    return (low(grad),)
low.defvjp(low_keep, low_pass)
low_back.defvjp(back_keep, back_low)

def dual(value):
    return low(low_back(value))

def matmul(first, second):
    return jnp.dot(first, second, precision=HIGHEST, preferred_element_type=jnp.float32)

def norm_forward(values, gain, shift):
    center = values - lax.optimization_barrier(jnp.mean(values, axis=-1, keepdims=True))
    spread = lax.optimization_barrier(jnp.mean(center * center, axis=-1, keepdims=True))
    return center * lax.rsqrt(spread + EPSILON) * gain + shift

def gelu_exact(values):
    return jax.nn.gelu(values, approximate=False)

def attend(queries, keys_in, values_in, allowed_of, head_count):
    length, width = queries.shape
    head_depth = width // head_count
    block_rows = 512 if length % 512 == 0 else length
    key_heads = keys_in.reshape(keys_in.shape[0], head_count, head_depth)
    value_heads = values_in.reshape(values_in.shape[0], head_count, head_depth)

    def one_block(offset):
        query_block = lax.dynamic_slice_in_dim(queries, offset, block_rows, 0).reshape(block_rows, head_count, head_depth)
        scores = low_back(jnp.einsum('thd,nhd->htn', query_block, key_heads, precision=HIGHEST) * SCALE)
        allowed = allowed_of(offset, block_rows)
        prob_block = jax.nn.softmax(jnp.where(allowed[None], scores, NEGATIVE), axis=-1)
        mixed_out = jnp.einsum('htn,nhd->thd', low(prob_block), value_heads, precision=HIGHEST)
        return mixed_out.reshape(block_rows, width)
    offsets = jnp.arange(length // block_rows, dtype=jnp.int32) * block_rows
    return lax.map(jax.checkpoint(one_block), offsets).reshape(length, width)

def layer_row(row_in, row_mem, row_segs, row_order, weights):
    length, width = row_in.shape
    positions = jnp.arange(length, dtype=jnp.int32)
    mem_pages = jnp.repeat(row_order, PAGE_TOK)

    def self_allowed(offset, block_rows):
        query_segs = lax.dynamic_slice_in_dim(row_segs, offset, block_rows, 0)
        query_pos = offset + jnp.arange(block_rows, dtype=jnp.int32)
        return (query_segs[:, None] == row_segs[None, :]) & (positions[None, :] <= query_pos[:, None])

    def cross_allowed(offset, block_rows):
        query_segs = lax.dynamic_slice_in_dim(row_segs, offset, block_rows, 0)
        return query_segs[:, None] == mem_pages[None, :]
    normed_one = low(norm_forward(row_in, weights['norm1_gain'], weights['norm1_bias']))
    qkv_out = matmul(normed_one, weights['qkv_weight'])
    qv_shift = weights['qv_bias']
    queries = dual(qkv_out[:, :width] + qv_shift[:width])
    self_keys = dual(qkv_out[:, width:2 * width])
    self_values = dual(qkv_out[:, 2 * width:] + qv_shift[width:])
    attended = dual(attend(queries, self_keys, self_values, self_allowed, HEADS))
    resid_one = row_in + low_back(matmul(attended, weights['self_out_weight']) + weights['self_out_bias'])
    normed_two = low(norm_forward(resid_one, weights['norm2_gain'], weights['norm2_bias']))
    cross_queries = dual(matmul(normed_two, weights['cross_q_weight']) + weights['cross_q_bias'])
    mem_proj = matmul(row_mem, weights['cross_kv_weight'])
    cross_keys = dual(mem_proj[:, :width])
    cross_values = dual(mem_proj[:, width:] + weights['cross_v_bias'])
    cross_out = dual(attend(cross_queries, cross_keys, cross_values, cross_allowed, HEADS))
    resid_two = resid_one + low_back(matmul(cross_out, weights['cross_out_weight']) + weights['cross_out_bias'])
    normed_three = low(norm_forward(resid_two, weights['norm3_gain'], weights['norm3_bias']))
    pre_act = low_back(matmul(normed_three, weights['fc1_weight']) + weights['fc1_bias'])
    hidden_act = low(gelu_exact(pre_act))
    return resid_two + matmul(hidden_act, weights['fc2_weight']) + weights['fc2_bias']

def reference(inputs, memory, out_grad, segment_ids, page_order, norm1_gain, norm1_bias, qkv_weight, qv_bias, self_out_weight, self_out_bias, norm2_gain, norm2_bias, cross_q_weight, cross_q_bias, cross_kv_weight, cross_v_bias, cross_out_weight, cross_out_bias, norm3_gain, norm3_bias, fc1_weight, fc1_bias, fc2_weight, fc2_bias):
    weights = dict(norm1_gain=norm1_gain, norm1_bias=norm1_bias, qkv_weight=qkv_weight, qv_bias=qv_bias, self_out_weight=self_out_weight, self_out_bias=self_out_bias, norm2_gain=norm2_gain, norm2_bias=norm2_bias, cross_q_weight=cross_q_weight, cross_q_bias=cross_q_bias, cross_kv_weight=cross_kv_weight, cross_v_bias=cross_v_bias, cross_out_weight=cross_out_weight, cross_out_bias=cross_out_bias, norm3_gain=norm3_gain, norm3_bias=norm3_bias, fc1_weight=fc1_weight, fc1_bias=fc1_bias, fc2_weight=fc2_weight, fc2_bias=fc2_bias)
    weights = jax.tree.map(lambda leaf_value: leaf_value.astype(jnp.float32), weights)
    resid = inputs.astype(jnp.float32)
    mem_in = memory.astype(jnp.float32)

    def forward(resid_in, mem_rows, params):
        return lax.map(lambda row_items: layer_row(row_items[0], row_items[1], row_items[2], row_items[3], params), (resid_in, mem_rows, segment_ids, page_order))
    result, pullback = jax.vjp(forward, resid, mem_in, weights)
    input_grad, memory_grad, weight_grads = pullback(out_grad.astype(jnp.float32))
    return (result.astype(jnp.bfloat16), input_grad, memory_grad, weight_grads['norm1_gain'], weight_grads['norm1_bias'], weight_grads['qkv_weight'], weight_grads['qv_bias'], weight_grads['self_out_weight'], weight_grads['self_out_bias'], weight_grads['norm2_gain'], weight_grads['norm2_bias'], weight_grads['cross_q_weight'], weight_grads['cross_q_bias'], weight_grads['cross_kv_weight'], weight_grads['cross_v_bias'], weight_grads['cross_out_weight'], weight_grads['cross_out_bias'], weight_grads['norm3_gain'], weight_grads['norm3_bias'], weight_grads['fc1_weight'], weight_grads['fc1_bias'], weight_grads['fc2_weight'], weight_grads['fc2_bias'])
```

```python
import functools

import jax
import jax.numpy as jnp
from jax import lax
from jax.experimental import pallas as pl
from jax.experimental.pallas import tpu as pltpu
from jax.sharding import PartitionSpec as P

HEADS = 16
DEPTH = 64
PAGES = 8
PAGE_TOK = 588
PAGE_PAD = 640
SLOTS = 128
BLOCK = 256


NEGATIVE = -1e30
SCALE = 0.125
EPSILON = 1e-05
MESH = pl.DeviceIdType.MESH
VMEM_LIMIT = 56 * 1024 * 1024


def norm_forward(values, gain, shift):
    center = values - jnp.mean(values, axis=-1, keepdims=True)
    spread = jnp.mean(center * center, axis=-1, keepdims=True)
    return center * lax.rsqrt(spread + EPSILON) * gain + shift


def gelu_exact(values):
    return jax.nn.gelu(values, approximate=False)


def norm_backward(values, gain, shift, grad_normed):
    _, pullback = jax.vjp(norm_forward, values, gain, shift)
    return pullback(grad_normed)


def dot_plain(first, second):
    return jnp.dot(first, second, preferred_element_type=jnp.float32)


def dot_left(first, second):
    return lax.dot_general(
        first, second, (((0,), (0,)), ((), ())), preferred_element_type=jnp.float32
    )


def dot_right(first, second):
    return lax.dot_general(
        first, second, (((1,), (1,)), ((), ())), preferred_element_type=jnp.float32
    )


def low(values):
    return values.astype(jnp.bfloat16)


def wide(values):
    return values.astype(jnp.float32)


def place(index):
    return (lax.axis_index("rows"), index)


def gather_kernel(count, block_ref, whole_ref, own_sem, send_sem, recv_sem):
    rows = block_ref.shape[0]
    me = lax.axis_index("seq")
    chip, core, chips = me // 2, me % 2, count // 2
    other = me + 1 - 2 * core
    barrier = pltpu.get_barrier_semaphore()

    def block(index):
        return whole_ref.at[pl.ds(index * rows, rows)]

    pl.semaphore_signal(barrier, inc=1, device_id=place(other), device_id_type=MESH)

    @pl.when(chip > 0)
    def _():
        pl.semaphore_signal(barrier, inc=1, device_id=place(me - 2), device_id_type=MESH)

    @pl.when(chip < chips - 1)
    def _():
        pl.semaphore_signal(barrier, inc=1, device_id=place(me + 2), device_id_type=MESH)

    peers = 1 + jnp.where(chip > 0, 1, 0) + jnp.where(chip < chips - 1, 1, 0)
    pl.semaphore_wait(barrier, peers)
    own = pltpu.make_async_copy(block_ref, block(me), own_sem)
    own.start()

    def copy(lane, source, target, from_own=False):
        there = block(2 * source + core)
        return pltpu.make_async_remote_copy(
            src_ref=block_ref if from_own else there,
            dst_ref=there,
            send_sem=send_sem.at[lane, source],
            recv_sem=recv_sem.at[lane, source],
            device_id=place(target),
            device_id_type=MESH,
        )

    def right(source, from_own=False):
        return copy(0, source, me + 2, from_own)

    def left(source, from_own=False):
        return copy(1, source, me - 2, from_own)

    def across(source, from_own=False):
        return copy(2, source, other, from_own)

    @pl.when(chip < chips - 1)
    def _():
        right(chip, True).start()

    @pl.when(chip > 0)
    def _():
        left(chip, True).start()

    across(chip, True).start()
    for step in range(1, chips):

        @pl.when(chip - step >= 0)
        def _():
            right(chip - step).wait_recv()

            @pl.when(chip < chips - 1)
            def _():
                right(chip - step).start()

            across(chip - step).start()

        @pl.when(chip + step < chips)
        def _():
            left(chip + step).wait_recv()

            @pl.when(chip > 0)
            def _():
                left(chip + step).start()

            across(chip + step).start()

    own.wait()
    for source in range(chips):
        there = block(2 * source + 1 - core)
        pltpu.make_async_remote_copy(
            src_ref=there,
            dst_ref=there,
            send_sem=send_sem.at[2, source],
            recv_sem=recv_sem.at[2, source],
            device_id=place(other),
            device_id_type=MESH,
        ).wait_recv()
        across(source).wait_send()

        @pl.when((source <= chip) & (chip < chips - 1))
        def _():
            right(source).wait_send()

        @pl.when((source >= chip) & (chip > 0))
        def _():
            left(source).wait_send()


def gather_rows(block_in, count, collective_id):
    rows, width = block_in.shape
    return pl.pallas_call(
        functools.partial(gather_kernel, count),
        out_shape=jax.ShapeDtypeStruct((count * rows, width), block_in.dtype),
        in_specs=[pl.BlockSpec(memory_space=pl.ANY)],
        out_specs=pl.BlockSpec(memory_space=pl.ANY),
        scratch_shapes=[
            pltpu.SemaphoreType.DMA,
            pltpu.SemaphoreType.DMA((3, count // 2)),
            pltpu.SemaphoreType.DMA((3, count // 2)),
        ],
        compiler_params=pltpu.CompilerParams(
            collective_id=collective_id, has_side_effects=True
        ),
    )(block_in)


def exchange_kernel(count, parts, *refs):
    ins, outs = refs[: len(parts)], refs[len(parts) : 2 * len(parts)]
    own_sem, send_sem, recv_sem = refs[2 * len(parts) :]
    me = lax.axis_index("seq")
    barrier = pltpu.get_barrier_semaphore()
    for step in range(1, count):
        pl.semaphore_signal(
            barrier, inc=1, device_id=place(lax.rem(me + step, count)), device_id_type=MESH
        )
    pl.semaphore_wait(barrier, count - 1)
    own = []
    for index, same in enumerate(parts):
        source = ins[index] if same else ins[index].at[me]
        own.append(pltpu.make_async_copy(source, outs[index].at[me], own_sem.at[index]))
        own[-1].start()
    copies = []
    order = sorted(range(1, count), key=lambda step: -min(step, count - step))
    for step in order:
        target = lax.rem(me + step, count)
        for index, same in enumerate(parts):
            copies.append(
                pltpu.make_async_remote_copy(
                    src_ref=ins[index] if same else ins[index].at[target],
                    dst_ref=outs[index].at[me],
                    send_sem=send_sem.at[index, step],
                    recv_sem=recv_sem.at[index, step],
                    device_id=place(target),
                    device_id_type=MESH,
                )
            )
            copies[-1].start()
    for copy in copies:
        copy.wait()
    for copy in own:
        copy.wait()


def exchange(arrays, parts, count, collective_id):
    shapes = [
        jax.ShapeDtypeStruct(
            (count,) + (array.shape if same else array.shape[1:]), array.dtype
        )
        for array, same in zip(arrays, parts)
    ]
    return pl.pallas_call(
        functools.partial(exchange_kernel, count, parts),
        out_shape=shapes,
        in_specs=[pl.BlockSpec(memory_space=pl.ANY)] * len(arrays),
        out_specs=[pl.BlockSpec(memory_space=pl.ANY)] * len(arrays),
        scratch_shapes=[
            pltpu.SemaphoreType.DMA((len(arrays),)),
            pltpu.SemaphoreType.DMA((len(arrays), count)),
            pltpu.SemaphoreType.DMA((len(arrays), count)),
        ],
        compiler_params=pltpu.CompilerParams(
            collective_id=collective_id, has_side_effects=True
        ),
    )(*arrays)


def head_lanes(width):
    return lax.broadcasted_iota(jnp.int32, (1, width), 1) // DEPTH


def pick_head(values, head, width):
    if width == DEPTH:
        return values
    return jnp.where(head_lanes(width) == head, values, jnp.zeros_like(values))


def self_forward_kernel(qkv_ref, start_ref, out_ref, stat_ref):
    length, width = out_ref.shape
    heads = width // DEPTH
    blocks = length // BLOCK
    for index in range(blocks):
        rows = pl.ds(index * BLOCK, BLOCK)
        keys_end = (index + 1) * BLOCK
        query = qkv_ref[rows, 0:width]
        begin = start_ref[rows, :]
        position = index * BLOCK + lax.broadcasted_iota(jnp.int32, (BLOCK, 1), 0)
        if index == blocks - 1 or index <= 1:
            cuts = [(0, keys_end)]
        else:
            cuts = [(0, BLOCK), (BLOCK, index * BLOCK), (index * BLOCK, keys_end)]
        outs, stats = [], []
        for head in range(heads):
            query_head = pick_head(query, head, width) * jnp.bfloat16(SCALE)
            scores = []
            for low_end, high_end in cuts:
                part = dot_right(query_head, qkv_ref[low_end:high_end, width : 2 * width])
                if low_end == 0 or high_end == keys_end:
                    column = low_end + lax.broadcasted_iota(jnp.int32, part.shape, 1)
                    allowed = column >= begin
                    if high_end == keys_end:
                        allowed = allowed & (column <= position)
                    part = jnp.where(allowed, part, NEGATIVE)
                scores.append(part)
            top = functools.reduce(
                jnp.maximum, [jnp.max(part, axis=-1, keepdims=True) for part in scores]
            )
            total, mixed = 0.0, 0.0
            for (low_end, high_end), part in zip(cuts, scores):
                weight = jnp.exp(part - top)
                total = total + jnp.sum(weight, axis=-1, keepdims=True)
                mixed = mixed + dot_plain(
                    low(weight), qkv_ref[low_end:high_end, 2 * width : 3 * width]
                )
            outs.append(mixed / total)
            stats.append(top + jnp.log(total))
        merged = outs[0]
        for head in range(1, heads):
            merged = jnp.where(head_lanes(width) == head, outs[head], merged)
        out_ref[rows, :] = low(merged)
        stat_ref[rows, :] = jnp.concatenate(stats, axis=1)


def self_forward(qkv, begins):
    length, width = qkv.shape[0], qkv.shape[1] // 3
    heads = width // DEPTH
    return pl.pallas_call(
        self_forward_kernel,
        out_shape=(
            jax.ShapeDtypeStruct((length, width), jnp.bfloat16),
            jax.ShapeDtypeStruct((length, heads), jnp.float32),
        ),
        in_specs=[pl.BlockSpec(memory_space=pltpu.VMEM)] * 2,
        out_specs=[pl.BlockSpec(memory_space=pltpu.VMEM)] * 2,
        compiler_params=pltpu.CompilerParams(vmem_limit_bytes=VMEM_LIMIT),
    )(qkv, begins[:, None])


def self_backward_kernel(qkv_ref, out_ref, grad_ref, start_ref, stat_ref, dqkv_ref, dk_ref, dv_ref):
    length, width = out_ref.shape
    heads = width // DEPTH
    blocks = length // BLOCK
    dk_ref[...] = jnp.zeros_like(dk_ref)
    dv_ref[...] = jnp.zeros_like(dv_ref)

    def query_block(index, carry):
        rows = pl.ds(pl.multiple_of(index * BLOCK, BLOCK), BLOCK)
        query = qkv_ref[rows, 0:width]
        grad = grad_ref[rows, :]
        product = (wide(grad) * wide(out_ref[rows, :])).T
        begin = start_ref[:, rows]
        position = index * BLOCK + lax.broadcasted_iota(jnp.int32, (1, BLOCK), 1)
        query_heads = [pick_head(query, head, width) * jnp.bfloat16(SCALE) for head in range(heads)]
        grad_heads = [pick_head(grad, head, width) for head in range(heads)]
        stats = [stat_ref[head : head + 1, rows] for head in range(heads)]
        deltas = [
            jnp.sum(product[head * DEPTH : (head + 1) * DEPTH, :], axis=0, keepdims=True)
            for head in range(heads)
        ]

        def key_block(key_index, sums):
            keys = pl.ds(pl.multiple_of(key_index * BLOCK, BLOCK), BLOCK)
            key = qkv_ref[keys, width : 2 * width]
            value = qkv_ref[keys, 2 * width : 3 * width]
            row = key_index * BLOCK + lax.broadcasted_iota(jnp.int32, (BLOCK, 1), 0)
            allowed = (row >= begin) & (row <= position)
            dk_part, dv_part, found = 0.0, 0.0, []
            for head in range(heads):
                scores = jnp.where(allowed, dot_right(key, query_heads[head]), NEGATIVE)
                prob = jnp.exp(scores - stats[head])
                dv_part = dv_part + dot_plain(low(prob), grad_heads[head])
                grad_prob = dot_right(value, grad_heads[head])
                grad_score = low(prob * (grad_prob - deltas[head]))
                dk_part = dk_part + dot_plain(grad_score, query_heads[head])
                found.append(sums[head] + dot_left(grad_score, key))
            dk_ref[keys, :] += dk_part
            dv_ref[keys, :] += dv_part
            return tuple(found)

        zero = tuple(jnp.zeros((BLOCK, width), jnp.float32) for _ in range(heads))
        sums = lax.fori_loop(0, index + 1, key_block, zero)
        merged = sums[0]
        for head in range(1, heads):
            merged = jnp.where(head_lanes(width) == head, sums[head], merged)
        dqkv_ref[rows, 0:width] = low(merged * SCALE)
        return carry

    lax.fori_loop(0, blocks, query_block, 0)
    dqkv_ref[:, width : 2 * width] = low(dk_ref[...])
    dqkv_ref[:, 2 * width : 3 * width] = low(dv_ref[...])


def self_backward(qkv, out, grad, begins, stats):
    length, width = out.shape
    return pl.pallas_call(
        self_backward_kernel,
        out_shape=jax.ShapeDtypeStruct((length, 3 * width), jnp.bfloat16),
        in_specs=[pl.BlockSpec(memory_space=pltpu.VMEM)] * 5,
        out_specs=pl.BlockSpec(memory_space=pltpu.VMEM),
        scratch_shapes=[pltpu.VMEM((length, width), jnp.float32)] * 2,
        compiler_params=pltpu.CompilerParams(vmem_limit_bytes=VMEM_LIMIT),
    )(qkv, out, grad, begins[None, :], stats.T)


def cross_forward_kernel(query_ref, key_ref, value_ref, own_key_ref, own_value_ref, out_ref, stat_ref):
    tokens = query_ref.shape[0] - SLOTS
    width = query_ref.shape[1]
    for begin, size, keys, values in (
        (0, tokens, key_ref, value_ref),
        (tokens, SLOTS, own_key_ref, own_value_ref),
    ):
        query = query_ref[begin : begin + size, :]
        outs = []
        for head in range(width // DEPTH):
            query_head = pick_head(query, head, width) * jnp.bfloat16(SCALE)
            scores = dot_right(query_head, keys[...])
            column = lax.broadcasted_iota(jnp.int32, scores.shape, 1)
            scores = jnp.where(column < PAGE_TOK, scores, NEGATIVE)
            top = jnp.max(scores, axis=-1, keepdims=True)
            weight = jnp.exp(scores - top)
            total = jnp.sum(weight, axis=-1, keepdims=True)
            outs.append(dot_plain(low(weight), values[...]) / total)
            stat_ref[0, begin : begin + size, head : head + 1] = top + jnp.log(total)
        merged = outs[0]
        for head in range(1, len(outs)):
            merged = jnp.where(head_lanes(width) == head, outs[head], merged)
        out_ref[begin : begin + size, :] = low(merged)


def cross_forward(query, kv_big, kv_own):
    rows, features = query.shape
    pair = 2 * DEPTH
    steps = features // pair
    tall = pl.BlockSpec((rows, pair), lambda i: (0, i))
    keys = pl.BlockSpec((PAGE_PAD, pair), lambda i: (0, i))
    values = pl.BlockSpec((PAGE_PAD, pair), lambda i: (0, i + steps))
    return pl.pallas_call(
        cross_forward_kernel,
        grid=(steps,),
        out_shape=(
            jax.ShapeDtypeStruct((rows, features), jnp.bfloat16),
            jax.ShapeDtypeStruct((steps, rows, 2), jnp.float32),
        ),
        in_specs=[tall, keys, values, keys, values],
        out_specs=[tall, pl.BlockSpec((1, rows, 2), lambda i: (i, 0, 0))],
        compiler_params=pltpu.CompilerParams(vmem_limit_bytes=VMEM_LIMIT),
    )(query, kv_big, kv_big, kv_own, kv_own)


def cross_backward_kernel(
    query_ref,
    key_ref,
    value_ref,
    own_key_ref,
    own_value_ref,
    out_ref,
    grad_ref,
    stat_ref,
    dq_ref,
    dk_ref,
    dv_ref,
    own_dk_ref,
    own_dv_ref,
):
    tokens = query_ref.shape[0] - SLOTS
    width = query_ref.shape[1]
    row = lax.broadcasted_iota(jnp.int32, (PAGE_PAD, 1), 0)
    for begin, size, keys, values, dk_out, dv_out in (
        (0, tokens, key_ref, value_ref, dk_ref, dv_ref),
        (tokens, SLOTS, own_key_ref, own_value_ref, own_dk_ref, own_dv_ref),
    ):
        rows = slice(begin, begin + size)
        query, grad = query_ref[rows, :], grad_ref[rows, :]
        product = (wide(grad) * wide(out_ref[rows, :])).T
        dk_sum, dv_sum, found = 0.0, 0.0, []
        for head in range(width // DEPTH):
            query_head = pick_head(query, head, width) * jnp.bfloat16(SCALE)
            grad_head = pick_head(grad, head, width)
            delta = jnp.sum(product[head * DEPTH : (head + 1) * DEPTH, :], axis=0, keepdims=True)
            scores = dot_right(keys[...], query_head)
            scores = jnp.where(row < PAGE_TOK, scores, NEGATIVE)
            prob = jnp.exp(scores - stat_ref[0, head : head + 1, rows])
            dv_sum = dv_sum + dot_plain(low(prob), grad_head)
            grad_prob = dot_right(values[...], grad_head)
            grad_score = low(prob * (grad_prob - delta))
            dk_sum = dk_sum + dot_plain(grad_score, query_head)
            found.append(dot_left(grad_score, keys[...]))
        merged = found[0]
        for head in range(1, len(found)):
            merged = jnp.where(head_lanes(width) == head, found[head], merged)
        dq_ref[rows, :] = low(merged * SCALE)
        dk_out[...] = low(dk_sum)
        dv_out[...] = low(dv_sum)


def cross_backward(query, kv_big, kv_own, out, grad, stats):
    rows, features = query.shape
    pair = 2 * DEPTH
    steps = features // pair
    tall = pl.BlockSpec((rows, pair), lambda i: (0, i))
    keys = pl.BlockSpec((PAGE_PAD, pair), lambda i: (0, i))
    values = pl.BlockSpec((PAGE_PAD, pair), lambda i: (0, i + steps))
    page = jax.ShapeDtypeStruct((PAGE_PAD, features), jnp.bfloat16)
    return pl.pallas_call(
        cross_backward_kernel,
        grid=(steps,),
        out_shape=(jax.ShapeDtypeStruct((rows, features), jnp.bfloat16), page, page, page, page),
        in_specs=[
            tall,
            keys,
            values,
            keys,
            values,
            tall,
            tall,
            pl.BlockSpec((1, 2, rows), lambda i: (i, 0, 0)),
        ],
        out_specs=[tall, keys, keys, keys, keys],
        compiler_params=pltpu.CompilerParams(vmem_limit_bytes=VMEM_LIMIT),
    )(query, kv_big, kv_big, kv_own, kv_own, out, grad, stats.transpose(0, 2, 1))


def body(
    inputs,
    memory,
    out_grad,
    segment_ids,
    page_order,
    norm1_gain,
    norm1_bias,
    qkv_weight,
    qv_bias,
    self_out_weight,
    self_out_bias,
    norm2_gain,
    norm2_bias,
    cross_q_weight,
    cross_q_bias,
    cross_kv_weight,
    cross_v_bias,
    cross_out_weight,
    cross_out_bias,
    norm3_gain,
    norm3_bias,
    fc1_weight,
    fc1_bias,
    fc2_weight,
    fc2_bias,
):
    tokens, features = inputs.shape[1:]
    count = lax.axis_size("seq")
    me = lax.axis_index("seq")
    length = tokens * count
    width = features // count
    mem_rows = memory.shape[1]
    sharers = PAGE_TOK // mem_rows
    row_segs = segment_ids[0]
    row_pages = page_order[0]
    gain_one, shift_one = wide(norm1_gain), wide(norm1_bias)
    gain_two, shift_two = wide(norm2_gain), wide(norm2_bias)
    gain_three, shift_three = wide(norm3_gain), wide(norm3_bias)

    page_sizes = jnp.sum(row_segs[None, :] == jnp.arange(PAGES)[:, None], axis=1)
    page_starts = jnp.cumsum(page_sizes) - page_sizes
    begins = sum(
        jnp.where(row_segs == page, page_starts[page], 0) for page in range(PAGES)
    ).astype(jnp.int32)
    big_page = row_segs[length // 2]
    big_start = jnp.sum(row_segs < big_page)
    own_page = lax.dynamic_index_in_dim(row_pages, me // sharers, 0, keepdims=False)
    slot = jnp.arange(SLOTS)
    in_front = (slot < big_start)[:, None]
    slot_segs = jnp.where(slot < big_start, row_segs[:SLOTS], row_segs[length - SLOTS :])
    slot_mine = (slot_segs == own_page) & (slot * sharers // SLOTS == me % sharers)
    home_segs = lax.dynamic_slice_in_dim(row_segs, me * tokens, tokens, 0)
    active = jnp.concatenate((home_segs == big_page, slot_mine))[:, None]
    is_first, is_last = me == 0, me == count - 1

    def slots_of(front, back):
        return jnp.where(in_front, front, back)

    mem_own = memory[0]
    mem_page = mem_own
    if sharers > 1:
        groups = [[g * sharers + s for s in range(sharers)] for g in range(count // sharers)]
        mem_page = lax.all_gather(mem_own, "seq", axis=0, tiled=True, axis_index_groups=groups)
    mem_page = jnp.pad(mem_page, ((0, PAGE_PAD - PAGE_TOK), (0, 0)))
    gives_big = (own_page == big_page) & (me % sharers == 0)
    ends_grad = jnp.where(
        is_first, out_grad[0, :SLOTS], jnp.zeros((SLOTS, features), jnp.bfloat16)
    ), jnp.where(is_last, out_grad[0, tokens - SLOTS :], jnp.zeros((SLOTS, features), jnp.bfloat16))
    mem_big, front_grad, back_grad = lax.psum(
        (jnp.where(gives_big, mem_page, jnp.zeros_like(mem_page)), *ends_grad), "seq"
    )

    x_own = inputs[0]
    x_all = gather_rows(x_own, count, 0)
    qkv_own_weight = jnp.concatenate(
        [
            lax.dynamic_slice_in_dim(qkv_weight, part * features + me * width, width, 1)
            for part in range(3)
        ],
        axis=1,
    )
    qkv_own_bias = jnp.concatenate(
        (
            lax.dynamic_slice_in_dim(qv_bias, me * width, width, 0),
            jnp.zeros((width,), jnp.bfloat16),
            lax.dynamic_slice_in_dim(qv_bias, features + me * width, width, 0),
        )
    )
    normed_all = low(norm_forward(wide(x_all), gain_one, shift_one))
    qkv = low(dot_plain(normed_all, qkv_own_weight) + wide(qkv_own_bias))
    mixed, mixed_stats = self_forward(qkv, begins)
    blocks_mixed, ends_mixed = exchange(
        (
            mixed.reshape(count, tokens, width),
            jnp.concatenate((mixed[:SLOTS], mixed[length - SLOTS :])),
        ),
        (False, True),
        count,
        1,
    )

    def beside(blocks):
        return blocks.transpose(1, 0, 2).reshape(blocks.shape[1], -1)

    attended = jnp.concatenate(
        (
            beside(blocks_mixed),
            slots_of(beside(ends_mixed[:, :SLOTS]), beside(ends_mixed[:, SLOTS:])),
        )
    )
    resid = wide(
        jnp.concatenate((x_own, slots_of(x_all[:SLOTS], x_all[length - SLOTS :])))
    )
    resid_one = resid + dot_plain(attended, self_out_weight) + wide(self_out_bias)
    normed_two = low(norm_forward(resid_one, gain_two, shift_two))
    cross_queries = low(dot_plain(normed_two, cross_q_weight) + wide(cross_q_bias))
    kv_shift = jnp.concatenate((jnp.zeros((features,), jnp.float32), wide(cross_v_bias)))
    kv_big = low(dot_plain(mem_big, cross_kv_weight) + kv_shift)
    kv_own = low(dot_plain(mem_page, cross_kv_weight) + kv_shift)
    cross_low, cross_stats = cross_forward(cross_queries, kv_big, kv_own)
    resid_two = resid_one + dot_plain(cross_low, cross_out_weight) + wide(cross_out_bias)
    normed_three = low(norm_forward(resid_two, gain_three, shift_three))
    pre_act = dot_plain(normed_three, fc1_weight) + wide(fc1_bias)
    hidden_act = low(gelu_exact(pre_act))
    final = low(resid_two + dot_plain(hidden_act, fc2_weight) + wide(fc2_bias))

    grad_out = jnp.concatenate((out_grad[0], slots_of(front_grad, back_grad)))
    grad_out = jnp.where(active, grad_out, jnp.zeros_like(grad_out))
    grad_act = dot_right(grad_out, fc2_weight)
    _, gelu_pull = jax.vjp(gelu_exact, pre_act)
    grad_pre = low(gelu_pull(grad_act)[0])
    grad_fc2_w = dot_left(hidden_act, grad_out)
    grad_fc2_b = jnp.sum(wide(grad_out), axis=0)
    grad_fc1_w = dot_left(normed_three, grad_pre)
    grad_fc1_b = jnp.sum(wide(grad_pre), axis=0)
    grad_two_norm, grad_gain_three, grad_shift_three = norm_backward(
        resid_two, gain_three, shift_three, dot_right(grad_pre, fc1_weight)
    )
    grad_resid_two = wide(grad_out) + grad_two_norm
    grad_branch_two = low(grad_resid_two)
    grad_co_w = dot_left(cross_low, grad_branch_two)
    grad_co_b = jnp.sum(wide(grad_branch_two), axis=0)
    grad_cross_low = low(dot_right(grad_branch_two, cross_out_weight))
    grad_cross_q, big_dk, big_dv, own_dk, own_dv = cross_backward(
        cross_queries, kv_big, kv_own, cross_low, grad_cross_low, cross_stats
    )
    big_dk, big_dv = lax.psum((big_dk, big_dv), "seq")
    grad_ckv = jnp.where(
        gives_big,
        jnp.concatenate((big_dk, big_dv), axis=1),
        jnp.concatenate((own_dk, own_dv), axis=1),
    )[:PAGE_TOK]
    if sharers > 1:
        grad_ckv = lax.psum_scatter(
            grad_ckv, "seq", scatter_dimension=0, tiled=True, axis_index_groups=groups
        )
    grad_ckv_w = dot_left(mem_own, grad_ckv)
    grad_cv_b = jnp.sum(wide(grad_ckv[:, features:]), axis=0)
    memory_grad = dot_right(grad_ckv, cross_kv_weight)[None]

    grad_cq_w = dot_left(normed_two, grad_cross_q)
    grad_cq_b = jnp.sum(wide(grad_cross_q), axis=0)
    grad_one_norm, grad_gain_two, grad_shift_two = norm_backward(
        resid_one, gain_two, shift_two, dot_right(grad_cross_q, cross_q_weight)
    )
    grad_resid_one = grad_resid_two + grad_one_norm
    grad_branch_one = low(grad_resid_one)
    grad_o_w = dot_left(attended, grad_branch_one)
    grad_o_b = jnp.sum(wide(grad_branch_one), axis=0)
    grad_attended = low(dot_right(grad_branch_one, self_out_weight))
    by_device = grad_attended.reshape(-1, count, width).transpose(1, 0, 2)
    blocks_grad, slots_grad = exchange(
        (by_device[:, :tokens], by_device[:, tokens:]), (False, False), count, 2
    )
    slots_grad = low(jnp.sum(wide(slots_grad), axis=0))
    grad_mixed = blocks_grad.reshape(length, width)
    no_slots = jnp.zeros_like(slots_grad)
    grad_mixed = jnp.concatenate(
        (
            grad_mixed[:SLOTS] + jnp.where(in_front, slots_grad, no_slots),
            grad_mixed[SLOTS : length - SLOTS],
            grad_mixed[length - SLOTS :] + jnp.where(in_front, no_slots, slots_grad),
        )
    )
    dqkv = self_backward(qkv, mixed, grad_mixed, begins, mixed_stats)

    slot_results = lax.psum(
        (
            jnp.where(active[tokens:], final[tokens:], jnp.zeros_like(final[tokens:])),
            low(grad_resid_one[tokens:]),
        ),
        "seq",
    )

    def at_home(own, returned, keep):
        front = is_first & in_front
        back = is_last & ~in_front
        head = jnp.where(front, returned.astype(own.dtype), own[:SLOTS])
        tail = jnp.where(back, returned.astype(own.dtype), own[tokens - SLOTS :])
        return jnp.concatenate((head, own[SLOTS : tokens - SLOTS], tail))

    layer_out = at_home(final[:tokens], slot_results[0], False)[None]
    grad_home = at_home(grad_resid_one[:tokens], slot_results[1], False)

    grad_qkv_w_own = low(dot_left(normed_all, dqkv))
    (blocks_dqkv,) = exchange((dqkv.reshape(count, tokens, 3 * width),), (False,), count, 3)
    grad_qkv = blocks_dqkv.reshape(count, tokens, 3, width).transpose(1, 2, 0, 3)
    grad_qkv = grad_qkv.reshape(tokens, 3 * features)
    grad_in_norm, grad_gain_one, grad_shift_one = norm_backward(
        wide(x_own), gain_one, shift_one, dot_right(grad_qkv, qkv_weight)
    )
    input_grad = (grad_home + grad_in_norm)[None]
    column_sums = jnp.sum(wide(grad_qkv), axis=0)
    grad_qv_b = jnp.concatenate((column_sums[:features], column_sums[2 * features :]))

    qkv_w_share = lax.all_to_all(grad_qkv_w_own, "seq", 0, 1, tiled=True)
    qkv_w_share = (
        qkv_w_share.reshape(-1, count, 3, width).transpose(0, 2, 1, 3).reshape(-1, 3 * features)
    )
    shares = [
        lax.psum_scatter(low(term), "seq", scatter_dimension=0, tiled=True)
        for term in (grad_o_w, grad_cq_w, grad_ckv_w, grad_co_w, grad_fc1_w, grad_fc2_w)
    ]
    shares = lax.psum((qkv_w_share, *shares), "rows")
    qkv_w, o_w, cq_w, ckv_w, co_w, fc1_w, fc2_w = [wide(share) for share in shares]
    vectors = (
        grad_gain_one,
        grad_shift_one,
        grad_qv_b,
        grad_o_b,
        grad_gain_two,
        grad_shift_two,
        grad_cq_b,
        grad_cv_b,
        grad_co_b,
        grad_gain_three,
        grad_shift_three,
        grad_fc1_b,
        grad_fc2_b,
    )
    joined = lax.psum(
        jnp.concatenate([vector.reshape(count, -1) for vector in vectors], axis=1),
        ("rows", "seq"),
    )
    joined = lax.dynamic_index_in_dim(joined, me, 0, keepdims=False)
    pieces, offset = [], 0
    for vector in vectors:
        size = vector.shape[0] // count
        pieces.append(joined[offset : offset + size])
        offset += size
    g1, s1, qvb, ob, g2, s2, cqb, cvb, cob, g3, s3, f1b, f2b = pieces
    return (
        layer_out,
        input_grad,
        memory_grad,
        g1,
        s1,
        qkv_w,
        qvb,
        o_w,
        ob,
        g2,
        s2,
        cq_w,
        cqb,
        ckv_w,
        cvb,
        co_w,
        cob,
        g3,
        s3,
        fc1_w,
        f1b,
        fc2_w,
        f2b,
    )


def solution(mesh):
    split = P("rows", "seq", None)
    in_specs = (split, split, split, P("rows", None), P("rows", None)) + (P(),) * 20
    vector, matrix = P("seq"), P("seq", None)
    out_specs = (split, split, split) + (
        vector,
        vector,
        matrix,
        vector,
        matrix,
        vector,
        vector,
        vector,
        matrix,
        vector,
        matrix,
        vector,
        matrix,
        vector,
        vector,
        vector,
        matrix,
        vector,
        matrix,
        vector,
    )
    return jax.shard_map(body, mesh=mesh, in_specs=in_specs, out_specs=out_specs, check_vma=False)
```

```python
import functools

import jax
import jax.numpy as jnp
from jax import lax
from jax.experimental import pallas as pl
from jax.experimental.pallas import tpu as pltpu
from jax.sharding import PartitionSpec as P

HEADS = 16
DEPTH = 64
PAGES = 8
PAGE_TOK = 588
PAGE_PAD = 640
SLOTS = 128
BLOCK = 256


NEGATIVE = -1e30
SCALE = 0.125
EPSILON = 1e-05
MESH = pl.DeviceIdType.MESH
VMEM_LIMIT = 56 * 1024 * 1024


def norm_forward(values, gain, shift):
    center = values - jnp.mean(values, axis=-1, keepdims=True)
    spread = jnp.mean(center * center, axis=-1, keepdims=True)
    return center * lax.rsqrt(spread + EPSILON) * gain + shift


def gelu_exact(values):
    return jax.nn.gelu(values, approximate=False)


def norm_backward(values, gain, shift, grad_normed):
    _, pullback = jax.vjp(norm_forward, values, gain, shift)
    return pullback(grad_normed)


def dot_plain(first, second):
    return jnp.dot(first, second, preferred_element_type=jnp.float32)


def dot_left(first, second):
    return lax.dot_general(
        first, second, (((0,), (0,)), ((), ())), preferred_element_type=jnp.float32
    )


def dot_right(first, second):
    return lax.dot_general(
        first, second, (((1,), (1,)), ((), ())), preferred_element_type=jnp.float32
    )


def low(values):
    return values.astype(jnp.bfloat16)


def wide(values):
    return values.astype(jnp.float32)


def place(index):
    return (lax.axis_index("rows"), index)


def gather_kernel(count, block_ref, whole_ref, own_sem, send_sem, recv_sem):
    rows = block_ref.shape[0]
    me = lax.axis_index("seq")
    chip, core, chips = me // 2, me % 2, count // 2
    other = me + 1 - 2 * core
    barrier = pltpu.get_barrier_semaphore()

    def block(index):
        return whole_ref.at[pl.ds(index * rows, rows)]

    pl.semaphore_signal(barrier, inc=1, device_id=place(other), device_id_type=MESH)

    @pl.when(chip > 0)
    def _():
        pl.semaphore_signal(barrier, inc=1, device_id=place(me - 2), device_id_type=MESH)

    @pl.when(chip < chips - 1)
    def _():
        pl.semaphore_signal(barrier, inc=1, device_id=place(me + 2), device_id_type=MESH)

    peers = 1 + jnp.where(chip > 0, 1, 0) + jnp.where(chip < chips - 1, 1, 0)
    pl.semaphore_wait(barrier, peers)
    own = pltpu.make_async_copy(block_ref, block(me), own_sem)
    own.start()

    def copy(lane, source, target, from_own=False):
        there = block(2 * source + core)
        return pltpu.make_async_remote_copy(
            src_ref=block_ref if from_own else there,
            dst_ref=there,
            send_sem=send_sem.at[lane, source],
            recv_sem=recv_sem.at[lane, source],
            device_id=place(target),
            device_id_type=MESH,
        )

    def right(source, from_own=False):
        return copy(0, source, me + 2, from_own)

    def left(source, from_own=False):
        return copy(1, source, me - 2, from_own)

    def across(source, from_own=False):
        return copy(2, source, other, from_own)

    @pl.when(chip < chips - 1)
    def _():
        right(chip, True).start()

    @pl.when(chip > 0)
    def _():
        left(chip, True).start()

    across(chip, True).start()
    for step in range(1, chips):

        @pl.when(chip - step >= 0)
        def _():
            right(chip - step).wait_recv()

            @pl.when(chip < chips - 1)
            def _():
                right(chip - step).start()

            across(chip - step).start()

        @pl.when(chip + step < chips)
        def _():
            left(chip + step).wait_recv()

            @pl.when(chip > 0)
            def _():
                left(chip + step).start()

            across(chip + step).start()

    own.wait()
    for source in range(chips):
        there = block(2 * source + 1 - core)
        pltpu.make_async_remote_copy(
            src_ref=there,
            dst_ref=there,
            send_sem=send_sem.at[2, source],
            recv_sem=recv_sem.at[2, source],
            device_id=place(other),
            device_id_type=MESH,
        ).wait_recv()
        across(source).wait_send()

        @pl.when((source <= chip) & (chip < chips - 1))
        def _():
            right(source).wait_send()

        @pl.when((source >= chip) & (chip > 0))
        def _():
            left(source).wait_send()


def gather_rows(block_in, count, collective_id):
    rows, width = block_in.shape
    return pl.pallas_call(
        functools.partial(gather_kernel, count),
        out_shape=jax.ShapeDtypeStruct((count * rows, width), block_in.dtype),
        in_specs=[pl.BlockSpec(memory_space=pl.ANY)],
        out_specs=pl.BlockSpec(memory_space=pl.ANY),
        scratch_shapes=[
            pltpu.SemaphoreType.DMA,
            pltpu.SemaphoreType.DMA((3, count // 2)),
            pltpu.SemaphoreType.DMA((3, count // 2)),
        ],
        compiler_params=pltpu.CompilerParams(
            collective_id=collective_id, has_side_effects=True
        ),
    )(block_in)


AXES = {"seq": 1, "chip": 1, "rows": 0}


def peer(axis, step, counts):
    row, me = lax.axis_index("rows"), lax.axis_index("seq")
    if axis == "rows":
        there = lax.rem(row + step, counts["rows"])
        return (there, me), there
    if axis == "seq":
        there = lax.rem(me + step, counts["seq"])
        return (row, there), there
    there = lax.rem(me // 2 + step, counts["chip"])
    return (row, there * 2 + me % 2), there


def own_place(axis):
    if axis == "rows":
        return lax.axis_index("rows")
    return lax.axis_index("seq") if axis == "seq" else lax.axis_index("seq") // 2


def whole(ref, index):
    return ref


def lead(ref, index):
    return ref.at[index]


def second_dim(ref, index):
    return ref.at[:, index]


def rows_of(size, first=0, lanes=None):
    def find(ref, index):
        rows = pl.ds(pl.multiple_of(index * size, size), size)
        return ref.at[rows] if lanes is None else ref.at[rows, first : first + lanes]

    return find


def columns_of(size, first=0):
    def find(ref, index):
        return ref.at[:, pl.ds(pl.multiple_of(first + index * size, size), size)]

    return find


def greet(axes, counts):
    barrier = pltpu.get_barrier_semaphore()
    total = 0
    for axis in axes:
        for step in range(1, counts[axis]):
            pl.semaphore_signal(
                barrier, inc=1, device_id=peer(axis, step, counts)[0], device_id_type=MESH
            )
            total += 1
    pl.semaphore_wait(barrier, total)


def steps_of(total):
    return sorted(range(1, total), key=lambda step: -min(step, total - step))


class Transfers:
    def __init__(self, part, counts, own_sem, send_sem, recv_sem):
        from_ref, to_ref, axis, source, target = part
        here = own_place(axis)
        self.own = pltpu.make_async_copy(source(from_ref, here), target(to_ref, here), own_sem)
        self.remote = []
        for step in steps_of(counts[axis]):
            device, there = peer(axis, step, counts)
            self.remote.append(
                pltpu.make_async_remote_copy(
                    src_ref=source(from_ref, there),
                    dst_ref=target(to_ref, here),
                    send_sem=send_sem.at[step],
                    recv_sem=recv_sem.at[step],
                    device_id=device,
                    device_id_type=MESH,
                )
            )

    def start(self):
        for copy in self.remote:
            copy.start()
        self.own.start()

    def arrived(self):
        self.own.wait()
        for copy in self.remote:
            copy.wait_recv()

    def sent(self):
        for copy in self.remote:
            copy.wait_send()


def axes_of(axes):
    return tuple(axis for axis in ("seq", "rows") if axis in axes)


def exchange_kernel(counts, ins_count, parts, *refs):
    outs_count = len({part[1] for part in parts})
    ins, outs = refs[:ins_count], refs[ins_count : ins_count + outs_count]
    own_sem, send_sem, recv_sem = refs[ins_count + outs_count :]
    greet(axes_of([part[2] for part in parts]), counts)
    moves = [
        Transfers(
            (ins[part[0]], outs[part[1]]) + part[2:],
            counts,
            own_sem.at[index],
            send_sem.at[index],
            recv_sem.at[index],
        )
        for index, part in enumerate(parts)
    ]
    for move in moves:
        move.start()
    for move in moves:
        move.arrived()
    for move in moves:
        move.sent()


def exchange(arrays, shapes, parts, counts, collective_id):
    longest = max(counts[part[2]] for part in parts)
    return pl.pallas_call(
        functools.partial(exchange_kernel, counts, len(arrays), parts),
        out_shape=shapes,
        in_specs=[pl.BlockSpec(memory_space=pl.ANY)] * len(arrays),
        out_specs=[pl.BlockSpec(memory_space=pl.ANY)] * len(shapes),
        scratch_shapes=[
            pltpu.SemaphoreType.DMA((len(parts),)),
            pltpu.SemaphoreType.DMA((len(parts), longest)),
            pltpu.SemaphoreType.DMA((len(parts), longest)),
        ],
        compiler_params=pltpu.CompilerParams(
            collective_id=collective_id, has_side_effects=True
        ),
    )(*arrays)


def add_slots(ref):
    return low(functools.reduce(jnp.add, [wide(ref[i]) for i in range(ref.shape[0])]))


def finish_kernel(counts, shapes, *refs):
    rows_done, rows_open, lanes_ok = shapes
    done, opened = len(rows_done), len(rows_open)
    refs = list(refs)

    def take(number):
        found = refs[:number]
        del refs[:number]
        return found

    dqkv_ref, own_ref = take(2)
    done_in, open_in = take(done), take(opened)
    tokens_ref, own_out = take(2)
    done_out, open_out = take(done), take(opened)
    own_slots, own_sum, own_block = take(3)
    open_slots, open_sum = take(opened), take(opened)
    chip_slots, chip_sum = take(done + opened), take(done + opened)
    sems = take(3)
    greet(("seq", "rows"), counts)
    number = 0

    def move(*part):
        nonlocal number
        found = Transfers(part, counts, *(sem.at[number] for sem in sems))
        number += 1
        return found

    count = counts["seq"]
    width = dqkv_ref.shape[1] // 3
    tokens = dqkv_ref.shape[0] // count
    if lanes_ok:
        home = [
            move(
                dqkv_ref,
                tokens_ref,
                "seq",
                rows_of(tokens, part * width, width),
                columns_of(width, part * width * count),
            )
            for part in range(3)
        ]
    else:
        home = [move(dqkv_ref, tokens_ref, "seq", rows_of(tokens), lead)]
    over_rows = [
        move(ref, slots, "rows", columns_of(slots.shape[2]), lead)
        for ref, slots in zip(open_in, open_slots)
    ]
    own_rows = move(own_ref, own_slots, "rows", second_dim, lead)
    done_chips = [
        move(ref, slots, "chip", rows_of(slots.shape[1]), lead)
        for ref, slots in zip(done_in, chip_slots[:done])
    ]
    for item in home + over_rows + [own_rows] + done_chips:
        item.start()
    open_chips = []
    for item, slots, total, place_ref in zip(over_rows, open_slots, open_sum, chip_slots[done:]):
        item.arrived()
        total[...] = add_slots(slots)
        open_chips.append(move(total, place_ref, "chip", rows_of(place_ref.shape[1]), lead))
        open_chips[-1].start()
    own_rows.arrived()
    own_sum[...] = add_slots(own_slots)
    if lanes_ok:
        own_chips = [
            move(
                own_sum.at[:, :, part * width : (part + 1) * width],
                own_block,
                "seq",
                lead,
                columns_of(width, part * width * count),
            )
            for part in range(3)
        ]
    else:
        own_chips = [move(own_sum, own_block, "seq", lead, lead)]
    for item in own_chips:
        item.start()
    last = []
    for item, slots, total, out in zip(
        done_chips + open_chips, chip_slots, chip_sum, done_out + open_out
    ):
        item.arrived()
        total[...] = add_slots(slots)
        last.append(move(total, out, "rows", whole, columns_of(total.shape[1])))
        last[-1].start()
    for item in own_chips:
        item.arrived()
    if lanes_ok:
        last.append(move(own_block, own_out, "rows", whole, rows_of(own_block.shape[0])))
    else:
        last.append(move(own_block, own_out, "rows", whole, lead))
    last[-1].start()
    for item in home + last:
        item.arrived()
    for item in home + over_rows + [own_rows] + done_chips + open_chips + own_chips + last:
        item.sent()


def finish(dqkv, own_grad, rows_done, rows_open, counts, collective_id):
    count, chips, rows = counts["seq"], counts["chip"], counts["rows"]
    length, all_width = dqkv.shape
    width = all_width // 3
    lanes_ok = width % 128 == 0
    tokens, short = length // count, own_grad.shape[2]
    bf = jnp.bfloat16
    if lanes_ok:
        tokens_shape = (tokens, all_width * count)
        own_block, own_out = (short, all_width * count), (rows * short, all_width * count)
    else:
        tokens_shape = (count, tokens, all_width)
        own_block, own_out = (count, short, all_width), (rows, count, short, all_width)
    shares = [term.shape for term in rows_done]
    shares += [(term.shape[0], term.shape[1] // rows) for term in rows_open]
    blocks = [(shape[0] // chips, shape[1]) for shape in shares]
    outs = [tokens_shape, own_out] + [(shape[0], shape[1] * rows) for shape in blocks]
    open_shares = shares[len(rows_done) :]
    scratch = [(rows,) + own_grad.shape[:1] + own_grad.shape[2:]]
    scratch += [own_grad.shape[:1] + own_grad.shape[2:], own_block]
    scratch += [(rows,) + shape for shape in open_shares] + open_shares
    scratch += [(chips,) + shape for shape in blocks] + blocks
    moves = 3 + 3 + 2 + len(rows_open) + 2 * len(shares)
    longest = max(count, rows)
    arrays = [dqkv, own_grad, *rows_done, *rows_open]
    return pl.pallas_call(
        functools.partial(
            finish_kernel,
            counts,
            (
                tuple(term.shape for term in rows_done),
                tuple(term.shape for term in rows_open),
                lanes_ok,
            ),
        ),
        out_shape=[jax.ShapeDtypeStruct(shape, bf) for shape in outs],
        in_specs=[pl.BlockSpec(memory_space=pl.ANY)] * len(arrays),
        out_specs=[pl.BlockSpec(memory_space=pl.ANY)] * len(outs),
        scratch_shapes=[pltpu.VMEM(shape, bf) for shape in scratch]
        + [
            pltpu.SemaphoreType.DMA((moves,)),
            pltpu.SemaphoreType.DMA((moves, longest)),
            pltpu.SemaphoreType.DMA((moves, longest)),
        ],
        compiler_params=pltpu.CompilerParams(
            collective_id=collective_id, has_side_effects=True, vmem_limit_bytes=VMEM_LIMIT
        ),
    )(*arrays)


def vectors_kernel(counts, given_ref, out_ref, slots, total, own_sem, send_sem, recv_sem):
    greet(("seq", "rows"), counts)
    over_seq = Transfers(
        (given_ref, slots, "seq", lead, lead), counts, own_sem.at[0], send_sem.at[0], recv_sem.at[0]
    )
    over_seq.start()
    over_seq.arrived()
    total[...] = functools.reduce(jnp.add, [slots[i] for i in range(slots.shape[0])])
    over_rows = Transfers(
        (total, out_ref, "rows", whole, lead), counts, own_sem.at[1], send_sem.at[1], recv_sem.at[1]
    )
    over_rows.start()
    over_rows.arrived()
    over_seq.sent()
    over_rows.sent()


def sum_vectors(given, counts, collective_id):
    longest = max(counts["seq"], counts["rows"])
    block = given.shape[1:]
    return pl.pallas_call(
        functools.partial(vectors_kernel, counts),
        out_shape=jax.ShapeDtypeStruct((counts["rows"],) + block, jnp.float32),
        in_specs=[pl.BlockSpec(memory_space=pl.ANY)],
        out_specs=pl.BlockSpec(memory_space=pl.ANY),
        scratch_shapes=[
            pltpu.VMEM((counts["seq"],) + block, jnp.float32),
            pltpu.VMEM(block, jnp.float32),
            pltpu.SemaphoreType.DMA((2,)),
            pltpu.SemaphoreType.DMA((2, longest)),
            pltpu.SemaphoreType.DMA((2, longest)),
        ],
        compiler_params=pltpu.CompilerParams(collective_id=collective_id, has_side_effects=True),
    )(given)


def weight_grad_kernel(which_ref, first_ref, second_ref, *refs):
    grad = dot_left(first_ref[...], second_ref[...])
    if len(refs) == 2:
        grad = grad + wide(refs[0][...])
    refs[-1][...] = low(grad)


def weight_grad(first, second, which, chips, given=None):
    tokens, depth = first.shape
    block, columns = depth // (2 * chips), second.shape[1]
    tile = min(columns, 1024)
    out = pl.BlockSpec((block, tile), lambda n, z, which: (z, n))
    specs = [
        pl.BlockSpec((tokens, block), lambda n, z, which: (0, 2 * z + which[0])),
        pl.BlockSpec((tokens, tile), lambda n, z, which: (0, n)),
    ]
    arrays = [first, second]
    if given is not None:
        specs.append(out)
        arrays.append(given)
    return pl.pallas_call(
        weight_grad_kernel,
        grid_spec=pltpu.PrefetchScalarGridSpec(
            num_scalar_prefetch=1,
            grid=(columns // tile, chips),
            in_specs=specs,
            out_specs=out,
        ),
        out_shape=jax.ShapeDtypeStruct((chips * block, columns), jnp.bfloat16),
        compiler_params=pltpu.CompilerParams(vmem_limit_bytes=VMEM_LIMIT),
        cost_estimate=pl.CostEstimate(
            flops=tokens * depth * columns,
            bytes_accessed=2 * (tokens * (depth + columns) + depth * columns),
            transcendentals=0,
        ),
    )(which, *arrays)


def head_lanes(width):
    return lax.broadcasted_iota(jnp.int32, (1, width), 1) // DEPTH


def pick_head(values, head, width):
    if width == DEPTH:
        return values
    return jnp.where(head_lanes(width) == head, values, jnp.zeros_like(values))


def as_row(column):
    return jnp.broadcast_to(column, (column.shape[0], 8)).T[:1]


def self_forward_kernel(qkv_ref, start_ref, out_ref, stat_ref):
    length, width = out_ref.shape
    heads = width // DEPTH
    blocks = length // BLOCK
    for index in range(blocks):
        rows = pl.ds(index * BLOCK, BLOCK)
        keys_end = (index + 1) * BLOCK
        query = qkv_ref[rows, 0:width]
        begin = jnp.broadcast_to(start_ref[:, rows], (8, BLOCK)).T[:, :1]
        position = index * BLOCK + lax.broadcasted_iota(jnp.int32, (BLOCK, 1), 0)
        if index == blocks - 1 or index <= 1:
            cuts = [(0, keys_end)]
        else:
            cuts = [(0, BLOCK), (BLOCK, index * BLOCK), (index * BLOCK, keys_end)]
        outs, stats = [], []
        for head in range(heads):
            query_head = pick_head(query, head, width) * jnp.bfloat16(SCALE)
            scores = []
            for low_end, high_end in cuts:
                part = dot_right(query_head, qkv_ref[low_end:high_end, width : 2 * width])
                if low_end == 0 or high_end == keys_end:
                    column = low_end + lax.broadcasted_iota(jnp.int32, part.shape, 1)
                    allowed = column >= begin
                    if high_end == keys_end:
                        allowed = allowed & (column <= position)
                    part = jnp.where(allowed, part, NEGATIVE)
                scores.append(part)
            top = functools.reduce(
                jnp.maximum, [jnp.max(part, axis=-1, keepdims=True) for part in scores]
            )
            total, mixed = 0.0, 0.0
            for (low_end, high_end), part in zip(cuts, scores):
                weight = jnp.exp(part - top)
                total = total + jnp.sum(weight, axis=-1, keepdims=True)
                mixed = mixed + dot_plain(
                    low(weight), qkv_ref[low_end:high_end, 2 * width : 3 * width]
                )
            outs.append(mixed / total)
            stats.append(top + jnp.log(total))
        merged = outs[0]
        for head in range(1, heads):
            merged = jnp.where(head_lanes(width) == head, outs[head], merged)
        out_ref[rows, :] = low(merged)
        for head in range(heads):
            stat_ref[head : head + 1, rows] = as_row(stats[head])


def self_forward(qkv, begins):
    length, width = qkv.shape[0], qkv.shape[1] // 3
    heads = width // DEPTH
    return pl.pallas_call(
        self_forward_kernel,
        out_shape=(
            jax.ShapeDtypeStruct((length, width), jnp.bfloat16),
            jax.ShapeDtypeStruct((heads, length), jnp.float32),
        ),
        in_specs=[pl.BlockSpec(memory_space=pltpu.VMEM)] * 2,
        out_specs=[pl.BlockSpec(memory_space=pltpu.VMEM)] * 2,
        compiler_params=pltpu.CompilerParams(vmem_limit_bytes=VMEM_LIMIT),
    )(qkv, begins[None, :])


def self_backward_kernel(qkv_ref, out_ref, grad_ref, start_ref, stat_ref, dqkv_ref, dk_ref, dv_ref):
    length, width = out_ref.shape
    heads = width // DEPTH
    blocks = length // BLOCK
    dk_ref[...] = jnp.zeros_like(dk_ref)
    dv_ref[...] = jnp.zeros_like(dv_ref)

    def query_block(index, carry):
        rows = pl.ds(pl.multiple_of(index * BLOCK, BLOCK), BLOCK)
        query = qkv_ref[rows, 0:width]
        grad = grad_ref[rows, :]
        product = (wide(grad) * wide(out_ref[rows, :])).T
        begin = start_ref[:, rows]
        position = index * BLOCK + lax.broadcasted_iota(jnp.int32, (1, BLOCK), 1)
        query_heads = [pick_head(query, head, width) * jnp.bfloat16(SCALE) for head in range(heads)]
        grad_heads = [pick_head(grad, head, width) for head in range(heads)]
        stats = [stat_ref[head : head + 1, rows] for head in range(heads)]
        deltas = [
            jnp.sum(product[head * DEPTH : (head + 1) * DEPTH, :], axis=0, keepdims=True)
            for head in range(heads)
        ]

        def key_block(key_index, sums):
            keys = pl.ds(pl.multiple_of(key_index * BLOCK, BLOCK), BLOCK)
            key = qkv_ref[keys, width : 2 * width]
            value = qkv_ref[keys, 2 * width : 3 * width]
            row = key_index * BLOCK + lax.broadcasted_iota(jnp.int32, (BLOCK, 1), 0)
            allowed = (row >= begin) & (row <= position)
            dk_part, dv_part, found = 0.0, 0.0, []
            for head in range(heads):
                scores = jnp.where(allowed, dot_right(key, query_heads[head]), NEGATIVE)
                prob = jnp.exp(scores - stats[head])
                dv_part = dv_part + dot_plain(low(prob), grad_heads[head])
                grad_prob = dot_right(value, grad_heads[head])
                grad_score = low(prob * (grad_prob - deltas[head]))
                dk_part = dk_part + dot_plain(grad_score, query_heads[head])
                found.append(sums[head] + dot_left(grad_score, key))
            dk_ref[keys, :] += dk_part
            dv_ref[keys, :] += dv_part
            return tuple(found)

        zero = tuple(jnp.zeros((BLOCK, width), jnp.float32) for _ in range(heads))
        sums = lax.fori_loop(0, index + 1, key_block, zero)
        merged = sums[0]
        for head in range(1, heads):
            merged = jnp.where(head_lanes(width) == head, sums[head], merged)
        dqkv_ref[rows, 0:width] = low(merged * SCALE)
        return carry

    lax.fori_loop(0, blocks, query_block, 0)
    dqkv_ref[:, width : 2 * width] = low(dk_ref[...])
    dqkv_ref[:, 2 * width : 3 * width] = low(dv_ref[...])


def self_backward(qkv, out, grad, begins, stats):
    length, width = out.shape
    return pl.pallas_call(
        self_backward_kernel,
        out_shape=jax.ShapeDtypeStruct((length, 3 * width), jnp.bfloat16),
        in_specs=[pl.BlockSpec(memory_space=pltpu.VMEM)] * 5,
        out_specs=pl.BlockSpec(memory_space=pltpu.VMEM),
        scratch_shapes=[pltpu.VMEM((length, width), jnp.float32)] * 2,
        compiler_params=pltpu.CompilerParams(vmem_limit_bytes=VMEM_LIMIT),
    )(qkv, out, grad, begins[None, :], stats)


def cross_forward_kernel(query_ref, key_ref, value_ref, own_key_ref, own_value_ref, out_ref, stat_ref):
    tokens = query_ref.shape[0] - SLOTS
    width = query_ref.shape[1]
    for begin, size, keys, values in (
        (0, tokens, key_ref, value_ref),
        (tokens, SLOTS, own_key_ref, own_value_ref),
    ):
        query = query_ref[begin : begin + size, :]
        outs = []
        for head in range(width // DEPTH):
            query_head = pick_head(query, head, width) * jnp.bfloat16(SCALE)
            scores = dot_right(query_head, keys[...])
            column = lax.broadcasted_iota(jnp.int32, scores.shape, 1)
            scores = jnp.where(column < PAGE_TOK, scores, NEGATIVE)
            top = jnp.max(scores, axis=-1, keepdims=True)
            weight = jnp.exp(scores - top)
            total = jnp.sum(weight, axis=-1, keepdims=True)
            outs.append(dot_plain(low(weight), values[...]) / total)
            stat_ref[0, head : head + 1, begin : begin + size] = as_row(top + jnp.log(total))
        merged = outs[0]
        for head in range(1, len(outs)):
            merged = jnp.where(head_lanes(width) == head, outs[head], merged)
        out_ref[begin : begin + size, :] = low(merged)


def cross_forward(query, kv_big, kv_own):
    rows, features = query.shape
    pair = 2 * DEPTH
    steps = features // pair
    tall = pl.BlockSpec((rows, pair), lambda i: (0, i))
    keys = pl.BlockSpec((PAGE_PAD, pair), lambda i: (0, i))
    values = pl.BlockSpec((PAGE_PAD, pair), lambda i: (0, i + steps))
    return pl.pallas_call(
        cross_forward_kernel,
        grid=(steps,),
        out_shape=(
            jax.ShapeDtypeStruct((rows, features), jnp.bfloat16),
            jax.ShapeDtypeStruct((steps, 2, rows), jnp.float32),
        ),
        in_specs=[tall, keys, values, keys, values],
        out_specs=[tall, pl.BlockSpec((1, 2, rows), lambda i: (i, 0, 0))],
        compiler_params=pltpu.CompilerParams(vmem_limit_bytes=VMEM_LIMIT),
    )(query, kv_big, kv_big, kv_own, kv_own)


def cross_backward_kernel(
    query_ref,
    key_ref,
    value_ref,
    own_key_ref,
    own_value_ref,
    out_ref,
    grad_ref,
    stat_ref,
    dq_ref,
    dk_ref,
    dv_ref,
    own_dk_ref,
    own_dv_ref,
):
    tokens = query_ref.shape[0] - SLOTS
    width = query_ref.shape[1]
    row = lax.broadcasted_iota(jnp.int32, (PAGE_PAD, 1), 0)
    for begin, size, keys, values, dk_out, dv_out in (
        (0, tokens, key_ref, value_ref, dk_ref, dv_ref),
        (tokens, SLOTS, own_key_ref, own_value_ref, own_dk_ref, own_dv_ref),
    ):
        rows = slice(begin, begin + size)
        query, grad = query_ref[rows, :], grad_ref[rows, :]
        product = (wide(grad) * wide(out_ref[rows, :])).T
        dk_sum, dv_sum, found = 0.0, 0.0, []
        for head in range(width // DEPTH):
            query_head = pick_head(query, head, width) * jnp.bfloat16(SCALE)
            grad_head = pick_head(grad, head, width)
            delta = jnp.sum(product[head * DEPTH : (head + 1) * DEPTH, :], axis=0, keepdims=True)
            scores = dot_right(keys[...], query_head)
            scores = jnp.where(row < PAGE_TOK, scores, NEGATIVE)
            prob = jnp.exp(scores - stat_ref[0, head : head + 1, rows])
            dv_sum = dv_sum + dot_plain(low(prob), grad_head)
            grad_prob = dot_right(values[...], grad_head)
            grad_score = low(prob * (grad_prob - delta))
            dk_sum = dk_sum + dot_plain(grad_score, query_head)
            found.append(dot_left(grad_score, keys[...]))
        merged = found[0]
        for head in range(1, len(found)):
            merged = jnp.where(head_lanes(width) == head, found[head], merged)
        dq_ref[rows, :] = low(merged * SCALE)
        dk_out[...] = low(dk_sum)
        dv_out[...] = low(dv_sum)


def cross_backward(query, kv_big, kv_own, out, grad, stats):
    rows, features = query.shape
    pair = 2 * DEPTH
    steps = features // pair
    tall = pl.BlockSpec((rows, pair), lambda i: (0, i))
    keys = pl.BlockSpec((PAGE_PAD, pair), lambda i: (0, i))
    values = pl.BlockSpec((PAGE_PAD, pair), lambda i: (0, i + steps))
    page = jax.ShapeDtypeStruct((PAGE_PAD, features), jnp.bfloat16)
    return pl.pallas_call(
        cross_backward_kernel,
        grid=(steps,),
        out_shape=(jax.ShapeDtypeStruct((rows, features), jnp.bfloat16), page, page, page, page),
        in_specs=[
            tall,
            keys,
            values,
            keys,
            values,
            tall,
            tall,
            pl.BlockSpec((1, 2, rows), lambda i: (i, 0, 0)),
        ],
        out_specs=[tall, keys, keys, keys, keys],
        compiler_params=pltpu.CompilerParams(vmem_limit_bytes=VMEM_LIMIT),
    )(query, kv_big, kv_big, kv_own, kv_own, out, grad, stats)


def body(
    inputs,
    memory,
    out_grad,
    segment_ids,
    page_order,
    norm1_gain,
    norm1_bias,
    qkv_weight,
    qv_bias,
    self_out_weight,
    self_out_bias,
    norm2_gain,
    norm2_bias,
    cross_q_weight,
    cross_q_bias,
    cross_kv_weight,
    cross_v_bias,
    cross_out_weight,
    cross_out_bias,
    norm3_gain,
    norm3_bias,
    fc1_weight,
    fc1_bias,
    fc2_weight,
    fc2_bias,
):
    tokens, features = inputs.shape[1:]
    count = lax.axis_size("seq")
    me = lax.axis_index("seq")
    length = tokens * count
    width = features // count
    rows_count = lax.axis_size("rows")
    counts = {"seq": count, "chip": count // 2, "rows": rows_count}
    core = me % 2

    def pair_sum(first, second):
        this = core.astype(jnp.int32)[None]
        if first.shape[1] // count % 128:
            wider = jnp.pad(
                first.reshape(-1, count, first.shape[1] // count),
                ((0, 0), (0, 0), (0, 128 - first.shape[1] // count)),
            ).reshape(first.shape[0], -1)
            theirs, mine = (weight_grad(wider, second, w, count // 2) for w in (1 - this, this))
            theirs, mine = (
                term.reshape(count // 2, 128, -1)[:, : first.shape[1] // count].reshape(
                    first.shape[1] // 2, -1
                )
                for term in (theirs, mine)
            )
            return low(wide(mine) + wide(swap(theirs)))
        theirs = weight_grad(first, second, 1 - this, count // 2)
        return weight_grad(first, second, this, count // 2, swap(theirs))

    def swap(value):
        return lax.ppermute(value, "seq", [(i, i ^ 1) for i in range(count)])

    def after(value, other):
        return lax.optimization_barrier((value, other))[0]

    mem_rows = memory.shape[1]
    sharers = PAGE_TOK // mem_rows
    row_segs = segment_ids[0]
    row_pages = page_order[0]
    gain_one, shift_one = wide(norm1_gain), wide(norm1_bias)
    gain_two, shift_two = wide(norm2_gain), wide(norm2_bias)
    gain_three, shift_three = wide(norm3_gain), wide(norm3_bias)

    page_sizes = jnp.sum(row_segs[None, :] == jnp.arange(PAGES)[:, None], axis=1)
    page_starts = jnp.cumsum(page_sizes) - page_sizes
    begins = sum(
        jnp.where(row_segs == page, page_starts[page], 0) for page in range(PAGES)
    ).astype(jnp.int32)
    big_page = row_segs[length // 2]
    big_start = jnp.sum(row_segs < big_page)
    own_page = lax.dynamic_index_in_dim(row_pages, me // sharers, 0, keepdims=False)
    slot = jnp.arange(SLOTS)
    in_front = (slot < big_start)[:, None]
    slot_segs = jnp.where(slot < big_start, row_segs[:SLOTS], row_segs[length - SLOTS :])
    slot_mine = (slot_segs == own_page) & (slot * sharers // SLOTS == me % sharers)
    home_segs = lax.dynamic_slice_in_dim(row_segs, me * tokens, tokens, 0)
    active = jnp.concatenate((home_segs == big_page, slot_mine))[:, None]
    is_first, is_last = me == 0, me == count - 1

    def slots_of(front, back):
        return jnp.where(in_front, front, back)

    mem_own = memory[0]
    mem_page = mem_own
    if sharers > 1:
        groups = [[g * sharers + s for s in range(sharers)] for g in range(count // sharers)]
        mem_page = lax.all_gather(mem_own, "seq", axis=0, tiled=True, axis_index_groups=groups)
    mem_page = jnp.pad(mem_page, ((0, PAGE_PAD - PAGE_TOK), (0, 0)))
    gives_big = (own_page == big_page) & (me % sharers == 0)

    x_own = inputs[0]
    x_all = gather_rows(x_own, count, 0)

    half = PAGE_PAD // 2
    masked_page = jnp.where(gives_big, mem_page, jnp.zeros_like(mem_page)).reshape(2, half, -1)
    pair_page = masked_page[core] + swap(masked_page[1 - core])
    at_end = jnp.where(core == 0, is_first, is_last)
    end_grad = jnp.where(core == 0, out_grad[0, :SLOTS], out_grad[0, tokens - SLOTS :])
    sent = jnp.concatenate((pair_page, jnp.where(at_end, end_grad, jnp.zeros_like(end_grad))))
    same_core = [[2 * chip + which for chip in range(count // 2)] for which in range(2)]
    mine = lax.psum(after(sent, x_all), "seq", axis_index_groups=same_core)
    theirs = swap(mine)
    zeroth, first = jnp.where(core == 0, mine, theirs), jnp.where(core == 0, theirs, mine)
    mem_big = jnp.concatenate((zeroth[:half], first[:half]))
    front_grad, back_grad = zeroth[half:], first[half:]

    qkv_own_weight = jnp.concatenate(
        [
            lax.dynamic_slice_in_dim(qkv_weight, part * features + me * width, width, 1)
            for part in range(3)
        ],
        axis=1,
    )
    qkv_own_bias = jnp.concatenate(
        (
            lax.dynamic_slice_in_dim(qv_bias, me * width, width, 0),
            jnp.zeros((width,), jnp.bfloat16),
            lax.dynamic_slice_in_dim(qv_bias, features + me * width, width, 0),
        )
    )
    normed_all = low(norm_forward(wide(x_all), gain_one, shift_one))
    qkv = low(dot_plain(normed_all, qkv_own_weight) + wide(qkv_own_bias))
    mixed, mixed_stats = self_forward(qkv, begins)
    bf = jnp.bfloat16
    lanes_ok = width % 128 == 0
    ends = jnp.concatenate((mixed[:SLOTS], mixed[length - SLOTS :]))
    if lanes_ok:
        blocks_mixed, ends_mixed = exchange(
            (mixed, ends),
            (
                jax.ShapeDtypeStruct((tokens, features), bf),
                jax.ShapeDtypeStruct((2 * SLOTS, features), bf),
            ),
            (
                (1, 1, "seq", whole, columns_of(width)),
                (0, 0, "seq", rows_of(tokens), columns_of(width)),
            ),
            counts,
            1,
        )
    else:
        blocks_mixed, ends_mixed = exchange(
            (mixed, ends),
            (
                jax.ShapeDtypeStruct((count, tokens, width), bf),
                jax.ShapeDtypeStruct((count, 2 * SLOTS, width), bf),
            ),
            ((1, 1, "seq", whole, lead), (0, 0, "seq", rows_of(tokens), lead)),
            counts,
            1,
        )
        blocks_mixed, ends_mixed = (
            blocks.transpose(1, 0, 2).reshape(blocks.shape[1], -1)
            for blocks in (blocks_mixed, ends_mixed)
        )
    attended = jnp.concatenate(
        (blocks_mixed, slots_of(ends_mixed[:SLOTS], ends_mixed[SLOTS:]))
    )
    resid = wide(
        jnp.concatenate((x_own, slots_of(x_all[:SLOTS], x_all[length - SLOTS :])))
    )
    resid_one = resid + dot_plain(attended, self_out_weight) + wide(self_out_bias)
    normed_two = low(norm_forward(resid_one, gain_two, shift_two))
    cross_queries = low(dot_plain(normed_two, cross_q_weight) + wide(cross_q_bias))
    kv_shift = jnp.concatenate((jnp.zeros((features,), jnp.float32), wide(cross_v_bias)))
    kv_big = low(dot_plain(mem_big, cross_kv_weight) + kv_shift)
    kv_own = low(dot_plain(mem_page, cross_kv_weight) + kv_shift)
    cross_low, cross_stats = cross_forward(cross_queries, kv_big, kv_own)
    resid_two = resid_one + dot_plain(cross_low, cross_out_weight) + wide(cross_out_bias)
    normed_three = low(norm_forward(resid_two, gain_three, shift_three))
    pre_act = dot_plain(normed_three, fc1_weight) + wide(fc1_bias)
    hidden_act = low(gelu_exact(pre_act))
    final = low(resid_two + dot_plain(hidden_act, fc2_weight) + wide(fc2_bias))

    grad_out = jnp.concatenate((out_grad[0], slots_of(front_grad, back_grad)))
    grad_out = jnp.where(active, grad_out, jnp.zeros_like(grad_out))
    grad_act = dot_right(grad_out, fc2_weight)
    _, gelu_pull = jax.vjp(gelu_exact, pre_act)
    grad_pre = low(gelu_pull(grad_act)[0])
    grad_fc2_w = pair_sum(hidden_act, grad_out)
    fc2_share = lax.psum_scatter(grad_fc2_w, "rows", scatter_dimension=1, tiled=True)
    grad_fc2_b = jnp.sum(wide(grad_out), axis=0)
    grad_fc1_w = pair_sum(normed_three, grad_pre)
    fc1_share = lax.psum_scatter(grad_fc1_w, "rows", scatter_dimension=1, tiled=True)
    grad_fc1_b = jnp.sum(wide(grad_pre), axis=0)
    grad_two_norm, grad_gain_three, grad_shift_three = norm_backward(
        resid_two, gain_three, shift_three, dot_right(grad_pre, fc1_weight)
    )
    grad_resid_two = wide(grad_out) + grad_two_norm
    grad_branch_two = low(grad_resid_two)
    grad_co_w = pair_sum(cross_low, grad_branch_two)
    grad_co_b = jnp.sum(wide(grad_branch_two), axis=0)
    grad_cross_low = low(dot_right(grad_branch_two, cross_out_weight))
    grad_cross_q, big_dk, big_dv, own_dk, own_dv = cross_backward(
        cross_queries, kv_big, kv_own, cross_low, grad_cross_low, cross_stats
    )
    grad_cq_w = pair_sum(normed_two, grad_cross_q)
    grad_cq_b = jnp.sum(wide(grad_cross_q), axis=0)
    grad_one_norm, grad_gain_two, grad_shift_two = norm_backward(
        resid_one, gain_two, shift_two, dot_right(grad_cross_q, cross_q_weight)
    )
    grad_resid_one = grad_resid_two + grad_one_norm
    grad_branch_one = low(grad_resid_one)
    grad_o_w = pair_sum(attended, grad_branch_one)
    grad_o_b = jnp.sum(wide(grad_branch_one), axis=0)
    grad_attended = low(dot_right(grad_branch_one, self_out_weight))
    if lanes_ok:
        given, home_part, slot_part = (grad_attended,), (0, 0), (0, 1)

        def piece(first, size):
            def find(ref, index):
                return ref.at[
                    first : first + size, pl.ds(pl.multiple_of(index * width, width), width)
                ]

            return find

        pieces = piece(0, tokens), piece(tokens, SLOTS)
    else:
        by_device = grad_attended.reshape(-1, count, width).transpose(1, 0, 2)
        given, home_part, slot_part = (by_device[:, :tokens], by_device[:, tokens:]), (0, 0), (1, 1)
        pieces = lead, lead
    grad_mixed, slots_grad = exchange(
        given,
        (
            jax.ShapeDtypeStruct((length, width), bf),
            jax.ShapeDtypeStruct((count, SLOTS, width), bf),
        ),
        (
            home_part + ("seq", pieces[0], rows_of(tokens)),
            slot_part + ("seq", pieces[1], lead),
        ),
        counts,
        2,
    )
    slots_grad = low(jnp.sum(wide(slots_grad), axis=0))
    no_slots = jnp.zeros_like(slots_grad)
    grad_mixed = jnp.concatenate(
        (
            grad_mixed[:SLOTS] + jnp.where(in_front, slots_grad, no_slots),
            grad_mixed[SLOTS : length - SLOTS],
            grad_mixed[length - SLOTS :] + jnp.where(in_front, no_slots, slots_grad),
        )
    )
    dqkv = self_backward(qkv, mixed, grad_mixed, begins, mixed_stats)

    slot_final = jnp.where(active[tokens:], final[tokens:], jnp.zeros_like(final[tokens:]))
    own_half = jnp.where(core == 0, big_dk, big_dv)
    own_half = own_half + swap(jnp.where(core == 0, big_dv, big_dk))
    slot_half = jnp.where(core == 0, slot_final, low(grad_resid_one[tokens:]))
    slot_half = slot_half + swap(jnp.where(core == 0, low(grad_resid_one[tokens:]), slot_final))
    mine = lax.psum(
        jnp.concatenate((own_half[:PAGE_TOK], slot_half)), "seq", axis_index_groups=same_core
    )
    mine = after(mine, dqkv)
    theirs = swap(mine)
    zeroth, first = jnp.where(core == 0, mine, theirs), jnp.where(core == 0, theirs, mine)
    big_dk, big_dv = zeroth[:PAGE_TOK], first[:PAGE_TOK]
    slot_final, slot_grad = zeroth[PAGE_TOK:], first[PAGE_TOK:]
    grad_ckv = jnp.where(
        gives_big,
        jnp.concatenate((big_dk, big_dv), axis=1),
        jnp.concatenate((own_dk[:PAGE_TOK], own_dv[:PAGE_TOK]), axis=1),
    )
    if sharers > 1:
        grad_ckv = lax.psum_scatter(
            grad_ckv, "seq", scatter_dimension=0, tiled=True, axis_index_groups=groups
        )
    grad_ckv_w = pair_sum(mem_own, grad_ckv)
    grad_cv_b = jnp.sum(wide(grad_ckv[:, features:]), axis=0)
    memory_grad = dot_right(grad_ckv, cross_kv_weight)[None]

    def at_home(own, returned):
        front = is_first & in_front
        back = is_last & ~in_front
        head = jnp.where(front, returned.astype(own.dtype), own[:SLOTS])
        tail = jnp.where(back, returned.astype(own.dtype), own[tokens - SLOTS :])
        return jnp.concatenate((head, own[SLOTS : tokens - SLOTS], tail))

    layer_out = at_home(final[:tokens], slot_final)[None]
    grad_home = at_home(grad_resid_one[:tokens], slot_grad)

    grad_qkv_w = low(dot_left(normed_all, dqkv))
    grad_qkv_w = grad_qkv_w.reshape(count, rows_count, -1, 3 * width)
    column_sums = jnp.sum(wide(dqkv), axis=0)

    def in_features(part):
        return lax.dynamic_update_slice_in_dim(
            jnp.zeros((features,), jnp.float32),
            column_sums[part * width : (part + 1) * width],
            me * width,
            0,
        )

    grad_qv_b = jnp.concatenate((in_features(0), in_features(2)))

    grad_qkv, qkv_w, fc1_w, fc2_w, o_w, cq_w, co_w, ckv_w = finish(
        dqkv,
        grad_qkv_w,
        (fc1_share, fc2_share),
        (grad_o_w, grad_cq_w, grad_co_w, grad_ckv_w),
        counts,
        3,
    )
    if not lanes_ok:
        grad_qkv = grad_qkv.reshape(count, tokens, 3, width).transpose(1, 2, 0, 3)
        grad_qkv = grad_qkv.reshape(tokens, 3 * features)
        qkv_w = qkv_w.reshape(rows_count, count, -1, 3, width).transpose(0, 2, 3, 1, 4)
        qkv_w = qkv_w.reshape(-1, 3 * features)
    qkv_w, fc1_w, fc2_w, o_w, cq_w, co_w, ckv_w = [
        wide(term) for term in (qkv_w, fc1_w, fc2_w, o_w, cq_w, co_w, ckv_w)
    ]
    grad_in_norm, grad_gain_one, grad_shift_one = norm_backward(
        wide(x_own), gain_one, shift_one, dot_right(grad_qkv, qkv_weight)
    )
    input_grad = (grad_home + grad_in_norm)[None]

    vectors = (
        grad_gain_one,
        grad_shift_one,
        grad_qv_b,
        grad_o_b,
        grad_gain_two,
        grad_shift_two,
        grad_cq_b,
        grad_cv_b,
        grad_co_b,
        grad_gain_three,
        grad_shift_three,
        grad_fc1_b,
        grad_fc2_b,
    )
    joined = jnp.concatenate([vector.reshape(count, -1) for vector in vectors], axis=1)
    joined = jnp.pad(joined, ((0, 0), (0, -joined.shape[1] % 1024))).reshape(count, 8, -1)
    joined = jnp.sum(sum_vectors(joined, counts, 4), axis=0).reshape(-1)
    pieces, offset = [], 0
    for vector in vectors:
        size = vector.shape[0] // count
        pieces.append(joined[offset : offset + size])
        offset += size
    g1, s1, qvb, ob, g2, s2, cqb, cvb, cob, g3, s3, f1b, f2b = pieces
    return (
        layer_out,
        input_grad,
        memory_grad,
        g1,
        s1,
        qkv_w,
        qvb,
        o_w,
        ob,
        g2,
        s2,
        cq_w,
        cqb,
        ckv_w,
        cvb,
        co_w,
        cob,
        g3,
        s3,
        fc1_w,
        f1b,
        fc2_w,
        f2b,
    )


def solution(mesh):
    split = P("rows", "seq", None)
    in_specs = (split, split, split, P("rows", None), P("rows", None)) + (P(),) * 20
    vector, matrix = P("seq"), P("seq", None)
    out_specs = (split, split, split) + (
        vector,
        vector,
        matrix,
        vector,
        matrix,
        vector,
        vector,
        vector,
        matrix,
        vector,
        matrix,
        vector,
        matrix,
        vector,
        vector,
        vector,
        matrix,
        vector,
        matrix,
        vector,
    )
    return jax.shard_map(body, mesh=mesh, in_specs=in_specs, out_specs=out_specs, check_vma=False)
```

```python
import functools

import jax
import jax.numpy as jnp
from jax import lax
from jax.experimental import pallas as pl
from jax.experimental.pallas import tpu as pltpu
from jax.sharding import PartitionSpec as P

HEADS = 16
DEPTH = 64
PAGES = 8
PAGE_TOK = 588
PAGE_PAD = 640
SLOTS = 128
BLOCK = 256


NEGATIVE = -1e30
SCALE = 0.125
EPSILON = 1e-05
MESH = pl.DeviceIdType.MESH
VMEM_LIMIT = 56 * 1024 * 1024


def norm_forward(values, gain, shift):
    center = values - jnp.mean(values, axis=-1, keepdims=True)
    spread = jnp.mean(center * center, axis=-1, keepdims=True)
    return center * lax.rsqrt(spread + EPSILON) * gain + shift


def gelu_exact(values):
    return jax.nn.gelu(values, approximate=False)


def norm_backward(values, gain, shift, grad_normed):
    _, pullback = jax.vjp(norm_forward, values, gain, shift)
    return pullback(grad_normed)


def dot_plain(first, second):
    return jnp.dot(first, second, preferred_element_type=jnp.float32)


def dot_left(first, second):
    return lax.dot_general(
        first, second, (((0,), (0,)), ((), ())), preferred_element_type=jnp.float32
    )


def dot_right(first, second):
    return lax.dot_general(
        first, second, (((1,), (1,)), ((), ())), preferred_element_type=jnp.float32
    )


def low(values):
    return values.astype(jnp.bfloat16)


def wide(values):
    return values.astype(jnp.float32)


def place(index):
    return (lax.axis_index("rows"), index)


def gather_kernel(count, block_ref, whole_ref, own_sem, send_sem, recv_sem):
    rows = block_ref.shape[0]
    me = lax.axis_index("seq")
    chip, core, chips = me // 2, me % 2, count // 2
    other = me + 1 - 2 * core
    barrier = pltpu.get_barrier_semaphore()

    def block(index):
        return whole_ref.at[pl.ds(index * rows, rows)]

    pl.semaphore_signal(barrier, inc=1, device_id=place(other), device_id_type=MESH)

    @pl.when(chip > 0)
    def _():
        pl.semaphore_signal(barrier, inc=1, device_id=place(me - 2), device_id_type=MESH)

    @pl.when(chip < chips - 1)
    def _():
        pl.semaphore_signal(barrier, inc=1, device_id=place(me + 2), device_id_type=MESH)

    peers = 1 + jnp.where(chip > 0, 1, 0) + jnp.where(chip < chips - 1, 1, 0)
    pl.semaphore_wait(barrier, peers)
    own = pltpu.make_async_copy(block_ref, block(me), own_sem)
    own.start()

    def copy(lane, source, target, from_own=False):
        there = block(2 * source + core)
        return pltpu.make_async_remote_copy(
            src_ref=block_ref if from_own else there,
            dst_ref=there,
            send_sem=send_sem.at[lane, source],
            recv_sem=recv_sem.at[lane, source],
            device_id=place(target),
            device_id_type=MESH,
        )

    def right(source, from_own=False):
        return copy(0, source, me + 2, from_own)

    def left(source, from_own=False):
        return copy(1, source, me - 2, from_own)

    def across(source, from_own=False):
        return copy(2, source, other, from_own)

    @pl.when(chip < chips - 1)
    def _():
        right(chip, True).start()

    @pl.when(chip > 0)
    def _():
        left(chip, True).start()

    across(chip, True).start()
    for step in range(1, chips):

        @pl.when(chip - step >= 0)
        def _():
            right(chip - step).wait_recv()

            @pl.when(chip < chips - 1)
            def _():
                right(chip - step).start()

            across(chip - step).start()

        @pl.when(chip + step < chips)
        def _():
            left(chip + step).wait_recv()

            @pl.when(chip > 0)
            def _():
                left(chip + step).start()

            across(chip + step).start()

    own.wait()
    for source in range(chips):
        there = block(2 * source + 1 - core)
        pltpu.make_async_remote_copy(
            src_ref=there,
            dst_ref=there,
            send_sem=send_sem.at[2, source],
            recv_sem=recv_sem.at[2, source],
            device_id=place(other),
            device_id_type=MESH,
        ).wait_recv()
        across(source).wait_send()

        @pl.when((source <= chip) & (chip < chips - 1))
        def _():
            right(source).wait_send()

        @pl.when((source >= chip) & (chip > 0))
        def _():
            left(source).wait_send()


def gather_rows(block_in, count, collective_id):
    rows, width = block_in.shape
    return pl.pallas_call(
        functools.partial(gather_kernel, count),
        out_shape=jax.ShapeDtypeStruct((count * rows, width), block_in.dtype),
        in_specs=[pl.BlockSpec(memory_space=pl.ANY)],
        out_specs=pl.BlockSpec(memory_space=pl.ANY),
        scratch_shapes=[
            pltpu.SemaphoreType.DMA,
            pltpu.SemaphoreType.DMA((3, count // 2)),
            pltpu.SemaphoreType.DMA((3, count // 2)),
        ],
        compiler_params=pltpu.CompilerParams(
            collective_id=collective_id, has_side_effects=True
        ),
    )(block_in)


AXES = {"seq": 1, "chip": 1, "rows": 0}


def peer(axis, step, counts):
    row, me = lax.axis_index("rows"), lax.axis_index("seq")
    if axis == "rows":
        there = lax.rem(row + step, counts["rows"])
        return (there, me), there
    if axis == "seq":
        there = lax.rem(me + step, counts["seq"])
        return (row, there), there
    there = lax.rem(me // 2 + step, counts["chip"])
    return (row, there * 2 + me % 2), there


def own_place(axis):
    if axis == "rows":
        return lax.axis_index("rows")
    return lax.axis_index("seq") if axis == "seq" else lax.axis_index("seq") // 2


def whole(ref, index):
    return ref


def lead(ref, index):
    return ref.at[index]


def second_dim(ref, index):
    return ref.at[:, index]


def rows_of(size, first=0, lanes=None):
    def find(ref, index):
        rows = pl.ds(pl.multiple_of(index * size, size), size)
        return ref.at[rows] if lanes is None else ref.at[rows, first : first + lanes]

    return find


def columns_of(size, first=0):
    def find(ref, index):
        return ref.at[:, pl.ds(pl.multiple_of(first + index * size, size), size)]

    return find


def greet(axes, counts):
    barrier = pltpu.get_barrier_semaphore()
    total = 0
    for axis in axes:
        for step in range(1, counts[axis]):
            pl.semaphore_signal(
                barrier, inc=1, device_id=peer(axis, step, counts)[0], device_id_type=MESH
            )
            total += 1
    pl.semaphore_wait(barrier, total)


def steps_of(total):
    return sorted(range(1, total), key=lambda step: -min(step, total - step))


class Transfers:
    def __init__(self, part, counts, own_sem, send_sem, recv_sem):
        from_ref, to_ref, axis, source, target = part
        here = own_place(axis)
        self.own = pltpu.make_async_copy(source(from_ref, here), target(to_ref, here), own_sem)
        self.remote = []
        for step in steps_of(counts[axis]):
            device, there = peer(axis, step, counts)
            self.remote.append(
                pltpu.make_async_remote_copy(
                    src_ref=source(from_ref, there),
                    dst_ref=target(to_ref, here),
                    send_sem=send_sem.at[step],
                    recv_sem=recv_sem.at[step],
                    device_id=device,
                    device_id_type=MESH,
                )
            )

    def start(self):
        for copy in self.remote:
            copy.start()
        self.own.start()

    def arrived(self):
        self.own.wait()
        for copy in self.remote:
            copy.wait_recv()

    def sent(self):
        for copy in self.remote:
            copy.wait_send()


def axes_of(axes):
    return tuple(axis for axis in ("seq", "rows") if axis in axes)


def exchange_kernel(counts, ins_count, parts, *refs):
    outs_count = len({part[1] for part in parts})
    ins, outs = refs[:ins_count], refs[ins_count : ins_count + outs_count]
    own_sem, send_sem, recv_sem = refs[ins_count + outs_count :]
    greet(axes_of([part[2] for part in parts]), counts)
    moves = [
        Transfers(
            (ins[part[0]], outs[part[1]]) + part[2:],
            counts,
            own_sem.at[index],
            send_sem.at[index],
            recv_sem.at[index],
        )
        for index, part in enumerate(parts)
    ]
    for move in moves:
        move.start()
    for move in moves:
        move.arrived()
    for move in moves:
        move.sent()


def exchange(arrays, shapes, parts, counts, collective_id):
    longest = max(counts[part[2]] for part in parts)
    return pl.pallas_call(
        functools.partial(exchange_kernel, counts, len(arrays), parts),
        out_shape=shapes,
        in_specs=[pl.BlockSpec(memory_space=pl.ANY)] * len(arrays),
        out_specs=[pl.BlockSpec(memory_space=pl.ANY)] * len(shapes),
        scratch_shapes=[
            pltpu.SemaphoreType.DMA((len(parts),)),
            pltpu.SemaphoreType.DMA((len(parts), longest)),
            pltpu.SemaphoreType.DMA((len(parts), longest)),
        ],
        compiler_params=pltpu.CompilerParams(
            collective_id=collective_id, has_side_effects=True
        ),
    )(*arrays)


def add_slots(ref):
    return low(functools.reduce(jnp.add, [wide(ref[i]) for i in range(ref.shape[0])]))


def finish_kernel(counts, sizes, lanes_ok, *refs):
    ready, opened = sizes
    over_chips, over_rows = ready
    done = over_chips + over_rows
    refs = list(refs)

    def take(number):
        found = refs[:number]
        del refs[:number]
        return found

    dqkv_ref, own_ref = take(2)
    done_in, open_in = take(done), take(opened)
    tokens_ref, own_out = take(2)
    outs = take(done + opened)
    own_slots, own_sum, own_block = take(3)
    row_slots, row_sum = take(over_rows + opened), take(over_rows + opened)
    chip_slots, chip_sum = take(done + opened), take(done + opened)
    load_sem, *sems = take(4)
    greet(("seq", "rows"), counts)
    number = 0

    def move(*part):
        nonlocal number
        found = Transfers(part, counts, *(sem.at[number] for sem in sems))
        number += 1
        return found

    count = counts["seq"]
    width = dqkv_ref.shape[1] // 3
    tokens = dqkv_ref.shape[0] // count
    if lanes_ok:
        home = [
            move(
                dqkv_ref,
                tokens_ref,
                "seq",
                rows_of(tokens, part * width, width),
                columns_of(width, part * width * count),
            )
            for part in range(3)
        ]
    else:
        home = [move(dqkv_ref, tokens_ref, "seq", rows_of(tokens), lead)]
    open_rows = [
        move(ref, slots, "rows", columns_of(slots.shape[2]), lead)
        for ref, slots in zip(open_in, row_slots[over_rows:])
    ]
    own_rows = move(own_ref, own_slots, "rows", second_dim, lead)
    for item in home + open_rows + [own_rows]:
        item.start()
    loads = [
        pltpu.make_async_copy(ref, slots, load_sem.at[index])
        for index, (ref, slots) in enumerate(
            zip(done_in, chip_slots[:over_chips] + row_slots[:over_rows])
        )
    ]
    for load in loads:
        load.start()
    chip_moves, last = [], []

    def to_chips(index):
        total, slots = row_sum[index], chip_slots[over_chips + index]
        total[...] = add_slots(row_slots[index])
        chip_moves.append(move(total, slots, "chip", rows_of(slots.shape[1]), lead))
        chip_moves[-1].start()

    def to_rows(index):
        total = chip_sum[index]
        total[...] = add_slots(chip_slots[index])
        last.append(move(total, outs[index], "rows", whole, columns_of(total.shape[1])))
        last[-1].start()

    for index in range(over_rows):
        loads[over_chips + index].wait()
        to_chips(index)
    for index in range(over_chips):
        loads[index].wait()
        to_rows(index)
    own_rows.arrived()
    own_sum[...] = add_slots(own_slots)
    if lanes_ok:
        own_chips = [
            move(
                own_sum.at[:, :, part * width : (part + 1) * width],
                own_block,
                "seq",
                lead,
                columns_of(width, part * width * count),
            )
            for part in range(3)
        ]
    else:
        own_chips = [move(own_sum, own_block, "seq", lead, lead)]
    for item in own_chips:
        item.start()
    for index, item in enumerate(open_rows):
        item.arrived()
        to_chips(over_rows + index)
    for index, item in enumerate(chip_moves):
        item.arrived()
        to_rows(over_chips + index)
    for item in own_chips:
        item.arrived()
    if lanes_ok:
        last.append(move(own_block, own_out, "rows", whole, rows_of(own_block.shape[0])))
    else:
        last.append(move(own_block, own_out, "rows", whole, lead))
    last[-1].start()
    for item in home + last:
        item.arrived()
    for item in home + open_rows + [own_rows] + chip_moves + own_chips + last:
        item.sent()


def finish(dqkv, own_grad, over_chips, over_rows, rows_open, counts, collective_id):
    count, chips, rows = counts["seq"], counts["chip"], counts["rows"]
    length, all_width = dqkv.shape
    width = all_width // 3
    lanes_ok = width % 128 == 0
    tokens, short = length // count, own_grad.shape[2]
    bf = jnp.bfloat16
    if lanes_ok:
        tokens_shape = (tokens, all_width * count)
        own_block, own_out = (short, all_width * count), (rows * short, all_width * count)
    else:
        tokens_shape = (count, tokens, all_width)
        own_block, own_out = (count, short, all_width), (rows, count, short, all_width)
    shares = [term.shape[1:] for term in over_rows]
    shares += [(term.shape[0], term.shape[1] // rows) for term in rows_open]
    blocks = [term.shape[1:] for term in over_chips]
    blocks += [(shape[0] // chips, shape[1]) for shape in shares]
    outs = [tokens_shape, own_out] + [(shape[0], shape[1] * rows) for shape in blocks]
    own_share = own_grad.shape[:1] + own_grad.shape[2:]
    scratch = [(rows,) + own_share, own_share, own_block]
    scratch += [(rows,) + shape for shape in shares] + shares
    scratch += [(chips,) + shape for shape in blocks] + blocks
    moves = 3 + 3 + 2 + len(rows_open) + len(shares) + len(blocks)
    longest = max(count, rows)
    arrays = [dqkv, own_grad, *over_chips, *over_rows, *rows_open]
    return pl.pallas_call(
        functools.partial(
            finish_kernel,
            counts,
            ((len(over_chips), len(over_rows)), len(rows_open)),
            lanes_ok,
        ),
        out_shape=[jax.ShapeDtypeStruct(shape, bf) for shape in outs],
        in_specs=[pl.BlockSpec(memory_space=pl.ANY)] * len(arrays),
        out_specs=[pl.BlockSpec(memory_space=pl.ANY)] * len(outs),
        scratch_shapes=[pltpu.VMEM(shape, bf) for shape in scratch]
        + [
            pltpu.SemaphoreType.DMA((len(over_chips) + len(over_rows),)),
            pltpu.SemaphoreType.DMA((moves,)),
            pltpu.SemaphoreType.DMA((moves, longest)),
            pltpu.SemaphoreType.DMA((moves, longest)),
        ],
        compiler_params=pltpu.CompilerParams(
            collective_id=collective_id, has_side_effects=True, vmem_limit_bytes=VMEM_LIMIT
        ),
    )(*arrays)


def vectors_kernel(counts, given_ref, out_ref, slots, total, own_sem, send_sem, recv_sem):
    greet(("seq", "rows"), counts)
    over_seq = Transfers(
        (given_ref, slots, "seq", lead, lead), counts, own_sem.at[0], send_sem.at[0], recv_sem.at[0]
    )
    over_seq.start()
    over_seq.arrived()
    total[...] = functools.reduce(jnp.add, [slots[i] for i in range(slots.shape[0])])
    over_rows = Transfers(
        (total, out_ref, "rows", whole, lead), counts, own_sem.at[1], send_sem.at[1], recv_sem.at[1]
    )
    over_rows.start()
    over_rows.arrived()
    over_seq.sent()
    over_rows.sent()


def sum_vectors(given, counts, collective_id):
    longest = max(counts["seq"], counts["rows"])
    block = given.shape[1:]
    return pl.pallas_call(
        functools.partial(vectors_kernel, counts),
        out_shape=jax.ShapeDtypeStruct((counts["rows"],) + block, jnp.float32),
        in_specs=[pl.BlockSpec(memory_space=pl.ANY)],
        out_specs=pl.BlockSpec(memory_space=pl.ANY),
        scratch_shapes=[
            pltpu.VMEM((counts["seq"],) + block, jnp.float32),
            pltpu.VMEM(block, jnp.float32),
            pltpu.SemaphoreType.DMA((2,)),
            pltpu.SemaphoreType.DMA((2, longest)),
            pltpu.SemaphoreType.DMA((2, longest)),
        ],
        compiler_params=pltpu.CompilerParams(collective_id=collective_id, has_side_effects=True),
    )(given)


def head_lanes(width):
    return lax.broadcasted_iota(jnp.int32, (1, width), 1) // DEPTH


def pick_head(values, head, width):
    if width == DEPTH:
        return values
    return jnp.where(head_lanes(width) == head, values, jnp.zeros_like(values))


def begin_of(start_ref, position):
    begin = jnp.zeros_like(position)
    for page in range(1, PAGES):
        begin = jnp.where(position >= start_ref[page], start_ref[page], begin)
    return begin


def as_row(column):
    return jnp.broadcast_to(column, (column.shape[0], 8)).T[:1]


def self_forward_kernel(qkv_ref, start_ref, out_ref, stat_ref):
    length, width = out_ref.shape
    heads = width // DEPTH
    blocks = length // BLOCK
    for index in range(blocks):
        rows = pl.ds(index * BLOCK, BLOCK)
        keys_end = (index + 1) * BLOCK
        query = qkv_ref[rows, 0:width]
        position = index * BLOCK + lax.broadcasted_iota(jnp.int32, (BLOCK, 1), 0)
        begin = begin_of(start_ref, position)
        if index == blocks - 1 or index <= 1:
            cuts = [(0, keys_end)]
        else:
            cuts = [(0, BLOCK), (BLOCK, index * BLOCK), (index * BLOCK, keys_end)]
        outs, stats = [], []
        for head in range(heads):
            query_head = pick_head(query, head, width) * jnp.bfloat16(SCALE)
            scores = []
            for low_end, high_end in cuts:
                part = dot_right(query_head, qkv_ref[low_end:high_end, width : 2 * width])
                if low_end == 0 or high_end == keys_end:
                    column = low_end + lax.broadcasted_iota(jnp.int32, part.shape, 1)
                    allowed = column >= begin
                    if high_end == keys_end:
                        allowed = allowed & (column <= position)
                    part = jnp.where(allowed, part, NEGATIVE)
                scores.append(part)
            top = functools.reduce(
                jnp.maximum, [jnp.max(part, axis=-1, keepdims=True) for part in scores]
            )
            total, mixed = 0.0, 0.0
            for (low_end, high_end), part in zip(cuts, scores):
                weight = jnp.exp(part - top)
                total = total + jnp.sum(weight, axis=-1, keepdims=True)
                mixed = mixed + dot_plain(
                    low(weight), qkv_ref[low_end:high_end, 2 * width : 3 * width]
                )
            outs.append(mixed / total)
            stats.append(top + jnp.log(total))
        merged = outs[0]
        for head in range(1, heads):
            merged = jnp.where(head_lanes(width) == head, outs[head], merged)
        out_ref[rows, :] = low(merged)
        for head in range(heads):
            stat_ref[head : head + 1, rows] = as_row(stats[head])


def self_forward(qkv, starts):
    length, width = qkv.shape[0], qkv.shape[1] // 3
    heads = width // DEPTH
    return pl.pallas_call(
        self_forward_kernel,
        out_shape=(
            jax.ShapeDtypeStruct((length, width), jnp.bfloat16),
            jax.ShapeDtypeStruct((heads, length), jnp.float32),
        ),
        in_specs=[
            pl.BlockSpec(memory_space=pltpu.VMEM),
            pl.BlockSpec(memory_space=pltpu.SMEM),
        ],
        out_specs=[pl.BlockSpec(memory_space=pltpu.VMEM)] * 2,
        compiler_params=pltpu.CompilerParams(vmem_limit_bytes=VMEM_LIMIT),
    )(qkv, starts)


def self_backward_kernel(counts, hosted, *refs):
    size = len(hosted)
    qkv_ref, out_ref, grad_ref, start_ref, stat_ref = refs[:5]
    sent, dqkv_ref, stacks = refs[5 : 5 + size], refs[5 + size], refs[6 + size : 6 + 2 * size]
    dk_ref, dv_ref, own_sem, send_sem, recv_sem = refs[6 + 2 * size :]
    length, width = out_ref.shape
    heads = width // DEPTH
    blocks = length // BLOCK
    greet(("seq", "rows"), counts)
    moves = []
    for index, ((axis, how), ref, stack) in enumerate(zip(hosted, sent, stacks)):
        source = rows_of(stack.shape[1]) if how == "rows" else columns_of(stack.shape[2])
        part = (ref, stack, axis, source, lead)
        moves.append(
            Transfers(part, counts, own_sem.at[index], send_sem.at[index], recv_sem.at[index])
        )
        moves[-1].start()
    dk_ref[...] = jnp.zeros_like(dk_ref)
    dv_ref[...] = jnp.zeros_like(dv_ref)

    def query_block(index, carry):
        rows = pl.ds(pl.multiple_of(index * BLOCK, BLOCK), BLOCK)
        query = qkv_ref[rows, 0:width]
        grad = grad_ref[rows, :]
        product = (wide(grad) * wide(out_ref[rows, :])).T
        position = index * BLOCK + lax.broadcasted_iota(jnp.int32, (1, BLOCK), 1)
        begin = begin_of(start_ref, position)
        query_heads = [pick_head(query, head, width) * jnp.bfloat16(SCALE) for head in range(heads)]
        grad_heads = [pick_head(grad, head, width) for head in range(heads)]
        stats = [stat_ref[head : head + 1, rows] for head in range(heads)]
        deltas = [
            jnp.sum(product[head * DEPTH : (head + 1) * DEPTH, :], axis=0, keepdims=True)
            for head in range(heads)
        ]

        def key_block(key_index, sums):
            keys = pl.ds(pl.multiple_of(key_index * BLOCK, BLOCK), BLOCK)
            key = qkv_ref[keys, width : 2 * width]
            value = qkv_ref[keys, 2 * width : 3 * width]
            row = key_index * BLOCK + lax.broadcasted_iota(jnp.int32, (BLOCK, 1), 0)
            allowed = (row >= begin) & (row <= position)
            dk_part, dv_part, found = 0.0, 0.0, []
            for head in range(heads):
                scores = jnp.where(allowed, dot_right(key, query_heads[head]), NEGATIVE)
                prob = jnp.exp(scores - stats[head])
                dv_part = dv_part + dot_plain(low(prob), grad_heads[head])
                grad_prob = dot_right(value, grad_heads[head])
                grad_score = low(prob * (grad_prob - deltas[head]))
                dk_part = dk_part + dot_plain(grad_score, query_heads[head])
                found.append(sums[head] + dot_left(grad_score, key))
            dk_ref[keys, :] += dk_part
            dv_ref[keys, :] += dv_part
            return tuple(found)

        zero = tuple(jnp.zeros((BLOCK, width), jnp.float32) for _ in range(heads))
        sums = lax.fori_loop(0, index + 1, key_block, zero)
        merged = sums[0]
        for head in range(1, heads):
            merged = jnp.where(head_lanes(width) == head, sums[head], merged)
        dqkv_ref[rows, 0:width] = low(merged * SCALE)
        return carry

    lax.fori_loop(0, blocks, query_block, 0)
    dqkv_ref[:, width : 2 * width] = low(dk_ref[...])
    dqkv_ref[:, 2 * width : 3 * width] = low(dv_ref[...])
    for item in moves:
        item.arrived()
    for item in moves:
        item.sent()


def self_backward(qkv, out, grad, starts, stats, sent, hosted, counts, collective_id):
    length, width = out.shape
    stacks = []
    for array, (axis, how) in zip(sent, hosted):
        rows, columns = array.shape
        total = counts[axis]
        block = (rows // total, columns) if how == "rows" else (rows, columns // total)
        stacks.append(jax.ShapeDtypeStruct((total,) + block, array.dtype))
    longest = max(counts["seq"], counts["rows"])
    vmem, anywhere = pl.BlockSpec(memory_space=pltpu.VMEM), pl.BlockSpec(memory_space=pl.ANY)
    return pl.pallas_call(
        functools.partial(self_backward_kernel, counts, hosted),
        out_shape=[jax.ShapeDtypeStruct((length, 3 * width), jnp.bfloat16), *stacks],
        in_specs=[vmem, vmem, vmem, pl.BlockSpec(memory_space=pltpu.SMEM), vmem]
        + [anywhere] * len(sent),
        out_specs=[vmem] + [anywhere] * len(sent),
        scratch_shapes=[pltpu.VMEM((length, width), jnp.float32)] * 2
        + [
            pltpu.SemaphoreType.DMA((len(sent),)),
            pltpu.SemaphoreType.DMA((len(sent), longest)),
            pltpu.SemaphoreType.DMA((len(sent), longest)),
        ],
        compiler_params=pltpu.CompilerParams(
            collective_id=collective_id, has_side_effects=True, vmem_limit_bytes=VMEM_LIMIT
        ),
    )(qkv, out, grad, starts, stats, *sent)


def cross_forward_kernel(query_ref, key_ref, value_ref, own_key_ref, own_value_ref, out_ref, stat_ref):
    tokens = query_ref.shape[0] - SLOTS
    width = query_ref.shape[1]
    for begin, size, keys, values in (
        (0, tokens, key_ref, value_ref),
        (tokens, SLOTS, own_key_ref, own_value_ref),
    ):
        query = query_ref[begin : begin + size, :]
        outs = []
        for head in range(width // DEPTH):
            query_head = pick_head(query, head, width) * jnp.bfloat16(SCALE)
            scores = dot_right(query_head, keys[...])
            column = lax.broadcasted_iota(jnp.int32, scores.shape, 1)
            scores = jnp.where(column < PAGE_TOK, scores, NEGATIVE)
            top = jnp.max(scores, axis=-1, keepdims=True)
            weight = jnp.exp(scores - top)
            total = jnp.sum(weight, axis=-1, keepdims=True)
            outs.append(dot_plain(low(weight), values[...]) / total)
            stat_ref[0, head : head + 1, begin : begin + size] = as_row(top + jnp.log(total))
        merged = outs[0]
        for head in range(1, len(outs)):
            merged = jnp.where(head_lanes(width) == head, outs[head], merged)
        out_ref[begin : begin + size, :] = low(merged)


def cross_forward(query, kv_big, kv_own):
    rows, features = query.shape
    pair = 2 * DEPTH
    steps = features // pair
    tall = pl.BlockSpec((rows, pair), lambda i: (0, i))
    keys = pl.BlockSpec((PAGE_PAD, pair), lambda i: (0, i))
    values = pl.BlockSpec((PAGE_PAD, pair), lambda i: (0, i + steps))
    return pl.pallas_call(
        cross_forward_kernel,
        grid=(steps,),
        out_shape=(
            jax.ShapeDtypeStruct((rows, features), jnp.bfloat16),
            jax.ShapeDtypeStruct((steps, 2, rows), jnp.float32),
        ),
        in_specs=[tall, keys, values, keys, values],
        out_specs=[tall, pl.BlockSpec((1, 2, rows), lambda i: (i, 0, 0))],
        compiler_params=pltpu.CompilerParams(vmem_limit_bytes=VMEM_LIMIT),
    )(query, kv_big, kv_big, kv_own, kv_own)


def cross_backward_kernel(
    query_ref,
    key_ref,
    value_ref,
    own_key_ref,
    own_value_ref,
    out_ref,
    grad_ref,
    stat_ref,
    dq_ref,
    dk_ref,
    dv_ref,
    own_dk_ref,
    own_dv_ref,
):
    tokens = query_ref.shape[0] - SLOTS
    width = query_ref.shape[1]
    row = lax.broadcasted_iota(jnp.int32, (PAGE_PAD, 1), 0)
    for begin, size, keys, values, dk_out, dv_out in (
        (0, tokens, key_ref, value_ref, dk_ref, dv_ref),
        (tokens, SLOTS, own_key_ref, own_value_ref, own_dk_ref, own_dv_ref),
    ):
        rows = slice(begin, begin + size)
        query, grad = query_ref[rows, :], grad_ref[rows, :]
        product = (wide(grad) * wide(out_ref[rows, :])).T
        dk_sum, dv_sum, found = 0.0, 0.0, []
        for head in range(width // DEPTH):
            query_head = pick_head(query, head, width) * jnp.bfloat16(SCALE)
            grad_head = pick_head(grad, head, width)
            delta = jnp.sum(product[head * DEPTH : (head + 1) * DEPTH, :], axis=0, keepdims=True)
            scores = dot_right(keys[...], query_head)
            scores = jnp.where(row < PAGE_TOK, scores, NEGATIVE)
            prob = jnp.exp(scores - stat_ref[0, head : head + 1, rows])
            dv_sum = dv_sum + dot_plain(low(prob), grad_head)
            grad_prob = dot_right(values[...], grad_head)
            grad_score = low(prob * (grad_prob - delta))
            dk_sum = dk_sum + dot_plain(grad_score, query_head)
            found.append(dot_left(grad_score, keys[...]))
        merged = found[0]
        for head in range(1, len(found)):
            merged = jnp.where(head_lanes(width) == head, found[head], merged)
        dq_ref[rows, :] = low(merged * SCALE)
        dk_out[...] = low(dk_sum)
        dv_out[...] = low(dv_sum)


def cross_backward(query, kv_big, kv_own, out, grad, stats):
    rows, features = query.shape
    pair = 2 * DEPTH
    steps = features // pair
    tall = pl.BlockSpec((rows, pair), lambda i: (0, i))
    keys = pl.BlockSpec((PAGE_PAD, pair), lambda i: (0, i))
    values = pl.BlockSpec((PAGE_PAD, pair), lambda i: (0, i + steps))
    page = jax.ShapeDtypeStruct((PAGE_PAD, features), jnp.bfloat16)
    return pl.pallas_call(
        cross_backward_kernel,
        grid=(steps,),
        out_shape=(jax.ShapeDtypeStruct((rows, features), jnp.bfloat16), page, page, page, page),
        in_specs=[
            tall,
            keys,
            values,
            keys,
            values,
            tall,
            tall,
            pl.BlockSpec((1, 2, rows), lambda i: (i, 0, 0)),
        ],
        out_specs=[tall, keys, keys, keys, keys],
        compiler_params=pltpu.CompilerParams(vmem_limit_bytes=VMEM_LIMIT),
    )(query, kv_big, kv_big, kv_own, kv_own, out, grad, stats)


def body(
    inputs,
    memory,
    out_grad,
    segment_ids,
    page_order,
    norm1_gain,
    norm1_bias,
    qkv_weight,
    qv_bias,
    self_out_weight,
    self_out_bias,
    norm2_gain,
    norm2_bias,
    cross_q_weight,
    cross_q_bias,
    cross_kv_weight,
    cross_v_bias,
    cross_out_weight,
    cross_out_bias,
    norm3_gain,
    norm3_bias,
    fc1_weight,
    fc1_bias,
    fc2_weight,
    fc2_bias,
):
    tokens, features = inputs.shape[1:]
    count = lax.axis_size("seq")
    me = lax.axis_index("seq")
    length = tokens * count
    width = features // count
    rows_count = lax.axis_size("rows")
    counts = {"seq": count, "chip": count // 2, "rows": rows_count}
    core = me % 2

    def pair_sum(first, second):
        size = first.shape[1] // count

        def blocks_of(which):
            return jnp.concatenate(
                [
                    lax.dynamic_slice_in_dim(first, (2 * chip + which) * size, size, 1)
                    for chip in range(count // 2)
                ],
                axis=1,
            )

        given = swap(low(dot_left(blocks_of(1 - core), second)))
        return low(dot_left(blocks_of(core), second) + wide(given))

    def swap(value):
        return lax.ppermute(value, "seq", [(i, i ^ 1) for i in range(count)])

    def after(value, other):
        return lax.optimization_barrier((value, other))[0]

    mem_rows = memory.shape[1]
    sharers = PAGE_TOK // mem_rows
    row_segs = segment_ids[0]
    row_pages = page_order[0]
    gain_one, shift_one = wide(norm1_gain), wide(norm1_bias)
    gain_two, shift_two = wide(norm2_gain), wide(norm2_bias)
    gain_three, shift_three = wide(norm3_gain), wide(norm3_bias)

    starts = jnp.sum(row_segs[None, :] < jnp.arange(PAGES)[:, None], axis=1, dtype=jnp.int32)
    big_page = row_segs[length // 2]
    big_start = jnp.sum(row_segs < big_page)
    own_page = lax.dynamic_index_in_dim(row_pages, me // sharers, 0, keepdims=False)
    slot = jnp.arange(SLOTS)
    in_front = (slot < big_start)[:, None]
    slot_segs = jnp.where(slot < big_start, row_segs[:SLOTS], row_segs[length - SLOTS :])
    slot_mine = (slot_segs == own_page) & (slot * sharers // SLOTS == me % sharers)
    home_segs = lax.dynamic_slice_in_dim(row_segs, me * tokens, tokens, 0)
    active = jnp.concatenate((home_segs == big_page, slot_mine))[:, None]
    is_first, is_last = me == 0, me == count - 1

    def slots_of(front, back):
        return jnp.where(in_front, front, back)

    mem_own = memory[0]
    mem_page = mem_own
    if sharers > 1:
        groups = [[g * sharers + s for s in range(sharers)] for g in range(count // sharers)]
        mem_page = lax.all_gather(mem_own, "seq", axis=0, tiled=True, axis_index_groups=groups)
    mem_page = jnp.pad(mem_page, ((0, PAGE_PAD - PAGE_TOK), (0, 0)))
    gives_big = (own_page == big_page) & (me % sharers == 0)

    x_own = inputs[0]
    x_all = gather_rows(x_own, count, 0)

    half = PAGE_PAD // 2
    masked_page = jnp.where(gives_big, mem_page, jnp.zeros_like(mem_page)).reshape(2, half, -1)
    pair_page = masked_page[core] + swap(masked_page[1 - core])
    at_end = jnp.where(core == 0, is_first, is_last)
    end_grad = jnp.where(core == 0, out_grad[0, :SLOTS], out_grad[0, tokens - SLOTS :])
    sent = jnp.concatenate((pair_page, jnp.where(at_end, end_grad, jnp.zeros_like(end_grad))))
    same_core = [[2 * chip + which for chip in range(count // 2)] for which in range(2)]
    mine = lax.psum(after(sent, x_all), "seq", axis_index_groups=same_core)
    theirs = swap(mine)
    zeroth, first = jnp.where(core == 0, mine, theirs), jnp.where(core == 0, theirs, mine)
    mem_big = jnp.concatenate((zeroth[:half], first[:half]))
    front_grad, back_grad = zeroth[half:], first[half:]

    qkv_own_weight = jnp.concatenate(
        [
            lax.dynamic_slice_in_dim(qkv_weight, part * features + me * width, width, 1)
            for part in range(3)
        ],
        axis=1,
    )
    qkv_own_bias = jnp.concatenate(
        (
            lax.dynamic_slice_in_dim(qv_bias, me * width, width, 0),
            jnp.zeros((width,), jnp.bfloat16),
            lax.dynamic_slice_in_dim(qv_bias, features + me * width, width, 0),
        )
    )
    normed_all = low(norm_forward(wide(x_all), gain_one, shift_one))
    qkv = low(dot_plain(normed_all, qkv_own_weight) + wide(qkv_own_bias))
    mixed, mixed_stats = self_forward(qkv, starts)
    bf = jnp.bfloat16
    lanes_ok = width % 128 == 0
    chosen = slots_of(mixed[:SLOTS], mixed[length - SLOTS :])
    if lanes_ok:
        blocks_mixed, slots_mixed = exchange(
            (mixed, chosen),
            (
                jax.ShapeDtypeStruct((tokens, features), bf),
                jax.ShapeDtypeStruct((SLOTS, features), bf),
            ),
            (
                (1, 1, "seq", whole, columns_of(width)),
                (0, 0, "seq", rows_of(tokens), columns_of(width)),
            ),
            counts,
            1,
        )
    else:
        blocks_mixed, slots_mixed = exchange(
            (mixed, chosen),
            (
                jax.ShapeDtypeStruct((count, tokens, width), bf),
                jax.ShapeDtypeStruct((count, SLOTS, width), bf),
            ),
            ((1, 1, "seq", whole, lead), (0, 0, "seq", rows_of(tokens), lead)),
            counts,
            1,
        )
        blocks_mixed, slots_mixed = (
            blocks.transpose(1, 0, 2).reshape(blocks.shape[1], -1)
            for blocks in (blocks_mixed, slots_mixed)
        )
    attended = jnp.concatenate((blocks_mixed, slots_mixed))
    resid = wide(
        jnp.concatenate((x_own, slots_of(x_all[:SLOTS], x_all[length - SLOTS :])))
    )
    resid_one = resid + dot_plain(attended, self_out_weight) + wide(self_out_bias)
    normed_two = low(norm_forward(resid_one, gain_two, shift_two))
    cross_queries = low(dot_plain(normed_two, cross_q_weight) + wide(cross_q_bias))
    kv_shift = jnp.concatenate((jnp.zeros((features,), jnp.float32), wide(cross_v_bias)))
    kv_big = low(dot_plain(mem_big, cross_kv_weight) + kv_shift)
    kv_own = low(dot_plain(mem_page, cross_kv_weight) + kv_shift)
    cross_low, cross_stats = cross_forward(cross_queries, kv_big, kv_own)
    resid_two = resid_one + dot_plain(cross_low, cross_out_weight) + wide(cross_out_bias)
    normed_three = low(norm_forward(resid_two, gain_three, shift_three))
    pre_act = dot_plain(normed_three, fc1_weight) + wide(fc1_bias)
    hidden_act = low(gelu_exact(pre_act))
    final = low(resid_two + dot_plain(hidden_act, fc2_weight) + wide(fc2_bias))

    grad_out = jnp.concatenate((out_grad[0], slots_of(front_grad, back_grad)))
    grad_out = jnp.where(active, grad_out, jnp.zeros_like(grad_out))
    grad_act = dot_right(grad_out, fc2_weight)
    _, gelu_pull = jax.vjp(gelu_exact, pre_act)
    grad_pre = low(gelu_pull(grad_act)[0])
    grad_fc2_w = pair_sum(hidden_act, grad_out)
    fc2_share = lax.psum_scatter(grad_fc2_w, "rows", scatter_dimension=1, tiled=True)
    grad_fc2_b = jnp.sum(wide(grad_out), axis=0)
    grad_fc1_w = pair_sum(normed_three, grad_pre)
    fc1_share = lax.psum_scatter(grad_fc1_w, "rows", scatter_dimension=1, tiled=True)
    grad_fc1_b = jnp.sum(wide(grad_pre), axis=0)
    grad_two_norm, grad_gain_three, grad_shift_three = norm_backward(
        resid_two, gain_three, shift_three, dot_right(grad_pre, fc1_weight)
    )
    grad_resid_two = wide(grad_out) + grad_two_norm
    grad_branch_two = low(grad_resid_two)
    grad_co_w = pair_sum(cross_low, grad_branch_two)
    grad_co_b = jnp.sum(wide(grad_branch_two), axis=0)
    grad_cross_low = low(dot_right(grad_branch_two, cross_out_weight))
    grad_cross_low = after(grad_cross_low, (grad_fc1_w, grad_fc2_w))
    grad_cross_q, big_dk, big_dv, own_dk, own_dv = cross_backward(
        cross_queries, kv_big, kv_own, cross_low, grad_cross_low, cross_stats
    )
    grad_cq_w = pair_sum(normed_two, grad_cross_q)
    grad_cq_b = jnp.sum(wide(grad_cross_q), axis=0)
    grad_one_norm, grad_gain_two, grad_shift_two = norm_backward(
        resid_one, gain_two, shift_two, dot_right(grad_cross_q, cross_q_weight)
    )
    grad_resid_one = grad_resid_two + grad_one_norm
    grad_branch_one = low(grad_resid_one)
    grad_o_w = pair_sum(attended, grad_branch_one)
    grad_o_b = jnp.sum(wide(grad_branch_one), axis=0)
    grad_attended = low(dot_right(grad_branch_one, self_out_weight))
    if lanes_ok:
        given, home_part, slot_part = (grad_attended,), (0, 0), (0, 1)

        def piece(first, size):
            def find(ref, index):
                return ref.at[
                    first : first + size, pl.ds(pl.multiple_of(index * width, width), width)
                ]

            return find

        pieces = piece(0, tokens), piece(tokens, SLOTS)
    else:
        by_device = grad_attended.reshape(-1, count, width).transpose(1, 0, 2)
        given, home_part, slot_part = (by_device[:, :tokens], by_device[:, tokens:]), (0, 0), (1, 1)
        pieces = lead, lead
    grad_mixed, slots_grad = exchange(
        given,
        (
            jax.ShapeDtypeStruct((length, width), bf),
            jax.ShapeDtypeStruct((count, SLOTS, width), bf),
        ),
        (
            home_part + ("seq", pieces[0], rows_of(tokens)),
            slot_part + ("seq", pieces[1], lead),
        ),
        counts,
        2,
    )
    slots_grad = low(jnp.sum(wide(slots_grad), axis=0))
    no_slots = jnp.zeros_like(slots_grad)
    grad_mixed = jnp.concatenate(
        (
            grad_mixed[:SLOTS] + jnp.where(in_front, slots_grad, no_slots),
            grad_mixed[SLOTS : length - SLOTS],
            grad_mixed[length - SLOTS :] + jnp.where(in_front, no_slots, slots_grad),
        )
    )
    dqkv, *stacks = self_backward(
        qkv,
        mixed,
        grad_mixed,
        starts,
        mixed_stats,
        (fc2_share, fc1_share, grad_co_w, grad_cq_w, grad_o_w),
        (("chip", "rows"), ("chip", "rows")) + (("rows", "columns"),) * 3,
        counts,
        3,
    )

    slot_final = jnp.where(active[tokens:], final[tokens:], jnp.zeros_like(final[tokens:]))
    own_half = jnp.where(core == 0, big_dk, big_dv)
    own_half = own_half + swap(jnp.where(core == 0, big_dv, big_dk))
    slot_half = jnp.where(core == 0, slot_final, low(grad_resid_one[tokens:]))
    slot_half = slot_half + swap(jnp.where(core == 0, low(grad_resid_one[tokens:]), slot_final))
    mine = lax.psum(
        jnp.concatenate((own_half[:PAGE_TOK], slot_half)), "seq", axis_index_groups=same_core
    )
    mine = after(mine, dqkv)
    theirs = swap(mine)
    zeroth, first = jnp.where(core == 0, mine, theirs), jnp.where(core == 0, theirs, mine)
    big_dk, big_dv = zeroth[:PAGE_TOK], first[:PAGE_TOK]
    slot_final, slot_grad = zeroth[PAGE_TOK:], first[PAGE_TOK:]
    grad_ckv = jnp.where(
        gives_big,
        jnp.concatenate((big_dk, big_dv), axis=1),
        jnp.concatenate((own_dk[:PAGE_TOK], own_dv[:PAGE_TOK]), axis=1),
    )
    if sharers > 1:
        grad_ckv = lax.psum_scatter(
            grad_ckv, "seq", scatter_dimension=0, tiled=True, axis_index_groups=groups
        )
    grad_ckv_w = pair_sum(mem_own, grad_ckv)
    grad_cv_b = jnp.sum(wide(grad_ckv[:, features:]), axis=0)
    memory_grad = dot_right(grad_ckv, cross_kv_weight)[None]

    def at_home(own, returned):
        front = is_first & in_front
        back = is_last & ~in_front
        head = jnp.where(front, returned.astype(own.dtype), own[:SLOTS])
        tail = jnp.where(back, returned.astype(own.dtype), own[tokens - SLOTS :])
        return jnp.concatenate((head, own[SLOTS : tokens - SLOTS], tail))

    layer_out = at_home(final[:tokens], slot_final)[None]
    grad_home = at_home(grad_resid_one[:tokens], slot_grad)

    grad_qkv_w = low(dot_left(normed_all, dqkv))
    grad_qkv_w = grad_qkv_w.reshape(count, rows_count, -1, 3 * width)
    column_sums = jnp.sum(wide(dqkv), axis=0)

    def in_features(part):
        return lax.dynamic_update_slice_in_dim(
            jnp.zeros((features,), jnp.float32),
            column_sums[part * width : (part + 1) * width],
            me * width,
            0,
        )

    grad_qv_b = jnp.concatenate((in_features(0), in_features(2)))

    grad_qkv, qkv_w, fc2_w, fc1_w, co_w, cq_w, o_w, ckv_w = finish(
        dqkv, grad_qkv_w, stacks[:2], stacks[2:], (grad_ckv_w,), counts, 4
    )
    if not lanes_ok:
        grad_qkv = grad_qkv.reshape(count, tokens, 3, width).transpose(1, 2, 0, 3)
        grad_qkv = grad_qkv.reshape(tokens, 3 * features)
        qkv_w = qkv_w.reshape(rows_count, count, -1, 3, width).transpose(0, 2, 3, 1, 4)
        qkv_w = qkv_w.reshape(-1, 3 * features)
    qkv_w, fc1_w, fc2_w, o_w, cq_w, co_w, ckv_w = [
        wide(term) for term in (qkv_w, fc1_w, fc2_w, o_w, cq_w, co_w, ckv_w)
    ]
    grad_in_norm, grad_gain_one, grad_shift_one = norm_backward(
        wide(x_own), gain_one, shift_one, dot_right(grad_qkv, qkv_weight)
    )
    input_grad = (grad_home + grad_in_norm)[None]

    vectors = (
        grad_gain_one,
        grad_shift_one,
        grad_qv_b,
        grad_o_b,
        grad_gain_two,
        grad_shift_two,
        grad_cq_b,
        grad_cv_b,
        grad_co_b,
        grad_gain_three,
        grad_shift_three,
        grad_fc1_b,
        grad_fc2_b,
    )
    joined = jnp.concatenate([vector.reshape(count, -1) for vector in vectors], axis=1)
    joined = jnp.pad(joined, ((0, 0), (0, -joined.shape[1] % 1024))).reshape(count, 8, -1)
    joined = jnp.sum(sum_vectors(joined, counts, 5), axis=0).reshape(-1)
    pieces, offset = [], 0
    for vector in vectors:
        size = vector.shape[0] // count
        pieces.append(joined[offset : offset + size])
        offset += size
    g1, s1, qvb, ob, g2, s2, cqb, cvb, cob, g3, s3, f1b, f2b = pieces
    return (
        layer_out,
        input_grad,
        memory_grad,
        g1,
        s1,
        qkv_w,
        qvb,
        o_w,
        ob,
        g2,
        s2,
        cq_w,
        cqb,
        ckv_w,
        cvb,
        co_w,
        cob,
        g3,
        s3,
        fc1_w,
        f1b,
        fc2_w,
        f2b,
    )


def solution(mesh):
    split = P("rows", "seq", None)
    in_specs = (split, split, split, P("rows", None), P("rows", None)) + (P(),) * 20
    vector, matrix = P("seq"), P("seq", None)
    out_specs = (split, split, split) + (
        vector,
        vector,
        matrix,
        vector,
        matrix,
        vector,
        vector,
        vector,
        matrix,
        vector,
        matrix,
        vector,
        matrix,
        vector,
        vector,
        vector,
        matrix,
        vector,
        matrix,
        vector,
    )
    return jax.shard_map(body, mesh=mesh, in_specs=in_specs, out_specs=out_specs, check_vma=False)
```

```python
import functools

import jax
import jax.numpy as jnp
from jax import lax
from jax.experimental import pallas as pl
from jax.experimental.pallas import tpu as pltpu
from jax.sharding import PartitionSpec as P

HEADS = 16
DEPTH = 64
PAGES = 8
PAGE_TOK = 588
PAGE_PAD = 640
SLOTS = 128
BLOCK = 256


NEGATIVE = -1e30
SCALE = 0.125
EPSILON = 1e-05
MESH = pl.DeviceIdType.MESH
VMEM_LIMIT = 56 * 1024 * 1024


def norm_forward(values, gain, shift):
    center = values - jnp.mean(values, axis=-1, keepdims=True)
    spread = jnp.mean(center * center, axis=-1, keepdims=True)
    return center * lax.rsqrt(spread + EPSILON) * gain + shift


def gelu_exact(values):
    return jax.nn.gelu(values, approximate=False)


def norm_backward(values, gain, shift, grad_normed):
    _, pullback = jax.vjp(norm_forward, values, gain, shift)
    return pullback(grad_normed)


def dot_plain(first, second):
    return jnp.dot(first, second, preferred_element_type=jnp.float32)


def dot_left(first, second):
    return lax.dot_general(
        first, second, (((0,), (0,)), ((), ())), preferred_element_type=jnp.float32
    )


def dot_right(first, second):
    return lax.dot_general(
        first, second, (((1,), (1,)), ((), ())), preferred_element_type=jnp.float32
    )


def low(values):
    return values.astype(jnp.bfloat16)


def wide(values):
    return values.astype(jnp.float32)


def place(index):
    return (lax.axis_index("rows"), index)


def gather_kernel(count, block_ref, whole_ref, own_sem, send_sem, recv_sem):
    rows = block_ref.shape[0]
    me = lax.axis_index("seq")
    chip, core, chips = me // 2, me % 2, count // 2
    other = me + 1 - 2 * core
    barrier = pltpu.get_barrier_semaphore()

    def block(index):
        return whole_ref.at[pl.ds(index * rows, rows)]

    pl.semaphore_signal(barrier, inc=1, device_id=place(other), device_id_type=MESH)

    @pl.when(chip > 0)
    def _():
        pl.semaphore_signal(barrier, inc=1, device_id=place(me - 2), device_id_type=MESH)

    @pl.when(chip < chips - 1)
    def _():
        pl.semaphore_signal(barrier, inc=1, device_id=place(me + 2), device_id_type=MESH)

    peers = 1 + jnp.where(chip > 0, 1, 0) + jnp.where(chip < chips - 1, 1, 0)
    pl.semaphore_wait(barrier, peers)
    own = pltpu.make_async_copy(block_ref, block(me), own_sem)
    own.start()

    def copy(lane, source, target, from_own=False):
        there = block(2 * source + core)
        return pltpu.make_async_remote_copy(
            src_ref=block_ref if from_own else there,
            dst_ref=there,
            send_sem=send_sem.at[lane, source],
            recv_sem=recv_sem.at[lane, source],
            device_id=place(target),
            device_id_type=MESH,
        )

    def right(source, from_own=False):
        return copy(0, source, me + 2, from_own)

    def left(source, from_own=False):
        return copy(1, source, me - 2, from_own)

    def across(source, from_own=False):
        return copy(2, source, other, from_own)

    @pl.when(chip < chips - 1)
    def _():
        right(chip, True).start()

    @pl.when(chip > 0)
    def _():
        left(chip, True).start()

    across(chip, True).start()
    for step in range(1, chips):

        @pl.when(chip - step >= 0)
        def _():
            right(chip - step).wait_recv()

            @pl.when(chip < chips - 1)
            def _():
                right(chip - step).start()

            across(chip - step).start()

        @pl.when(chip + step < chips)
        def _():
            left(chip + step).wait_recv()

            @pl.when(chip > 0)
            def _():
                left(chip + step).start()

            across(chip + step).start()

    own.wait()
    for source in range(chips):
        there = block(2 * source + 1 - core)
        pltpu.make_async_remote_copy(
            src_ref=there,
            dst_ref=there,
            send_sem=send_sem.at[2, source],
            recv_sem=recv_sem.at[2, source],
            device_id=place(other),
            device_id_type=MESH,
        ).wait_recv()
        across(source).wait_send()

        @pl.when((source <= chip) & (chip < chips - 1))
        def _():
            right(source).wait_send()

        @pl.when((source >= chip) & (chip > 0))
        def _():
            left(source).wait_send()


def gather_rows(block_in, count, collective_id):
    rows, width = block_in.shape
    return pl.pallas_call(
        functools.partial(gather_kernel, count),
        out_shape=jax.ShapeDtypeStruct((count * rows, width), block_in.dtype),
        in_specs=[pl.BlockSpec(memory_space=pl.ANY)],
        out_specs=pl.BlockSpec(memory_space=pl.ANY),
        scratch_shapes=[
            pltpu.SemaphoreType.DMA,
            pltpu.SemaphoreType.DMA((3, count // 2)),
            pltpu.SemaphoreType.DMA((3, count // 2)),
        ],
        compiler_params=pltpu.CompilerParams(
            collective_id=collective_id, has_side_effects=True
        ),
    )(block_in)


AXES = {"seq": 1, "chip": 1, "rows": 0}


def peer(axis, step, counts):
    row, me = lax.axis_index("rows"), lax.axis_index("seq")
    if axis == "rows":
        there = lax.rem(row + step, counts["rows"])
        return (there, me), there
    if axis == "seq":
        there = lax.rem(me + step, counts["seq"])
        return (row, there), there
    there = lax.rem(me // 2 + step, counts["chip"])
    return (row, there * 2 + me % 2), there


def own_place(axis):
    if axis == "rows":
        return lax.axis_index("rows")
    return lax.axis_index("seq") if axis == "seq" else lax.axis_index("seq") // 2


def whole(ref, index):
    return ref


def lead(ref, index):
    return ref.at[index]


def second_dim(ref, index):
    return ref.at[:, index]


def rows_of(size, first=0, lanes=None):
    def find(ref, index):
        rows = pl.ds(pl.multiple_of(index * size, size), size)
        return ref.at[rows] if lanes is None else ref.at[rows, first : first + lanes]

    return find


def columns_of(size, first=0):
    def find(ref, index):
        return ref.at[:, pl.ds(pl.multiple_of(first + index * size, size), size)]

    return find


def greet(axes, counts):
    barrier = pltpu.get_barrier_semaphore()
    total = 0
    for axis in axes:
        for step in range(1, counts[axis]):
            pl.semaphore_signal(
                barrier, inc=1, device_id=peer(axis, step, counts)[0], device_id_type=MESH
            )
            total += 1
    pl.semaphore_wait(barrier, total)


def steps_of(total):
    return sorted(range(1, total), key=lambda step: -min(step, total - step))


class Transfers:
    def __init__(self, part, counts, own_sem, send_sem, recv_sem):
        from_ref, to_ref, axis, source, target = part
        here = own_place(axis)
        self.own = pltpu.make_async_copy(source(from_ref, here), target(to_ref, here), own_sem)
        self.remote = []
        for step in steps_of(counts[axis]):
            device, there = peer(axis, step, counts)
            self.remote.append(
                pltpu.make_async_remote_copy(
                    src_ref=source(from_ref, there),
                    dst_ref=target(to_ref, here),
                    send_sem=send_sem.at[step],
                    recv_sem=recv_sem.at[step],
                    device_id=device,
                    device_id_type=MESH,
                )
            )

    def start(self):
        for copy in self.remote:
            copy.start()
        self.own.start()

    def arrived(self):
        self.own.wait()
        for copy in self.remote:
            copy.wait_recv()

    def sent(self):
        for copy in self.remote:
            copy.wait_send()


def axes_of(axes):
    return tuple(axis for axis in ("seq", "rows") if axis in axes)


def exchange_kernel(counts, ins_count, parts, *refs):
    outs_count = len({part[1] for part in parts})
    ins, outs = refs[:ins_count], refs[ins_count : ins_count + outs_count]
    own_sem, send_sem, recv_sem = refs[ins_count + outs_count :]
    greet(axes_of([part[2] for part in parts]), counts)
    moves = [
        Transfers(
            (ins[part[0]], outs[part[1]]) + part[2:],
            counts,
            own_sem.at[index],
            send_sem.at[index],
            recv_sem.at[index],
        )
        for index, part in enumerate(parts)
    ]
    for move in moves:
        move.start()
    for move in moves:
        move.arrived()
    for move in moves:
        move.sent()


def exchange(arrays, shapes, parts, counts, collective_id):
    longest = max(counts[part[2]] for part in parts)
    return pl.pallas_call(
        functools.partial(exchange_kernel, counts, len(arrays), parts),
        out_shape=shapes,
        in_specs=[pl.BlockSpec(memory_space=pl.ANY)] * len(arrays),
        out_specs=[pl.BlockSpec(memory_space=pl.ANY)] * len(shapes),
        scratch_shapes=[
            pltpu.SemaphoreType.DMA((len(parts),)),
            pltpu.SemaphoreType.DMA((len(parts), longest)),
            pltpu.SemaphoreType.DMA((len(parts), longest)),
        ],
        compiler_params=pltpu.CompilerParams(
            collective_id=collective_id, has_side_effects=True
        ),
    )(*arrays)


def add_slots(ref):
    return low(functools.reduce(jnp.add, [wide(ref[i]) for i in range(ref.shape[0])]))


def packed(sizes, lanes):
    places, row, lane = [], 0, 0
    for size in sizes:
        if lane + size > lanes:
            row, lane = row + 1, 0
        places.append((row, lane))
        lane += size
    return places


def finish_kernel(counts, sizes, places, lanes_ok, *refs):
    over_chips, over_rows, opened = sizes
    total_count = over_chips + over_rows + opened
    refs = list(refs)

    def take(number):
        found = refs[:number]
        del refs[:number]
        return found

    dqkv_ref, normed_in, inputs_ref, gain_ref, weight_in, part_ref = take(6)
    vectors_in = take(len(places) - 2)
    chips_in, rows_in, open_in = take(over_chips), take(over_rows), take(opened)
    grad_out, vectors_out, part_out, own_out = take(4)
    outs = take(total_count)
    tokens_ref, weight_ref, normed_ref, dqkv_here = take(4)
    vectors_ref, vector_slots, vector_sum = take(3)
    own_ref, own_slots, own_sum, own_block = take(4)
    row_slots, row_sum = take(over_rows + opened), take(over_rows + opened)
    chip_slots, chip_sum = take(total_count), take(total_count)
    load_sem, *sems = take(4)
    greet(("seq", "rows"), counts)
    number = 0

    def move(*part):
        nonlocal number
        found = Transfers(part, counts, *(sem.at[number] for sem in sems))
        number += 1
        return found

    count = counts["seq"]
    width = dqkv_ref.shape[1] // 3
    tokens = dqkv_ref.shape[0] // count
    if lanes_ok:
        home = [
            move(
                dqkv_ref,
                tokens_ref,
                "seq",
                rows_of(tokens, part * width, width),
                columns_of(width, part * width * count),
            )
            for part in range(3)
        ]
    else:
        home = [move(dqkv_ref, tokens_ref, "seq", rows_of(tokens), lead)]
    open_rows = [
        move(ref, slots, "rows", columns_of(slots.shape[2]), lead)
        for ref, slots in zip(open_in, row_slots[over_rows:])
    ]
    for item in open_rows:
        item.start()
    sources = [*chips_in, *rows_in, dqkv_ref, normed_in, weight_in]
    targets = [*chip_slots[:over_chips], *row_slots[:over_rows], dqkv_here, normed_ref, weight_ref]
    loads = [
        pltpu.make_async_copy(ref, there, load_sem.at[index])
        for index, (ref, there) in enumerate(zip(sources, targets))
    ]
    for load in loads:
        load.start()
    chip_moves, last = [], []

    def to_chips(index):
        total, slots = row_sum[index], chip_slots[over_chips + index]
        total[...] = add_slots(row_slots[index])
        chip_moves.append(move(total, slots, "chip", rows_of(slots.shape[1]), lead))
        chip_moves[-1].start()

    def to_rows(index):
        total = chip_sum[index]
        total[...] = add_slots(chip_slots[index])
        last.append(move(total, outs[index], "rows", whole, columns_of(total.shape[1])))
        last[-1].start()

    for index in range(over_rows):
        loads[over_chips + index].wait()
        to_chips(index)
    for item in home:
        item.start()
    for index in range(over_chips):
        loads[index].wait()
        to_rows(index)
    for load in loads[over_chips + over_rows :]:
        load.wait()
    own_grad = dot_left(dqkv_here[...], normed_ref[...]).T
    own_ref[...] = low(own_grad).reshape(own_ref.shape)
    own_rows = move(own_ref, own_slots, "rows", second_dim, lead)
    own_rows.start()
    for index, item in enumerate(open_rows):
        item.arrived()
        to_chips(over_rows + index)
    last.append(move(part_ref, part_out, "chip", whole, lead))
    last[-1].start()
    own_rows.arrived()
    own_sum[...] = add_slots(own_slots)
    if lanes_ok:
        own_chips = [
            move(
                own_sum.at[:, :, part * width : (part + 1) * width],
                own_block,
                "seq",
                lead,
                columns_of(width, part * width * count),
            )
            for part in range(3)
        ]
    else:
        own_chips = [move(own_sum, own_block, "seq", lead, lead)]
    for item in own_chips:
        item.start()
    for item in home:
        item.arrived()
    if lanes_ok:
        grad_tokens = tokens_ref[...]
    else:
        grad_tokens = jnp.concatenate(
            [
                tokens_ref[index, :, part * width : (part + 1) * width]
                for part in range(3)
                for index in range(count)
            ],
            axis=1,
        )
    normed_grad = dot_right(grad_tokens, weight_ref[...])
    values = wide(inputs_ref[...])
    center = values - jnp.mean(values, axis=-1, keepdims=True)
    scale = lax.rsqrt(jnp.mean(center * center, axis=-1, keepdims=True) + EPSILON)
    unit = center * scale
    gain_grad = jnp.sum(normed_grad * unit, axis=0, keepdims=True)
    shift_grad = jnp.sum(normed_grad, axis=0, keepdims=True)
    normed_grad = normed_grad * gain_ref[...]
    grad_out[...] = scale * (
        normed_grad
        - jnp.mean(normed_grad, axis=-1, keepdims=True)
        - unit * jnp.mean(normed_grad * unit, axis=-1, keepdims=True)
    )
    vectors_ref[...] = jnp.zeros_like(vectors_ref)
    for vector, (row, lane) in zip(
        [gain_grad, shift_grad] + [ref[...] for ref in vectors_in], places
    ):
        size = vector.shape[1] // count
        for index in range(count):
            vectors_ref[index, row : row + 1, lane : lane + size] = vector[
                :, index * size : (index + 1) * size
            ]
    vectors = move(vectors_ref, vector_slots, "seq", lead, lead)
    vectors.start()
    for index, item in enumerate(chip_moves):
        item.arrived()
        to_rows(over_chips + index)
    for item in own_chips:
        item.arrived()
    if lanes_ok:
        last.append(move(own_block, own_out, "rows", whole, rows_of(own_block.shape[0])))
    else:
        last.append(move(own_block, own_out, "rows", whole, lead))
    last[-1].start()
    vectors.arrived()
    vector_sum[...] = functools.reduce(jnp.add, [vector_slots[i] for i in range(count)])
    last.append(move(vector_sum, vectors_out, "rows", whole, lead))
    last[-1].start()
    for item in last:
        item.arrived()
    for item in home + open_rows + [own_rows, vectors] + chip_moves + own_chips + last:
        item.sent()


def finish(
    dqkv,
    normed,
    inputs,
    gain,
    weight,
    part,
    vectors,
    over_chips,
    over_rows,
    rows_open,
    counts,
    collective_id,
):
    count, chips, rows = counts["seq"], counts["chip"], counts["rows"]
    length, all_width = dqkv.shape
    features = inputs.shape[1]
    width = all_width // 3
    lanes_ok = width % 128 == 0
    tokens, short = length // count, features // count // rows
    bf, lanes = jnp.bfloat16, 512
    if lanes_ok:
        tokens_shape = (tokens, all_width * count)
        own_block, own_out = (short, all_width * count), (rows * short, all_width * count)
    else:
        tokens_shape = (count, tokens, all_width)
        own_block, own_out = (count, short, all_width), (rows, count, short, all_width)
    pieces = [features // count] * 2 + [vector.shape[1] // count for vector in vectors]
    places = packed(pieces, lanes)
    vector = (8, lanes)
    shares = [term.shape[1:] for term in over_rows]
    shares += [(term.shape[0], term.shape[1] // rows) for term in rows_open]
    blocks = [term.shape[1:] for term in over_chips]
    blocks += [(shape[0] // chips, shape[1]) for shape in shares]
    outs = [own_out] + [(shape[0], shape[1] * rows) for shape in blocks]
    own_share = (count, short, all_width)
    scratch = [(count, rows, short, all_width), (rows,) + own_share, own_share, own_block]
    scratch += [(rows,) + shape for shape in shares] + shares
    scratch += [(chips,) + shape for shape in blocks] + blocks
    moves = 3 + 3 + 2 + 3 + len(rows_open) + len(shares) + len(blocks)
    longest = max(count, rows)
    vmem, anywhere = pl.BlockSpec(memory_space=pltpu.VMEM), pl.BlockSpec(memory_space=pl.ANY)
    rest = [*over_chips, *over_rows, *rows_open]
    found = pl.pallas_call(
        functools.partial(
            finish_kernel,
            counts,
            (len(over_chips), len(over_rows), len(rows_open)),
            places,
            lanes_ok,
        ),
        out_shape=[
            jax.ShapeDtypeStruct(inputs.shape, jnp.float32),
            jax.ShapeDtypeStruct((rows,) + vector, jnp.float32),
            jax.ShapeDtypeStruct((chips,) + part.shape, bf),
        ]
        + [jax.ShapeDtypeStruct(shape, bf) for shape in outs],
        in_specs=[anywhere, anywhere, vmem, vmem, anywhere, anywhere]
        + [vmem] * len(vectors)
        + [anywhere] * len(rest),
        out_specs=[vmem] + [anywhere] * (2 + len(outs)),
        scratch_shapes=[
            pltpu.VMEM(tokens_shape, bf),
            pltpu.VMEM(weight.shape, bf),
            pltpu.VMEM(normed.shape, bf),
            pltpu.VMEM(dqkv.shape, bf),
            pltpu.VMEM((count,) + vector, jnp.float32),
            pltpu.VMEM((count,) + vector, jnp.float32),
            pltpu.VMEM(vector, jnp.float32),
        ]
        + [pltpu.VMEM(shape, bf) for shape in scratch]
        + [
            pltpu.SemaphoreType.DMA((len(over_chips) + len(over_rows) + 3,)),
            pltpu.SemaphoreType.DMA((moves,)),
            pltpu.SemaphoreType.DMA((moves, longest)),
            pltpu.SemaphoreType.DMA((moves, longest)),
        ],
        compiler_params=pltpu.CompilerParams(
            collective_id=collective_id, has_side_effects=True, vmem_limit_bytes=VMEM_LIMIT
        ),
    )(dqkv, normed, inputs, gain, weight, part, *vectors, *rest)
    return found[0], found[1], [(r, lane, size) for (r, lane), size in zip(places, pieces)], found[2:]


def widen_kernel(*refs):
    for given, out in zip(refs[: len(refs) // 2], refs[len(refs) // 2 :]):
        out[...] = wide(given[...])


def widen(arrays):
    vmem = pl.BlockSpec(memory_space=pltpu.VMEM)
    return pl.pallas_call(
        widen_kernel,
        out_shape=[jax.ShapeDtypeStruct(array.shape, jnp.float32) for array in arrays],
        in_specs=[vmem] * len(arrays),
        out_specs=[vmem] * len(arrays),
        compiler_params=pltpu.CompilerParams(vmem_limit_bytes=VMEM_LIMIT),
    )(*arrays)


def head_lanes(width):
    return lax.broadcasted_iota(jnp.int32, (1, width), 1) // DEPTH


def pick_head(values, head, width):
    if width == DEPTH:
        return values
    return jnp.where(head_lanes(width) == head, values, jnp.zeros_like(values))


def begin_of(start_ref, position):
    begin = jnp.zeros_like(position)
    for page in range(1, PAGES):
        begin = jnp.where(position >= start_ref[page], start_ref[page], begin)
    return begin


def as_row(column):
    return jnp.broadcast_to(column, (column.shape[0], 8)).T[:1]


def self_forward_kernel(qkv_ref, start_ref, out_ref, stat_ref):
    length, width = out_ref.shape
    heads = width // DEPTH
    blocks = length // BLOCK
    for index in range(blocks):
        rows = pl.ds(index * BLOCK, BLOCK)
        keys_end = (index + 1) * BLOCK
        query = qkv_ref[rows, 0:width]
        position = index * BLOCK + lax.broadcasted_iota(jnp.int32, (BLOCK, 1), 0)
        begin = begin_of(start_ref, position)
        if index == blocks - 1 or index <= 1:
            cuts = [(0, keys_end)]
        else:
            cuts = [(0, BLOCK), (BLOCK, index * BLOCK), (index * BLOCK, keys_end)]
        outs, stats = [], []
        for head in range(heads):
            query_head = pick_head(query, head, width) * jnp.bfloat16(SCALE)
            scores = []
            for low_end, high_end in cuts:
                part = dot_right(query_head, qkv_ref[low_end:high_end, width : 2 * width])
                if low_end == 0 or high_end == keys_end:
                    column = low_end + lax.broadcasted_iota(jnp.int32, part.shape, 1)
                    allowed = column >= begin
                    if high_end == keys_end:
                        allowed = allowed & (column <= position)
                    part = jnp.where(allowed, part, NEGATIVE)
                scores.append(part)
            top = functools.reduce(
                jnp.maximum, [jnp.max(part, axis=-1, keepdims=True) for part in scores]
            )
            total, mixed = 0.0, 0.0
            for (low_end, high_end), part in zip(cuts, scores):
                weight = jnp.exp(part - top)
                total = total + jnp.sum(weight, axis=-1, keepdims=True)
                mixed = mixed + dot_plain(
                    low(weight), qkv_ref[low_end:high_end, 2 * width : 3 * width]
                )
            outs.append(mixed / total)
            stats.append(top + jnp.log(total))
        merged = outs[0]
        for head in range(1, heads):
            merged = jnp.where(head_lanes(width) == head, outs[head], merged)
        out_ref[rows, :] = low(merged)
        for head in range(heads):
            stat_ref[head : head + 1, rows] = as_row(stats[head])


def self_forward(qkv, starts):
    length, width = qkv.shape[0], qkv.shape[1] // 3
    heads = width // DEPTH
    return pl.pallas_call(
        self_forward_kernel,
        out_shape=(
            jax.ShapeDtypeStruct((length, width), jnp.bfloat16),
            jax.ShapeDtypeStruct((heads, length), jnp.float32),
        ),
        in_specs=[
            pl.BlockSpec(memory_space=pltpu.VMEM),
            pl.BlockSpec(memory_space=pltpu.SMEM),
        ],
        out_specs=[pl.BlockSpec(memory_space=pltpu.VMEM)] * 2,
        compiler_params=pltpu.CompilerParams(vmem_limit_bytes=VMEM_LIMIT),
    )(qkv, starts)


def self_backward_kernel(counts, hosted, *refs):
    size = len(hosted)
    qkv_ref, out_ref, blocks_ref, slots_ref, start_ref, stat_ref = refs[:6]
    sent, dqkv_ref, stacks = refs[6 : 6 + size], refs[6 + size], refs[7 + size : 7 + 2 * size]
    dk_ref, dv_ref, grad_ref, own_sem, send_sem, recv_sem = refs[7 + 2 * size :]
    length, width = out_ref.shape
    heads = width // DEPTH
    blocks = length // BLOCK
    greet(("seq", "rows"), counts)
    moves = []
    for index, ((axis, how), ref, stack) in enumerate(zip(hosted, sent, stacks)):
        source = rows_of(stack.shape[1]) if how == "rows" else columns_of(stack.shape[2])
        part = (ref, stack, axis, source, lead)
        moves.append(
            Transfers(part, counts, own_sem.at[index], send_sem.at[index], recv_sem.at[index])
        )
        moves[-1].start()
    dk_ref[...] = jnp.zeros_like(dk_ref)
    dv_ref[...] = jnp.zeros_like(dv_ref)
    grad_ref[...] = blocks_ref[...]
    slots = add_slots(slots_ref)
    in_front = lax.broadcasted_iota(jnp.int32, slots.shape, 0) < start_ref[PAGES]
    nothing = jnp.zeros_like(slots)
    grad_ref[0:SLOTS, :] += jnp.where(in_front, slots, nothing)
    grad_ref[length - SLOTS : length, :] += jnp.where(in_front, nothing, slots)

    def query_block(index, carry):
        rows = pl.ds(pl.multiple_of(index * BLOCK, BLOCK), BLOCK)
        query = qkv_ref[rows, 0:width]
        grad = grad_ref[rows, :]
        product = (wide(grad) * wide(out_ref[rows, :])).T
        position = index * BLOCK + lax.broadcasted_iota(jnp.int32, (1, BLOCK), 1)
        begin = begin_of(start_ref, position)
        query_heads = [pick_head(query, head, width) * jnp.bfloat16(SCALE) for head in range(heads)]
        grad_heads = [pick_head(grad, head, width) for head in range(heads)]
        stats = [stat_ref[head : head + 1, rows] for head in range(heads)]
        deltas = [
            jnp.sum(product[head * DEPTH : (head + 1) * DEPTH, :], axis=0, keepdims=True)
            for head in range(heads)
        ]

        def key_block(key_index, sums):
            keys = pl.ds(pl.multiple_of(key_index * BLOCK, BLOCK), BLOCK)
            key = qkv_ref[keys, width : 2 * width]
            value = qkv_ref[keys, 2 * width : 3 * width]
            row = key_index * BLOCK + lax.broadcasted_iota(jnp.int32, (BLOCK, 1), 0)
            allowed = (row >= begin) & (row <= position)
            dk_part, dv_part, found = 0.0, 0.0, []
            for head in range(heads):
                scores = jnp.where(allowed, dot_right(key, query_heads[head]), NEGATIVE)
                prob = jnp.exp(scores - stats[head])
                dv_part = dv_part + dot_plain(low(prob), grad_heads[head])
                grad_prob = dot_right(value, grad_heads[head])
                grad_score = low(prob * (grad_prob - deltas[head]))
                dk_part = dk_part + dot_plain(grad_score, query_heads[head])
                found.append(sums[head] + dot_left(grad_score, key))
            dk_ref[keys, :] += dk_part
            dv_ref[keys, :] += dv_part
            return tuple(found)

        zero = tuple(jnp.zeros((BLOCK, width), jnp.float32) for _ in range(heads))
        sums = lax.fori_loop(0, index + 1, key_block, zero)
        merged = sums[0]
        for head in range(1, heads):
            merged = jnp.where(head_lanes(width) == head, sums[head], merged)
        dqkv_ref[rows, 0:width] = low(merged * SCALE)
        return carry

    lax.fori_loop(0, blocks, query_block, 0)
    dqkv_ref[:, width : 2 * width] = low(dk_ref[...])
    dqkv_ref[:, 2 * width : 3 * width] = low(dv_ref[...])
    for item in moves:
        item.arrived()
    for item in moves:
        item.sent()


def self_backward(
    qkv, out, grad, slots, starts, stats, sent, hosted, counts, collective_id
):
    length, width = out.shape
    stacks = []
    for array, (axis, how) in zip(sent, hosted):
        rows, columns = array.shape
        total = counts[axis]
        block = (rows // total, columns) if how == "rows" else (rows, columns // total)
        stacks.append(jax.ShapeDtypeStruct((total,) + block, array.dtype))
    longest = max(counts["seq"], counts["rows"])
    vmem, anywhere = pl.BlockSpec(memory_space=pltpu.VMEM), pl.BlockSpec(memory_space=pl.ANY)
    return pl.pallas_call(
        functools.partial(self_backward_kernel, counts, hosted),
        out_shape=[jax.ShapeDtypeStruct((length, 3 * width), jnp.bfloat16), *stacks],
        in_specs=[vmem] * 4
        + [pl.BlockSpec(memory_space=pltpu.SMEM), vmem]
        + [anywhere] * len(sent),
        out_specs=[vmem] + [anywhere] * len(sent),
        scratch_shapes=[pltpu.VMEM((length, width), jnp.float32)] * 2
        + [
            pltpu.VMEM((length, width), jnp.bfloat16),
            pltpu.SemaphoreType.DMA((len(sent),)),
            pltpu.SemaphoreType.DMA((len(sent), longest)),
            pltpu.SemaphoreType.DMA((len(sent), longest)),
        ],
        compiler_params=pltpu.CompilerParams(
            collective_id=collective_id, has_side_effects=True, vmem_limit_bytes=VMEM_LIMIT
        ),
    )(qkv, out, grad, slots, starts, stats, *sent)


def cross_forward_kernel(query_ref, key_ref, value_ref, own_key_ref, own_value_ref, out_ref, stat_ref):
    tokens = query_ref.shape[0] - SLOTS
    width = query_ref.shape[1]
    for begin, size, keys, values in (
        (0, tokens, key_ref, value_ref),
        (tokens, SLOTS, own_key_ref, own_value_ref),
    ):
        query = query_ref[begin : begin + size, :]
        outs = []
        for head in range(width // DEPTH):
            query_head = pick_head(query, head, width) * jnp.bfloat16(SCALE)
            scores = dot_right(query_head, keys[...])
            column = lax.broadcasted_iota(jnp.int32, scores.shape, 1)
            scores = jnp.where(column < PAGE_TOK, scores, NEGATIVE)
            top = jnp.max(scores, axis=-1, keepdims=True)
            weight = jnp.exp(scores - top)
            total = jnp.sum(weight, axis=-1, keepdims=True)
            outs.append(dot_plain(low(weight), values[...]) / total)
            stat_ref[0, head : head + 1, begin : begin + size] = as_row(top + jnp.log(total))
        merged = outs[0]
        for head in range(1, len(outs)):
            merged = jnp.where(head_lanes(width) == head, outs[head], merged)
        out_ref[begin : begin + size, :] = low(merged)


def cross_forward(query, kv_big, kv_own):
    rows, features = query.shape
    pair = 2 * DEPTH
    steps = features // pair
    tall = pl.BlockSpec((rows, pair), lambda i: (0, i))
    keys = pl.BlockSpec((PAGE_PAD, pair), lambda i: (0, i))
    values = pl.BlockSpec((PAGE_PAD, pair), lambda i: (0, i + steps))
    return pl.pallas_call(
        cross_forward_kernel,
        grid=(steps,),
        out_shape=(
            jax.ShapeDtypeStruct((rows, features), jnp.bfloat16),
            jax.ShapeDtypeStruct((steps, 2, rows), jnp.float32),
        ),
        in_specs=[tall, keys, values, keys, values],
        out_specs=[tall, pl.BlockSpec((1, 2, rows), lambda i: (i, 0, 0))],
        compiler_params=pltpu.CompilerParams(vmem_limit_bytes=VMEM_LIMIT),
    )(query, kv_big, kv_big, kv_own, kv_own)


def cross_backward_kernel(
    counts,
    query_ref,
    key_ref,
    value_ref,
    own_key_ref,
    own_value_ref,
    out_ref,
    grad_ref,
    stat_ref,
    sent_ref,
    dq_ref,
    dk_ref,
    dv_ref,
    own_dk_ref,
    own_dv_ref,
    stack_ref,
    own_sem,
    send_sem,
    recv_sem,
):
    step, steps = pl.program_id(0), pl.num_programs(0)

    def move():
        part = (sent_ref, stack_ref, "chip", rows_of(stack_ref.shape[1]), lead)
        return Transfers(part, counts, own_sem, send_sem, recv_sem)

    @pl.when(step == 0)
    def _():
        greet(("chip",), counts)
        move().start()

    tokens = query_ref.shape[0] - SLOTS
    width = query_ref.shape[1]
    row = lax.broadcasted_iota(jnp.int32, (PAGE_PAD, 1), 0)
    for begin, size, keys, values, dk_out, dv_out in (
        (0, tokens, key_ref, value_ref, dk_ref, dv_ref),
        (tokens, SLOTS, own_key_ref, own_value_ref, own_dk_ref, own_dv_ref),
    ):
        rows = slice(begin, begin + size)
        query, grad = query_ref[rows, :], grad_ref[rows, :]
        product = (wide(grad) * wide(out_ref[rows, :])).T
        dk_sum, dv_sum, found = 0.0, 0.0, []
        for head in range(width // DEPTH):
            query_head = pick_head(query, head, width) * jnp.bfloat16(SCALE)
            grad_head = pick_head(grad, head, width)
            delta = jnp.sum(product[head * DEPTH : (head + 1) * DEPTH, :], axis=0, keepdims=True)
            scores = dot_right(keys[...], query_head)
            scores = jnp.where(row < PAGE_TOK, scores, NEGATIVE)
            prob = jnp.exp(scores - stat_ref[0, head : head + 1, rows])
            dv_sum = dv_sum + dot_plain(low(prob), grad_head)
            grad_prob = dot_right(values[...], grad_head)
            grad_score = low(prob * (grad_prob - delta))
            dk_sum = dk_sum + dot_plain(grad_score, query_head)
            found.append(dot_left(grad_score, keys[...]))
        merged = found[0]
        for head in range(1, len(found)):
            merged = jnp.where(head_lanes(width) == head, found[head], merged)
        dq_ref[rows, :] = low(merged * SCALE)
        dk_out[...] = low(dk_sum)
        dv_out[...] = low(dv_sum)

    @pl.when(step == steps - 1)
    def _():
        found = move()
        found.arrived()
        found.sent()


def cross_backward(query, kv_big, kv_own, out, grad, stats, sent, counts, collective_id):
    rows, features = query.shape
    pair = 2 * DEPTH
    steps = features // pair
    tall = pl.BlockSpec((rows, pair), lambda i: (0, i))
    keys = pl.BlockSpec((PAGE_PAD, pair), lambda i: (0, i))
    values = pl.BlockSpec((PAGE_PAD, pair), lambda i: (0, i + steps))
    page = jax.ShapeDtypeStruct((PAGE_PAD, features), jnp.bfloat16)
    chips = counts["chip"]
    stack = jax.ShapeDtypeStruct(
        (chips, sent.shape[0] // chips, sent.shape[1]), jnp.bfloat16
    )
    anywhere = pl.BlockSpec(memory_space=pl.ANY)
    return pl.pallas_call(
        functools.partial(cross_backward_kernel, counts),
        grid=(steps,),
        out_shape=(
            jax.ShapeDtypeStruct((rows, features), jnp.bfloat16),
            page,
            page,
            page,
            page,
            stack,
        ),
        in_specs=[
            tall,
            keys,
            values,
            keys,
            values,
            tall,
            tall,
            pl.BlockSpec((1, 2, rows), lambda i: (i, 0, 0)),
            anywhere,
        ],
        out_specs=[tall, keys, keys, keys, keys, anywhere],
        scratch_shapes=[
            pltpu.SemaphoreType.DMA,
            pltpu.SemaphoreType.DMA((chips,)),
            pltpu.SemaphoreType.DMA((chips,)),
        ],
        compiler_params=pltpu.CompilerParams(
            collective_id=collective_id, has_side_effects=True, vmem_limit_bytes=VMEM_LIMIT
        ),
    )(query, kv_big, kv_big, kv_own, kv_own, out, grad, stats, sent)


def body(
    inputs,
    memory,
    out_grad,
    segment_ids,
    page_order,
    norm1_gain,
    norm1_bias,
    qkv_weight,
    qv_bias,
    self_out_weight,
    self_out_bias,
    norm2_gain,
    norm2_bias,
    cross_q_weight,
    cross_q_bias,
    cross_kv_weight,
    cross_v_bias,
    cross_out_weight,
    cross_out_bias,
    norm3_gain,
    norm3_bias,
    fc1_weight,
    fc1_bias,
    fc2_weight,
    fc2_bias,
):
    tokens, features = inputs.shape[1:]
    count = lax.axis_size("seq")
    me = lax.axis_index("seq")
    length = tokens * count
    width = features // count
    rows_count = lax.axis_size("rows")
    counts = {"seq": count, "chip": count // 2, "rows": rows_count}
    core = me % 2

    def blocks_of(first, which):
        size = first.shape[1] // count
        return jnp.concatenate(
            [
                lax.dynamic_slice_in_dim(first, (2 * chip + which) * size, size, 1)
                for chip in range(count // 2)
            ],
            axis=1,
        )

    def pair_sum(first, second, behind=None):
        given = swap(low(dot_left(blocks_of(first, 1 - core), second)))
        if behind is not None:
            given = after(given, behind)
        return low(dot_left(blocks_of(first, core), second) + wide(given))

    def swap(value):
        return lax.ppermute(value, "seq", [(i, i ^ 1) for i in range(count)])

    def after(value, other):
        return lax.optimization_barrier((value, other))[0]

    mem_rows = memory.shape[1]
    sharers = PAGE_TOK // mem_rows
    row_segs = segment_ids[0]
    row_pages = page_order[0]
    gain_one, shift_one = wide(norm1_gain), wide(norm1_bias)
    gain_two, shift_two = wide(norm2_gain), wide(norm2_bias)
    gain_three, shift_three = wide(norm3_gain), wide(norm3_bias)

    starts = jnp.sum(row_segs[None, :] < jnp.arange(PAGES)[:, None], axis=1, dtype=jnp.int32)
    big_page = row_segs[length // 2]
    big_start = jnp.sum(row_segs < big_page, dtype=jnp.int32)
    own_page = lax.dynamic_index_in_dim(row_pages, me // sharers, 0, keepdims=False)
    slot = jnp.arange(SLOTS)
    in_front = (slot < big_start)[:, None]
    slot_segs = jnp.where(slot < big_start, row_segs[:SLOTS], row_segs[length - SLOTS :])
    slot_mine = (slot_segs == own_page) & (slot * sharers // SLOTS == me % sharers)
    home_segs = lax.dynamic_slice_in_dim(row_segs, me * tokens, tokens, 0)
    active = jnp.concatenate((home_segs == big_page, slot_mine))[:, None]
    is_first, is_last = me == 0, me == count - 1

    def slots_of(front, back):
        return jnp.where(in_front, front, back)

    mem_own = memory[0]
    mem_page = mem_own
    if sharers > 1:
        groups = [[g * sharers + s for s in range(sharers)] for g in range(count // sharers)]
        mem_page = lax.all_gather(mem_own, "seq", axis=0, tiled=True, axis_index_groups=groups)
    mem_page = jnp.pad(mem_page, ((0, PAGE_PAD - PAGE_TOK), (0, 0)))
    gives_big = (own_page == big_page) & (me % sharers == 0)

    x_own = inputs[0]
    x_all = gather_rows(x_own, count, 0)

    half = PAGE_PAD // 2
    masked_page = jnp.where(gives_big, mem_page, jnp.zeros_like(mem_page)).reshape(2, half, -1)
    pair_page = masked_page[core] + swap(masked_page[1 - core])
    at_end = jnp.where(core == 0, is_first, is_last)
    end_grad = jnp.where(core == 0, out_grad[0, :SLOTS], out_grad[0, tokens - SLOTS :])
    sent = jnp.concatenate((pair_page, jnp.where(at_end, end_grad, jnp.zeros_like(end_grad))))
    same_core = [[2 * chip + which for chip in range(count // 2)] for which in range(2)]
    mine = lax.psum(sent, "seq", axis_index_groups=same_core)
    theirs = swap(mine)
    zeroth, first = jnp.where(core == 0, mine, theirs), jnp.where(core == 0, theirs, mine)
    mem_big = jnp.concatenate((zeroth[:half], first[:half]))
    front_grad, back_grad = zeroth[half:], first[half:]

    qkv_own_weight = jnp.concatenate(
        [
            lax.dynamic_slice_in_dim(qkv_weight, part * features + me * width, width, 1)
            for part in range(3)
        ],
        axis=1,
    )
    qkv_own_bias = jnp.concatenate(
        (
            lax.dynamic_slice_in_dim(qv_bias, me * width, width, 0),
            jnp.zeros((width,), jnp.bfloat16),
            lax.dynamic_slice_in_dim(qv_bias, features + me * width, width, 0),
        )
    )
    normed_all = low(norm_forward(wide(x_all), gain_one, shift_one))
    qkv = low(dot_plain(normed_all, qkv_own_weight) + wide(qkv_own_bias))
    mixed, mixed_stats = self_forward(qkv, starts)
    bf = jnp.bfloat16
    lanes_ok = width % 128 == 0
    chosen = slots_of(mixed[:SLOTS], mixed[length - SLOTS :])
    if lanes_ok:
        blocks_mixed, slots_mixed = exchange(
            (mixed, chosen),
            (
                jax.ShapeDtypeStruct((tokens, features), bf),
                jax.ShapeDtypeStruct((SLOTS, features), bf),
            ),
            (
                (1, 1, "seq", whole, columns_of(width)),
                (0, 0, "seq", rows_of(tokens), columns_of(width)),
            ),
            counts,
            1,
        )
    else:
        blocks_mixed, slots_mixed = exchange(
            (mixed, chosen),
            (
                jax.ShapeDtypeStruct((count, tokens, width), bf),
                jax.ShapeDtypeStruct((count, SLOTS, width), bf),
            ),
            ((1, 1, "seq", whole, lead), (0, 0, "seq", rows_of(tokens), lead)),
            counts,
            1,
        )
        blocks_mixed, slots_mixed = (
            blocks.transpose(1, 0, 2).reshape(blocks.shape[1], -1)
            for blocks in (blocks_mixed, slots_mixed)
        )
    attended = jnp.concatenate((blocks_mixed, slots_mixed))
    resid = wide(
        jnp.concatenate((x_own, slots_of(x_all[:SLOTS], x_all[length - SLOTS :])))
    )
    resid_one = resid + dot_plain(attended, self_out_weight) + wide(self_out_bias)
    normed_two = low(norm_forward(resid_one, gain_two, shift_two))
    cross_queries = low(dot_plain(normed_two, cross_q_weight) + wide(cross_q_bias))
    kv_shift = jnp.concatenate((jnp.zeros((features,), jnp.float32), wide(cross_v_bias)))
    kv_big = low(dot_plain(mem_big, cross_kv_weight) + kv_shift)
    kv_own = low(dot_plain(mem_page, cross_kv_weight) + kv_shift)
    cross_low, cross_stats = cross_forward(cross_queries, kv_big, kv_own)
    resid_two = resid_one + dot_plain(cross_low, cross_out_weight) + wide(cross_out_bias)
    normed_three = low(norm_forward(resid_two, gain_three, shift_three))
    pre_act = dot_plain(normed_three, fc1_weight) + wide(fc1_bias)
    hidden_act = low(gelu_exact(pre_act))
    final = low(resid_two + dot_plain(hidden_act, fc2_weight) + wide(fc2_bias))

    grad_out = jnp.concatenate((out_grad[0], slots_of(front_grad, back_grad)))
    grad_out = jnp.where(active, grad_out, jnp.zeros_like(grad_out))
    grad_act = dot_right(grad_out, fc2_weight)
    _, gelu_pull = jax.vjp(gelu_exact, pre_act)
    grad_pre = low(gelu_pull(grad_act)[0])
    grad_fc2_b = jnp.sum(wide(grad_out), axis=0)
    grad_fc2_w = pair_sum(hidden_act, grad_out, grad_pre)
    fc2_share = lax.psum_scatter(grad_fc2_w, "rows", scatter_dimension=1, tiled=True)
    grad_normed_three = dot_right(grad_pre, fc1_weight)
    grad_fc1_w = pair_sum(normed_three, grad_pre, grad_normed_three)
    fc1_share = lax.psum_scatter(grad_fc1_w, "rows", scatter_dimension=1, tiled=True)
    grad_fc1_b = jnp.sum(wide(grad_pre), axis=0)
    grad_two_norm, grad_gain_three, grad_shift_three = norm_backward(
        resid_two, gain_three, shift_three, grad_normed_three
    )
    grad_resid_two = wide(grad_out) + grad_two_norm
    grad_branch_two = low(grad_resid_two)
    grad_co_w = pair_sum(cross_low, grad_branch_two)
    grad_co_b = jnp.sum(wide(grad_branch_two), axis=0)
    grad_cross_low = low(dot_right(grad_branch_two, cross_out_weight))
    grad_cross_low = after(grad_cross_low, (grad_fc1_w, grad_fc2_w))
    grad_cross_q, big_dk, big_dv, own_dk, own_dv, fc2_stack = cross_backward(
        cross_queries, kv_big, kv_own, cross_low, grad_cross_low, cross_stats, fc2_share, counts, 5
    )
    grad_cq_w = pair_sum(normed_two, grad_cross_q)
    grad_cq_b = jnp.sum(wide(grad_cross_q), axis=0)
    grad_one_norm, grad_gain_two, grad_shift_two = norm_backward(
        resid_one, gain_two, shift_two, dot_right(grad_cross_q, cross_q_weight)
    )
    grad_resid_one = grad_resid_two + grad_one_norm
    grad_branch_one = low(grad_resid_one)
    grad_o_w = pair_sum(attended, grad_branch_one)
    grad_o_b = jnp.sum(wide(grad_branch_one), axis=0)
    grad_attended = low(dot_right(grad_branch_one, self_out_weight))
    if lanes_ok:
        given, home_part, slot_part = (grad_attended,), (0, 0), (0, 1)

        def piece(first, size):
            def find(ref, index):
                return ref.at[
                    first : first + size, pl.ds(pl.multiple_of(index * width, width), width)
                ]

            return find

        pieces = piece(0, tokens), piece(tokens, SLOTS)
    else:
        by_device = grad_attended.reshape(-1, count, width).transpose(1, 0, 2)
        given, home_part, slot_part = (by_device[:, :tokens], by_device[:, tokens:]), (0, 0), (1, 1)
        pieces = lead, lead
    grad_mixed, slots_grad = exchange(
        given,
        (
            jax.ShapeDtypeStruct((length, width), bf),
            jax.ShapeDtypeStruct((count, SLOTS, width), bf),
        ),
        (
            home_part + ("seq", pieces[0], rows_of(tokens)),
            slot_part + ("seq", pieces[1], lead),
        ),
        counts,
        2,
    )
    dqkv, *stacks = self_backward(
        qkv,
        mixed,
        grad_mixed,
        slots_grad,
        jnp.concatenate((starts, big_start[None])),
        mixed_stats,
        (fc1_share, grad_co_w, grad_cq_w, grad_o_w),
        (("chip", "rows"),) + (("rows", "columns"),) * 3,
        counts,
        3,
    )

    slot_final = jnp.where(active[tokens:], final[tokens:], jnp.zeros_like(final[tokens:]))
    part_rows = PAGE_PAD // (count // 2)
    own_half = jnp.where(core == 0, big_dk, big_dv)
    own_half = own_half + swap(jnp.where(core == 0, big_dv, big_dk))
    part = lax.psum_scatter(
        after(own_half, (fc1_share, grad_mixed)), "seq", scatter_dimension=0, tiled=True, axis_index_groups=same_core
    )
    slot_half = jnp.where(core == 0, slot_final, low(grad_resid_one[tokens:]))
    slot_half = slot_half + swap(jnp.where(core == 0, low(grad_resid_one[tokens:]), slot_final))
    slot_half = lax.psum(after(slot_half, part), "seq", axis_index_groups=same_core)
    grad_ckv = jnp.concatenate((own_dk[:PAGE_TOK], own_dv[:PAGE_TOK]), axis=1)
    if sharers > 1:
        grad_ckv = lax.psum_scatter(
            grad_ckv, "seq", scatter_dimension=0, tiled=True, axis_index_groups=groups
        )
    part = after(part, dqkv)
    nothing = jnp.zeros_like(part)
    part_wide = jnp.concatenate(
        (jnp.where(core == 0, part, nothing), jnp.where(core == 0, nothing, part)), axis=1
    )
    part_memory = lax.dynamic_slice_in_dim(mem_big, me // 2 * part_rows, part_rows, 0)

    def ckv_terms(which):
        return dot_left(blocks_of(mem_own, which), grad_ckv) + dot_left(
            blocks_of(part_memory, which), part_wide
        )

    grad_ckv_w = low(ckv_terms(core) + wide(swap(low(ckv_terms(1 - core)))))
    grad_cv_b = jnp.sum(wide(grad_ckv[:, features:]), axis=0) + jnp.sum(
        wide(part_wide[:, features:]), axis=0
    )
    half_weight = lax.dynamic_slice_in_dim(cross_kv_weight, core * features, features, 1)
    part_grad = dot_right(part, half_weight)
    part_grad = part_grad.reshape(2, part_rows // 2, features)
    part_grad = low(part_grad[core] + swap(part_grad[1 - core]))
    memory_grad = dot_right(grad_ckv, cross_kv_weight)

    def at_home(own, returned):
        front = is_first & in_front
        back = is_last & ~in_front
        head = jnp.where(front, returned.astype(own.dtype), own[:SLOTS])
        tail = jnp.where(back, returned.astype(own.dtype), own[tokens - SLOTS :])
        return jnp.concatenate((head, own[SLOTS : tokens - SLOTS], tail))


    column_sums = jnp.sum(wide(dqkv), axis=0)

    def in_features(part):
        return lax.dynamic_update_slice_in_dim(
            jnp.zeros((features,), jnp.float32),
            column_sums[part * width : (part + 1) * width],
            me * width,
            0,
        )

    grad_qv_b = jnp.concatenate((in_features(0), in_features(2)))

    vectors = (
        grad_qv_b,
        grad_o_b,
        grad_gain_two,
        grad_shift_two,
        grad_cq_b,
        grad_cv_b,
        grad_co_b,
        grad_gain_three,
        grad_shift_three,
        grad_fc1_b,
        grad_fc2_b,
    )
    grad_in_norm, joined, places, sums = finish(
        dqkv,
        normed_all,
        x_own,
        gain_one[None, :],
        qkv_weight,
        part_grad,
        [vector[None, :] for vector in vectors],
        (fc2_stack, stacks[0]),
        stacks[1:],
        (grad_ckv_w,),
        counts,
        4,
    )
    big_grad, qkv_w, fc2_w, fc1_w, co_w, cq_w, o_w, ckv_w = sums
    if not lanes_ok:
        qkv_w = qkv_w.reshape(rows_count, count, -1, 3, width).transpose(0, 2, 3, 1, 4)
        qkv_w = qkv_w.reshape(-1, 3 * features)
    qkv_w, fc1_w, fc2_w, o_w, cq_w, co_w, ckv_w = widen(
        (qkv_w, fc1_w, fc2_w, o_w, cq_w, co_w, ckv_w)
    )
    joined = jnp.sum(joined, axis=0)
    slot_half = after(slot_half, joined)
    theirs = swap(slot_half)
    slot_final, slot_grad = (
        jnp.where(core == 0, slot_half, theirs),
        jnp.where(core == 0, theirs, slot_half),
    )
    layer_out = at_home(final[:tokens], slot_final)[None]
    input_grad = (at_home(grad_resid_one[:tokens], slot_grad) + grad_in_norm)[None]
    big_other = swap(big_grad)
    big_grad = jnp.stack(
        (jnp.where(core == 0, big_grad, big_other), jnp.where(core == 0, big_other, big_grad)), axis=1
    ).reshape(PAGE_PAD, features)
    big_grad = lax.dynamic_slice_in_dim(big_grad, me % sharers * mem_rows, mem_rows, 0)
    memory_grad = jnp.where(own_page == big_page, memory_grad + wide(big_grad), memory_grad)[None]
    pieces = [joined[row, lane : lane + size] for row, lane, size in places]
    g1, s1, qvb, ob, g2, s2, cqb, cvb, cob, g3, s3, f1b, f2b = pieces
    return (
        layer_out,
        input_grad,
        memory_grad,
        g1,
        s1,
        qkv_w,
        qvb,
        o_w,
        ob,
        g2,
        s2,
        cq_w,
        cqb,
        ckv_w,
        cvb,
        co_w,
        cob,
        g3,
        s3,
        fc1_w,
        f1b,
        fc2_w,
        f2b,
    )


def solution(mesh):
    split = P("rows", "seq", None)
    in_specs = (split, split, split, P("rows", None), P("rows", None)) + (P(),) * 20
    vector, matrix = P("seq"), P("seq", None)
    out_specs = (split, split, split) + (
        vector,
        vector,
        matrix,
        vector,
        matrix,
        vector,
        vector,
        vector,
        matrix,
        vector,
        matrix,
        vector,
        matrix,
        vector,
        vector,
        vector,
        matrix,
        vector,
        matrix,
        vector,
    )
    return jax.shard_map(body, mesh=mesh, in_specs=in_specs, out_specs=out_specs, check_vma=False)
```

```python
import functools

import jax
import jax.numpy as jnp
from jax import lax
from jax.experimental import pallas as pl
from jax.experimental.pallas import tpu as pltpu
from jax.sharding import PartitionSpec as P

HEADS = 16
DEPTH = 64
PAGES = 8
PAGE_TOK = 588
PAGE_PAD = 640
SLOTS = 128
BLOCK = 256


NEGATIVE = -1e30
SCALE = 0.125
EPSILON = 1e-05
MESH = pl.DeviceIdType.MESH
VMEM_LIMIT = 56 * 1024 * 1024


def norm_forward(values, gain, shift):
    center = values - jnp.mean(values, axis=-1, keepdims=True)
    spread = jnp.mean(center * center, axis=-1, keepdims=True)
    return center * lax.rsqrt(spread + EPSILON) * gain + shift


def gelu_exact(values):
    return jax.nn.gelu(values, approximate=False)


def norm_backward(values, gain, shift, grad_normed):
    _, pullback = jax.vjp(norm_forward, values, gain, shift)
    return pullback(grad_normed)


def dot_plain(first, second):
    return jnp.dot(first, second, preferred_element_type=jnp.float32)


def dot_left(first, second):
    return lax.dot_general(
        first, second, (((0,), (0,)), ((), ())), preferred_element_type=jnp.float32
    )


def dot_right(first, second):
    return lax.dot_general(
        first, second, (((1,), (1,)), ((), ())), preferred_element_type=jnp.float32
    )


def low(values):
    return values.astype(jnp.bfloat16)


def wide(values):
    return values.astype(jnp.float32)


def place(index):
    return (lax.axis_index("rows"), index)


def gather_kernel(
    count,
    lanes_ok,
    block_ref,
    gain_ref,
    shift_ref,
    weight_in,
    bias_ref,
    page_in,
    kv_in,
    kv_shift_ref,
    normed_ref,
    qkv_ref,
    ends_ref,
    kv_ref,
    whole_ref,
    weight_ref,
    page_ref,
    kv_weight_ref,
    load_sem,
    own_sem,
    send_sem,
    recv_sem,
):
    rows, features = block_ref.shape
    width = qkv_ref.shape[1] // 3
    me = lax.axis_index("seq")
    chip, core, chips = me // 2, me % 2, count // 2
    other = me + 1 - 2 * core
    barrier = pltpu.get_barrier_semaphore()

    def block(index):
        return whole_ref.at[pl.ds(index * rows, rows)]

    pl.semaphore_signal(barrier, inc=1, device_id=place(other), device_id_type=MESH)

    @pl.when(chip > 0)
    def _():
        pl.semaphore_signal(barrier, inc=1, device_id=place(me - 2), device_id_type=MESH)

    @pl.when(chip < chips - 1)
    def _():
        pl.semaphore_signal(barrier, inc=1, device_id=place(me + 2), device_id_type=MESH)

    if lanes_ok:
        loads = [
            pltpu.make_async_copy(
                weight_in.at[
                    :, pl.ds(pl.multiple_of(part * features + me * width, width), width)
                ],
                weight_ref.at[:, part * width : (part + 1) * width],
                load_sem.at[part],
            )
            for part in range(3)
        ]
        bias_query = bias_ref[:, pl.ds(pl.multiple_of(me * width, width), width)]
        bias_value = bias_ref[:, pl.ds(pl.multiple_of(features + me * width, width), width)]
    else:
        loads = [pltpu.make_async_copy(weight_in, weight_ref, load_sem.at[0])]
        bias_query = bias_ref[:, 0:width]
        bias_value = bias_ref[:, width : 2 * width]
    later_loads = [
        pltpu.make_async_copy(page_in, page_ref, load_sem.at[3]),
        pltpu.make_async_copy(kv_in, kv_weight_ref, load_sem.at[4]),
    ]
    own = pltpu.make_async_copy(block_ref, block(me), own_sem)
    for load in [own] + loads + later_loads:
        load.start()
    peers = 1 + jnp.where(chip > 0, 1, 0) + jnp.where(chip < chips - 1, 1, 0)
    pl.semaphore_wait(barrier, peers)

    def copy(lane, source, target, from_own=False):
        there = block(2 * source + core)
        return pltpu.make_async_remote_copy(
            src_ref=block_ref if from_own else there,
            dst_ref=there,
            send_sem=send_sem.at[lane, source],
            recv_sem=recv_sem.at[lane, source],
            device_id=place(target),
            device_id_type=MESH,
        )

    def right(source, from_own=False):
        return copy(0, source, me + 2, from_own)

    def left(source, from_own=False):
        return copy(1, source, me - 2, from_own)

    def across(source, from_own=False):
        return copy(2, source, other, from_own)

    def from_across(source):
        there = block(2 * source + 1 - core)
        return pltpu.make_async_remote_copy(
            src_ref=there,
            dst_ref=there,
            send_sem=send_sem.at[2, source],
            recv_sem=recv_sem.at[2, source],
            device_id=place(other),
            device_id_type=MESH,
        )

    def process(index):
        piece = rows // 2

        def half(number, carry):
            here = pl.ds(pl.multiple_of(index * rows + number * piece, piece), piece)
            normed = low(norm_forward(wide(whole_ref[here, :]), gain_ref[...], shift_ref[...]))
            normed_ref[here, :] = normed
            product = dot_plain(normed, weight_ref[...])
            qkv_ref[here, 0:width] = low(product[:, 0:width] + bias_query)
            qkv_ref[here, width : 2 * width] = low(product[:, width : 2 * width])
            qkv_ref[here, 2 * width : 3 * width] = low(product[:, 2 * width :] + bias_value)
            return carry

        lax.fori_loop(0, 2, half, 0)

    @pl.when(chip < chips - 1)
    def _():
        right(chip, True).start()

    @pl.when(chip > 0)
    def _():
        left(chip, True).start()

    across(chip, True).start()
    for load in [own] + loads:
        load.wait()
    process(me)
    from_across(chip).wait_recv()
    process(other)
    for load in later_loads:
        load.wait()
    pages = page_ref.shape[0]
    for first in range(0, pages, pages // 5):
        here = slice(first, first + pages // 5)
        kv_ref[here, :] = low(dot_plain(page_ref[here, :], kv_weight_ref[...]) + kv_shift_ref[...])
    for step in range(1, chips):

        @pl.when(chip - step >= 0)
        def _():
            right(chip - step).wait_recv()

            @pl.when(chip < chips - 1)
            def _():
                right(chip - step).start()

            across(chip - step).start()

        @pl.when(chip + step < chips)
        def _():
            left(chip + step).wait_recv()

            @pl.when(chip > 0)
            def _():
                left(chip + step).start()

            across(chip + step).start()

        for source, there in ((chip - step, chip - step >= 0), (chip + step, chip + step < chips)):

            @pl.when(there)
            def _():
                process(2 * source + core)
                from_across(source).wait_recv()
                process(2 * source + 1 - core)

    ends_ref[0:SLOTS, :] = whole_ref[0:SLOTS, :]
    ends_ref[SLOTS : 2 * SLOTS, :] = whole_ref[count * rows - SLOTS : count * rows, :]
    for source in range(chips):
        across(source).wait_send()

        @pl.when((source <= chip) & (chip < chips - 1))
        def _():
            right(source).wait_send()

        @pl.when((source >= chip) & (chip > 0))
        def _():
            left(source).wait_send()


def gather_rows(block_in, gain, shift, weight, bias, page, kv_weight, kv_shift, count, collective_id):
    rows, features = block_in.shape
    width = features // count
    lanes_ok = width % 128 == 0
    bf = jnp.bfloat16
    vmem, anywhere = pl.BlockSpec(memory_space=pltpu.VMEM), pl.BlockSpec(memory_space=pl.ANY)
    return pl.pallas_call(
        functools.partial(gather_kernel, count, lanes_ok),
        out_shape=[
            jax.ShapeDtypeStruct((count * rows, features), bf),
            jax.ShapeDtypeStruct((count * rows, 3 * width), bf),
            jax.ShapeDtypeStruct((2 * SLOTS, features), bf),
            jax.ShapeDtypeStruct((page.shape[0], kv_weight.shape[1]), bf),
        ],
        in_specs=[anywhere, vmem, vmem, anywhere, vmem, anywhere, anywhere, vmem],
        out_specs=[vmem] * 4,
        scratch_shapes=[
            pltpu.VMEM((count * rows, features), bf),
            pltpu.VMEM((features, 3 * width), bf),
            pltpu.VMEM(page.shape, bf),
            pltpu.VMEM(kv_weight.shape, bf),
            pltpu.SemaphoreType.DMA((5,)),
            pltpu.SemaphoreType.DMA,
            pltpu.SemaphoreType.DMA((3, count // 2)),
            pltpu.SemaphoreType.DMA((3, count // 2)),
        ],
        compiler_params=pltpu.CompilerParams(
            collective_id=collective_id, has_side_effects=True, vmem_limit_bytes=VMEM_LIMIT
        ),
    )(block_in, gain, shift, weight, bias, page, kv_weight, kv_shift)


AXES = {"seq": 1, "chip": 1, "rows": 0}


def peer(axis, step, counts):
    row, me = lax.axis_index("rows"), lax.axis_index("seq")
    if axis == "rows":
        there = lax.rem(row + step, counts["rows"])
        return (there, me), there
    if axis == "seq":
        there = lax.rem(me + step, counts["seq"])
        return (row, there), there
    there = lax.rem(me // 2 + step, counts["chip"])
    return (row, there * 2 + me % 2), there


def own_place(axis):
    if axis == "rows":
        return lax.axis_index("rows")
    return lax.axis_index("seq") if axis == "seq" else lax.axis_index("seq") // 2


def whole(ref, index):
    return ref


def lead(ref, index):
    return ref.at[index]


def second_dim(ref, index):
    return ref.at[:, index]


def rows_of(size, first=0, lanes=None):
    def find(ref, index):
        rows = pl.ds(pl.multiple_of(index * size, size), size)
        return ref.at[rows] if lanes is None else ref.at[rows, first : first + lanes]

    return find


def columns_of(size, first=0):
    def find(ref, index):
        return ref.at[:, pl.ds(pl.multiple_of(first + index * size, size), size)]

    return find


def greet(axes, counts):
    barrier = pltpu.get_barrier_semaphore()
    total = 0
    for axis in axes:
        for step in range(1, counts[axis]):
            pl.semaphore_signal(
                barrier, inc=1, device_id=peer(axis, step, counts)[0], device_id_type=MESH
            )
            total += 1
    pl.semaphore_wait(barrier, total)


def steps_of(total):
    return sorted(range(1, total), key=lambda step: -min(step, total - step))


class Transfers:
    def __init__(self, part, counts, own_sem, send_sem, recv_sem):
        from_ref, to_ref, axis, source, target = part
        here = own_place(axis)
        self.own = pltpu.make_async_copy(source(from_ref, here), target(to_ref, here), own_sem)
        self.remote = []
        for step in steps_of(counts[axis]):
            device, there = peer(axis, step, counts)
            self.remote.append(
                pltpu.make_async_remote_copy(
                    src_ref=source(from_ref, there),
                    dst_ref=target(to_ref, here),
                    send_sem=send_sem.at[step],
                    recv_sem=recv_sem.at[step],
                    device_id=device,
                    device_id_type=MESH,
                )
            )

    def start(self):
        for copy in self.remote:
            copy.start()
        self.own.start()

    def arrived(self):
        self.own.wait()
        for copy in self.remote:
            copy.wait_recv()

    def sent(self):
        for copy in self.remote:
            copy.wait_send()


def axes_of(axes):
    return tuple(axis for axis in ("seq", "rows") if axis in axes)


def exchange_kernel(counts, ins_count, parts, *refs):
    outs_count = len({part[1] for part in parts})
    ins, outs = refs[:ins_count], refs[ins_count : ins_count + outs_count]
    own_sem, send_sem, recv_sem = refs[ins_count + outs_count :]
    greet(axes_of([part[2] for part in parts]), counts)
    moves = [
        Transfers(
            (ins[part[0]], outs[part[1]]) + part[2:],
            counts,
            own_sem.at[index],
            send_sem.at[index],
            recv_sem.at[index],
        )
        for index, part in enumerate(parts)
    ]
    for move in moves:
        move.start()
    for move in moves:
        move.arrived()
    for move in moves:
        move.sent()


def exchange(arrays, shapes, parts, counts, collective_id):
    longest = max(counts[part[2]] for part in parts)
    return pl.pallas_call(
        functools.partial(exchange_kernel, counts, len(arrays), parts),
        out_shape=shapes,
        in_specs=[pl.BlockSpec(memory_space=pl.ANY)] * len(arrays),
        out_specs=[pl.BlockSpec(memory_space=pl.ANY)] * len(shapes),
        scratch_shapes=[
            pltpu.SemaphoreType.DMA((len(parts),)),
            pltpu.SemaphoreType.DMA((len(parts), longest)),
            pltpu.SemaphoreType.DMA((len(parts), longest)),
        ],
        compiler_params=pltpu.CompilerParams(
            collective_id=collective_id, has_side_effects=True
        ),
    )(*arrays)


def add_slots(ref):
    return low(functools.reduce(jnp.add, [wide(ref[i]) for i in range(ref.shape[0])]))


def packed(sizes, lanes):
    places, row, lane = [], 0, 0
    for size in sizes:
        if lane + size > lanes:
            row, lane = row + 1, 0
        places.append((row, lane))
        lane += size
    return places


def finish_kernel(counts, sizes, places, lanes_ok, *refs):
    over_chips, over_rows, opened = sizes
    total_count = over_chips + over_rows + opened
    refs = list(refs)

    def take(number):
        found = refs[:number]
        del refs[:number]
        return found

    dqkv_ref, normed_in, inputs_ref, gain_ref, weight_in, part_ref = take(6)
    vectors_in = take(len(places) - 2)
    chips_in, rows_in, open_in = take(over_chips), take(over_rows), take(opened)
    grad_out, vectors_out, part_out, own_out = take(4)
    outs = take(total_count)
    tokens_ref, weight_ref, normed_ref, dqkv_here = take(4)
    vectors_ref, vector_slots, vector_sum = take(3)
    own_ref, own_slots, own_sum, own_block = take(4)
    row_slots, row_sum = take(over_rows + opened), take(over_rows + opened)
    chip_slots, chip_sum = take(total_count), take(total_count)
    load_sem, *sems = take(4)
    greet(("seq", "rows"), counts)
    number = 0

    def move(*part):
        nonlocal number
        found = Transfers(part, counts, *(sem.at[number] for sem in sems))
        number += 1
        return found

    count = counts["seq"]
    width = dqkv_ref.shape[1] // 3
    tokens = dqkv_ref.shape[0] // count
    if lanes_ok:
        home = [
            move(
                dqkv_ref,
                tokens_ref,
                "seq",
                rows_of(tokens, part * width, width),
                columns_of(width, part * width * count),
            )
            for part in range(3)
        ]
    else:
        home = [move(dqkv_ref, tokens_ref, "seq", rows_of(tokens), lead)]
    open_rows = [
        move(ref, slots, "rows", columns_of(slots.shape[2]), lead)
        for ref, slots in zip(open_in, row_slots[over_rows:])
    ]
    for item in open_rows:
        item.start()
    sources = [*chips_in, *rows_in, dqkv_ref, normed_in, weight_in]
    targets = [*chip_slots[:over_chips], *row_slots[:over_rows], dqkv_here, normed_ref, weight_ref]
    loads = [
        pltpu.make_async_copy(ref, there, load_sem.at[index])
        for index, (ref, there) in enumerate(zip(sources, targets))
    ]
    for load in loads:
        load.start()
    chip_moves, last = [], []

    def to_chips(index):
        total, slots = row_sum[index], chip_slots[over_chips + index]
        total[...] = add_slots(row_slots[index])
        chip_moves.append(move(total, slots, "chip", rows_of(slots.shape[1]), lead))
        chip_moves[-1].start()

    def to_rows(index):
        total = chip_sum[index]
        total[...] = add_slots(chip_slots[index])
        last.append(move(total, outs[index], "rows", whole, columns_of(total.shape[1])))
        last[-1].start()

    for index in range(over_rows):
        loads[over_chips + index].wait()
        to_chips(index)
    for item in home:
        item.start()
    for index in range(over_chips):
        loads[index].wait()
        to_rows(index)
    for load in loads[over_chips + over_rows :]:
        load.wait()
    own_grad = dot_left(dqkv_here[...], normed_ref[...]).T
    own_ref[...] = low(own_grad).reshape(own_ref.shape)
    own_rows = move(own_ref, own_slots, "rows", second_dim, lead)
    own_rows.start()
    for index, item in enumerate(open_rows):
        item.arrived()
        to_chips(over_rows + index)
    last.append(move(part_ref, part_out, "chip", whole, lead))
    last[-1].start()
    own_rows.arrived()
    own_sum[...] = add_slots(own_slots)
    if lanes_ok:
        own_chips = [
            move(
                own_sum.at[:, :, part * width : (part + 1) * width],
                own_block,
                "seq",
                lead,
                columns_of(width, part * width * count),
            )
            for part in range(3)
        ]
    else:
        own_chips = [move(own_sum, own_block, "seq", lead, lead)]
    for item in own_chips:
        item.start()
    for item in home:
        item.arrived()
    if lanes_ok:
        grad_tokens = tokens_ref[...]
    else:
        grad_tokens = jnp.concatenate(
            [
                tokens_ref[index, :, part * width : (part + 1) * width]
                for part in range(3)
                for index in range(count)
            ],
            axis=1,
        )
    normed_grad = dot_right(grad_tokens, weight_ref[...])
    values = wide(inputs_ref[...])
    center = values - jnp.mean(values, axis=-1, keepdims=True)
    scale = lax.rsqrt(jnp.mean(center * center, axis=-1, keepdims=True) + EPSILON)
    unit = center * scale
    gain_grad = jnp.sum(normed_grad * unit, axis=0, keepdims=True)
    shift_grad = jnp.sum(normed_grad, axis=0, keepdims=True)
    normed_grad = normed_grad * gain_ref[...]
    grad_out[...] = scale * (
        normed_grad
        - jnp.mean(normed_grad, axis=-1, keepdims=True)
        - unit * jnp.mean(normed_grad * unit, axis=-1, keepdims=True)
    )
    vectors_ref[...] = jnp.zeros_like(vectors_ref)
    for vector, (row, lane) in zip(
        [gain_grad, shift_grad] + [ref[...] for ref in vectors_in], places
    ):
        size = vector.shape[1] // count
        for index in range(count):
            vectors_ref[index, row : row + 1, lane : lane + size] = vector[
                :, index * size : (index + 1) * size
            ]
    vectors = move(vectors_ref, vector_slots, "seq", lead, lead)
    vectors.start()
    for index, item in enumerate(chip_moves):
        item.arrived()
        to_rows(over_chips + index)
    for item in own_chips:
        item.arrived()
    if lanes_ok:
        last.append(move(own_block, own_out, "rows", whole, rows_of(own_block.shape[0])))
    else:
        last.append(move(own_block, own_out, "rows", whole, lead))
    last[-1].start()
    vectors.arrived()
    vector_sum[...] = functools.reduce(jnp.add, [vector_slots[i] for i in range(count)])
    last.append(move(vector_sum, vectors_out, "rows", whole, lead))
    last[-1].start()
    for item in last:
        item.arrived()
    for item in home + open_rows + [own_rows, vectors] + chip_moves + own_chips + last:
        item.sent()


def finish(
    dqkv,
    normed,
    inputs,
    gain,
    weight,
    part,
    vectors,
    over_chips,
    over_rows,
    rows_open,
    counts,
    collective_id,
):
    count, chips, rows = counts["seq"], counts["chip"], counts["rows"]
    length, all_width = dqkv.shape
    features = inputs.shape[1]
    width = all_width // 3
    lanes_ok = width % 128 == 0
    tokens, short = length // count, features // count // rows
    bf, lanes = jnp.bfloat16, 512
    if lanes_ok:
        tokens_shape = (tokens, all_width * count)
        own_block, own_out = (short, all_width * count), (rows * short, all_width * count)
    else:
        tokens_shape = (count, tokens, all_width)
        own_block, own_out = (count, short, all_width), (rows, count, short, all_width)
    pieces = [features // count] * 2 + [vector.shape[1] // count for vector in vectors]
    places = packed(pieces, lanes)
    vector = (8, lanes)
    shares = [term.shape[1:] for term in over_rows]
    shares += [(term.shape[0], term.shape[1] // rows) for term in rows_open]
    blocks = [term.shape[1:] for term in over_chips]
    blocks += [(shape[0] // chips, shape[1]) for shape in shares]
    outs = [own_out] + [(shape[0], shape[1] * rows) for shape in blocks]
    own_share = (count, short, all_width)
    scratch = [(count, rows, short, all_width), (rows,) + own_share, own_share, own_block]
    scratch += [(rows,) + shape for shape in shares] + shares
    scratch += [(chips,) + shape for shape in blocks] + blocks
    moves = 3 + 3 + 2 + 3 + len(rows_open) + len(shares) + len(blocks)
    longest = max(count, rows)
    vmem, anywhere = pl.BlockSpec(memory_space=pltpu.VMEM), pl.BlockSpec(memory_space=pl.ANY)
    rest = [*over_chips, *over_rows, *rows_open]
    found = pl.pallas_call(
        functools.partial(
            finish_kernel,
            counts,
            (len(over_chips), len(over_rows), len(rows_open)),
            places,
            lanes_ok,
        ),
        out_shape=[
            jax.ShapeDtypeStruct(inputs.shape, jnp.float32),
            jax.ShapeDtypeStruct((rows,) + vector, jnp.float32),
            jax.ShapeDtypeStruct((chips,) + part.shape, bf),
        ]
        + [jax.ShapeDtypeStruct(shape, bf) for shape in outs],
        in_specs=[anywhere, anywhere, vmem, vmem, anywhere, anywhere]
        + [vmem] * len(vectors)
        + [anywhere] * len(rest),
        out_specs=[vmem] + [anywhere] * (2 + len(outs)),
        scratch_shapes=[
            pltpu.VMEM(tokens_shape, bf),
            pltpu.VMEM(weight.shape, bf),
            pltpu.VMEM(normed.shape, bf),
            pltpu.VMEM(dqkv.shape, bf),
            pltpu.VMEM((count,) + vector, jnp.float32),
            pltpu.VMEM((count,) + vector, jnp.float32),
            pltpu.VMEM(vector, jnp.float32),
        ]
        + [pltpu.VMEM(shape, bf) for shape in scratch]
        + [
            pltpu.SemaphoreType.DMA((len(over_chips) + len(over_rows) + 3,)),
            pltpu.SemaphoreType.DMA((moves,)),
            pltpu.SemaphoreType.DMA((moves, longest)),
            pltpu.SemaphoreType.DMA((moves, longest)),
        ],
        compiler_params=pltpu.CompilerParams(
            collective_id=collective_id, has_side_effects=True, vmem_limit_bytes=VMEM_LIMIT
        ),
    )(dqkv, normed, inputs, gain, weight, part, *vectors, *rest)
    return found[0], found[1], [(r, lane, size) for (r, lane), size in zip(places, pieces)], found[2:]


def widen_kernel(*refs):
    for given, out in zip(refs[: len(refs) // 2], refs[len(refs) // 2 :]):
        out[...] = wide(given[...])


def widen(arrays):
    vmem = pl.BlockSpec(memory_space=pltpu.VMEM)
    return pl.pallas_call(
        widen_kernel,
        out_shape=[jax.ShapeDtypeStruct(array.shape, jnp.float32) for array in arrays],
        in_specs=[vmem] * len(arrays),
        out_specs=[vmem] * len(arrays),
        compiler_params=pltpu.CompilerParams(vmem_limit_bytes=VMEM_LIMIT),
    )(*arrays)


def head_lanes(width):
    return lax.broadcasted_iota(jnp.int32, (1, width), 1) // DEPTH


def pick_head(values, head, width):
    if width == DEPTH:
        return values
    return jnp.where(head_lanes(width) == head, values, jnp.zeros_like(values))


def begin_of(start_ref, position):
    begin = jnp.zeros_like(position)
    for page in range(1, PAGES):
        begin = jnp.where(position >= start_ref[page], start_ref[page], begin)
    return begin


def as_row(column):
    return jnp.broadcast_to(column, (column.shape[0], 8)).T[:1]


def self_forward_kernel(qkv_ref, start_ref, out_ref, stat_ref):
    length, width = out_ref.shape
    heads = width // DEPTH
    blocks = length // BLOCK
    for index in range(blocks):
        rows = pl.ds(index * BLOCK, BLOCK)
        keys_end = (index + 1) * BLOCK
        query = qkv_ref[rows, 0:width]
        position = index * BLOCK + lax.broadcasted_iota(jnp.int32, (BLOCK, 1), 0)
        begin = begin_of(start_ref, position)
        if index == blocks - 1 or index <= 1:
            cuts = [(0, keys_end)]
        else:
            cuts = [(0, BLOCK), (BLOCK, index * BLOCK), (index * BLOCK, keys_end)]
        outs, stats = [], []
        for head in range(heads):
            query_head = pick_head(query, head, width) * jnp.bfloat16(SCALE)
            scores = []
            for low_end, high_end in cuts:
                part = dot_right(query_head, qkv_ref[low_end:high_end, width : 2 * width])
                if low_end == 0 or high_end == keys_end:
                    column = low_end + lax.broadcasted_iota(jnp.int32, part.shape, 1)
                    allowed = column >= begin
                    if high_end == keys_end:
                        allowed = allowed & (column <= position)
                    part = jnp.where(allowed, part, NEGATIVE)
                scores.append(part)
            top = functools.reduce(
                jnp.maximum, [jnp.max(part, axis=-1, keepdims=True) for part in scores]
            )
            total, mixed = 0.0, 0.0
            for (low_end, high_end), part in zip(cuts, scores):
                weight = jnp.exp(part - top)
                total = total + jnp.sum(weight, axis=-1, keepdims=True)
                mixed = mixed + dot_plain(
                    low(weight), qkv_ref[low_end:high_end, 2 * width : 3 * width]
                )
            outs.append(mixed / total)
            stats.append(top + jnp.log(total))
        merged = outs[0]
        for head in range(1, heads):
            merged = jnp.where(head_lanes(width) == head, outs[head], merged)
        out_ref[rows, :] = low(merged)
        for head in range(heads):
            stat_ref[head : head + 1, rows] = as_row(stats[head])


def self_forward(qkv, starts):
    length, width = qkv.shape[0], qkv.shape[1] // 3
    heads = width // DEPTH
    return pl.pallas_call(
        self_forward_kernel,
        out_shape=(
            jax.ShapeDtypeStruct((length, width), jnp.bfloat16),
            jax.ShapeDtypeStruct((heads, length), jnp.float32),
        ),
        in_specs=[
            pl.BlockSpec(memory_space=pltpu.VMEM),
            pl.BlockSpec(memory_space=pltpu.SMEM),
        ],
        out_specs=[pl.BlockSpec(memory_space=pltpu.VMEM)] * 2,
        compiler_params=pltpu.CompilerParams(vmem_limit_bytes=VMEM_LIMIT),
    )(qkv, starts)


def self_backward_kernel(counts, hosted, *refs):
    size = len(hosted)
    qkv_ref, out_ref, blocks_ref, slots_ref, start_ref, stat_ref = refs[:6]
    sent, dqkv_ref, stacks = refs[6 : 6 + size], refs[6 + size], refs[7 + size : 7 + 2 * size]
    dk_ref, dv_ref, grad_ref, own_sem, send_sem, recv_sem = refs[7 + 2 * size :]
    length, width = out_ref.shape
    heads = width // DEPTH
    blocks = length // BLOCK
    greet(("seq", "rows"), counts)
    moves = []
    for index, ((axis, how), ref, stack) in enumerate(zip(hosted, sent, stacks)):
        source = rows_of(stack.shape[1]) if how == "rows" else columns_of(stack.shape[2])
        part = (ref, stack, axis, source, lead)
        moves.append(
            Transfers(part, counts, own_sem.at[index], send_sem.at[index], recv_sem.at[index])
        )
        moves[-1].start()
    dk_ref[...] = jnp.zeros_like(dk_ref)
    dv_ref[...] = jnp.zeros_like(dv_ref)
    grad_ref[...] = blocks_ref[...]
    slots = add_slots(slots_ref)
    in_front = lax.broadcasted_iota(jnp.int32, slots.shape, 0) < start_ref[PAGES]
    nothing = jnp.zeros_like(slots)
    grad_ref[0:SLOTS, :] += jnp.where(in_front, slots, nothing)
    grad_ref[length - SLOTS : length, :] += jnp.where(in_front, nothing, slots)

    def query_block(index, carry):
        rows = pl.ds(pl.multiple_of(index * BLOCK, BLOCK), BLOCK)
        query = qkv_ref[rows, 0:width]
        grad = grad_ref[rows, :]
        product = (wide(grad) * wide(out_ref[rows, :])).T
        position = index * BLOCK + lax.broadcasted_iota(jnp.int32, (1, BLOCK), 1)
        begin = begin_of(start_ref, position)
        query_heads = [pick_head(query, head, width) * jnp.bfloat16(SCALE) for head in range(heads)]
        grad_heads = [pick_head(grad, head, width) for head in range(heads)]
        stats = [stat_ref[head : head + 1, rows] for head in range(heads)]
        deltas = [
            jnp.sum(product[head * DEPTH : (head + 1) * DEPTH, :], axis=0, keepdims=True)
            for head in range(heads)
        ]

        def key_block(key_index, sums):
            keys = pl.ds(pl.multiple_of(key_index * BLOCK, BLOCK), BLOCK)
            key = qkv_ref[keys, width : 2 * width]
            value = qkv_ref[keys, 2 * width : 3 * width]
            row = key_index * BLOCK + lax.broadcasted_iota(jnp.int32, (BLOCK, 1), 0)
            allowed = (row >= begin) & (row <= position)
            dk_part, dv_part, found = 0.0, 0.0, []
            for head in range(heads):
                scores = jnp.where(allowed, dot_right(key, query_heads[head]), NEGATIVE)
                prob = jnp.exp(scores - stats[head])
                dv_part = dv_part + dot_plain(low(prob), grad_heads[head])
                grad_prob = dot_right(value, grad_heads[head])
                grad_score = low(prob * (grad_prob - deltas[head]))
                dk_part = dk_part + dot_plain(grad_score, query_heads[head])
                found.append(sums[head] + dot_left(grad_score, key))
            dk_ref[keys, :] += dk_part
            dv_ref[keys, :] += dv_part
            return tuple(found)

        zero = tuple(jnp.zeros((BLOCK, width), jnp.float32) for _ in range(heads))
        sums = lax.fori_loop(0, index + 1, key_block, zero)
        merged = sums[0]
        for head in range(1, heads):
            merged = jnp.where(head_lanes(width) == head, sums[head], merged)
        dqkv_ref[rows, 0:width] = low(merged * SCALE)
        return carry

    lax.fori_loop(0, blocks, query_block, 0)
    dqkv_ref[:, width : 2 * width] = low(dk_ref[...])
    dqkv_ref[:, 2 * width : 3 * width] = low(dv_ref[...])
    for item in moves:
        item.arrived()
    for item in moves:
        item.sent()


def self_backward(
    qkv, out, grad, slots, starts, stats, sent, hosted, counts, collective_id
):
    length, width = out.shape
    stacks = []
    for array, (axis, how) in zip(sent, hosted):
        rows, columns = array.shape
        total = counts[axis]
        block = (rows // total, columns) if how == "rows" else (rows, columns // total)
        stacks.append(jax.ShapeDtypeStruct((total,) + block, array.dtype))
    longest = max(counts["seq"], counts["rows"])
    vmem, anywhere = pl.BlockSpec(memory_space=pltpu.VMEM), pl.BlockSpec(memory_space=pl.ANY)
    return pl.pallas_call(
        functools.partial(self_backward_kernel, counts, hosted),
        out_shape=[jax.ShapeDtypeStruct((length, 3 * width), jnp.bfloat16), *stacks],
        in_specs=[vmem] * 4
        + [pl.BlockSpec(memory_space=pltpu.SMEM), vmem]
        + [anywhere] * len(sent),
        out_specs=[vmem] + [anywhere] * len(sent),
        scratch_shapes=[pltpu.VMEM((length, width), jnp.float32)] * 2
        + [
            pltpu.VMEM((length, width), jnp.bfloat16),
            pltpu.SemaphoreType.DMA((len(sent),)),
            pltpu.SemaphoreType.DMA((len(sent), longest)),
            pltpu.SemaphoreType.DMA((len(sent), longest)),
        ],
        compiler_params=pltpu.CompilerParams(
            collective_id=collective_id, has_side_effects=True, vmem_limit_bytes=VMEM_LIMIT
        ),
    )(qkv, out, grad, slots, starts, stats, *sent)


def cross_forward_kernel(query_ref, key_ref, value_ref, own_key_ref, own_value_ref, out_ref, stat_ref):
    tokens = query_ref.shape[0] - SLOTS
    width = query_ref.shape[1]
    for begin, size, keys, values in (
        (0, tokens, key_ref, value_ref),
        (tokens, SLOTS, own_key_ref, own_value_ref),
    ):
        query = query_ref[begin : begin + size, :]
        outs = []
        for head in range(width // DEPTH):
            query_head = pick_head(query, head, width) * jnp.bfloat16(SCALE)
            scores = dot_right(query_head, keys[...])
            column = lax.broadcasted_iota(jnp.int32, scores.shape, 1)
            scores = jnp.where(column < PAGE_TOK, scores, NEGATIVE)
            top = jnp.max(scores, axis=-1, keepdims=True)
            weight = jnp.exp(scores - top)
            total = jnp.sum(weight, axis=-1, keepdims=True)
            outs.append(dot_plain(low(weight), values[...]) / total)
            stat_ref[0, head : head + 1, begin : begin + size] = as_row(top + jnp.log(total))
        merged = outs[0]
        for head in range(1, len(outs)):
            merged = jnp.where(head_lanes(width) == head, outs[head], merged)
        out_ref[begin : begin + size, :] = low(merged)


def cross_forward(query, kv_big, kv_own):
    rows, features = query.shape
    pair = 2 * DEPTH
    steps = features // pair
    tall = pl.BlockSpec((rows, pair), lambda i: (0, i))
    keys = pl.BlockSpec((PAGE_PAD, pair), lambda i: (0, i))
    values = pl.BlockSpec((PAGE_PAD, pair), lambda i: (0, i + steps))
    return pl.pallas_call(
        cross_forward_kernel,
        grid=(steps,),
        out_shape=(
            jax.ShapeDtypeStruct((rows, features), jnp.bfloat16),
            jax.ShapeDtypeStruct((steps, 2, rows), jnp.float32),
        ),
        in_specs=[tall, keys, values, keys, values],
        out_specs=[tall, pl.BlockSpec((1, 2, rows), lambda i: (i, 0, 0))],
        compiler_params=pltpu.CompilerParams(vmem_limit_bytes=VMEM_LIMIT),
    )(query, kv_big, kv_big, kv_own, kv_own)


def cross_backward_kernel(
    counts,
    query_ref,
    key_ref,
    value_ref,
    own_key_ref,
    own_value_ref,
    out_ref,
    grad_ref,
    stat_ref,
    sent_ref,
    dq_ref,
    dk_ref,
    dv_ref,
    own_dk_ref,
    own_dv_ref,
    stack_ref,
    own_sem,
    send_sem,
    recv_sem,
):
    step, steps = pl.program_id(0), pl.num_programs(0)

    def move():
        part = (sent_ref, stack_ref, "chip", rows_of(stack_ref.shape[1]), lead)
        return Transfers(part, counts, own_sem, send_sem, recv_sem)

    @pl.when(step == 0)
    def _():
        greet(("chip",), counts)
        move().start()

    tokens = query_ref.shape[0] - SLOTS
    width = query_ref.shape[1]
    row = lax.broadcasted_iota(jnp.int32, (PAGE_PAD, 1), 0)
    for begin, size, keys, values, dk_out, dv_out in (
        (0, tokens, key_ref, value_ref, dk_ref, dv_ref),
        (tokens, SLOTS, own_key_ref, own_value_ref, own_dk_ref, own_dv_ref),
    ):
        rows = slice(begin, begin + size)
        query, grad = query_ref[rows, :], grad_ref[rows, :]
        product = (wide(grad) * wide(out_ref[rows, :])).T
        dk_sum, dv_sum, found = 0.0, 0.0, []
        for head in range(width // DEPTH):
            query_head = pick_head(query, head, width) * jnp.bfloat16(SCALE)
            grad_head = pick_head(grad, head, width)
            delta = jnp.sum(product[head * DEPTH : (head + 1) * DEPTH, :], axis=0, keepdims=True)
            scores = dot_right(keys[...], query_head)
            scores = jnp.where(row < PAGE_TOK, scores, NEGATIVE)
            prob = jnp.exp(scores - stat_ref[0, head : head + 1, rows])
            dv_sum = dv_sum + dot_plain(low(prob), grad_head)
            grad_prob = dot_right(values[...], grad_head)
            grad_score = low(prob * (grad_prob - delta))
            dk_sum = dk_sum + dot_plain(grad_score, query_head)
            found.append(dot_left(grad_score, keys[...]))
        merged = found[0]
        for head in range(1, len(found)):
            merged = jnp.where(head_lanes(width) == head, found[head], merged)
        dq_ref[rows, :] = low(merged * SCALE)
        dk_out[...] = low(dk_sum)
        dv_out[...] = low(dv_sum)

    @pl.when(step == steps - 1)
    def _():
        found = move()
        found.arrived()
        found.sent()


def cross_backward(query, kv_big, kv_own, out, grad, stats, sent, counts, collective_id):
    rows, features = query.shape
    pair = 2 * DEPTH
    steps = features // pair
    tall = pl.BlockSpec((rows, pair), lambda i: (0, i))
    keys = pl.BlockSpec((PAGE_PAD, pair), lambda i: (0, i))
    values = pl.BlockSpec((PAGE_PAD, pair), lambda i: (0, i + steps))
    page = jax.ShapeDtypeStruct((PAGE_PAD, features), jnp.bfloat16)
    chips = counts["chip"]
    stack = jax.ShapeDtypeStruct(
        (chips, sent.shape[0] // chips, sent.shape[1]), jnp.bfloat16
    )
    anywhere = pl.BlockSpec(memory_space=pl.ANY)
    return pl.pallas_call(
        functools.partial(cross_backward_kernel, counts),
        grid=(steps,),
        out_shape=(
            jax.ShapeDtypeStruct((rows, features), jnp.bfloat16),
            page,
            page,
            page,
            page,
            stack,
        ),
        in_specs=[
            tall,
            keys,
            values,
            keys,
            values,
            tall,
            tall,
            pl.BlockSpec((1, 2, rows), lambda i: (i, 0, 0)),
            anywhere,
        ],
        out_specs=[tall, keys, keys, keys, keys, anywhere],
        scratch_shapes=[
            pltpu.SemaphoreType.DMA,
            pltpu.SemaphoreType.DMA((chips,)),
            pltpu.SemaphoreType.DMA((chips,)),
        ],
        compiler_params=pltpu.CompilerParams(
            collective_id=collective_id, has_side_effects=True, vmem_limit_bytes=VMEM_LIMIT
        ),
    )(query, kv_big, kv_big, kv_own, kv_own, out, grad, stats, sent)


def body(
    inputs,
    memory,
    out_grad,
    segment_ids,
    page_order,
    norm1_gain,
    norm1_bias,
    qkv_weight,
    qv_bias,
    self_out_weight,
    self_out_bias,
    norm2_gain,
    norm2_bias,
    cross_q_weight,
    cross_q_bias,
    cross_kv_weight,
    cross_v_bias,
    cross_out_weight,
    cross_out_bias,
    norm3_gain,
    norm3_bias,
    fc1_weight,
    fc1_bias,
    fc2_weight,
    fc2_bias,
):
    tokens, features = inputs.shape[1:]
    count = lax.axis_size("seq")
    me = lax.axis_index("seq")
    length = tokens * count
    width = features // count
    rows_count = lax.axis_size("rows")
    counts = {"seq": count, "chip": count // 2, "rows": rows_count}
    core = me % 2

    def blocks_of(first, which):
        size = first.shape[1] // count
        return jnp.concatenate(
            [
                lax.dynamic_slice_in_dim(first, (2 * chip + which) * size, size, 1)
                for chip in range(count // 2)
            ],
            axis=1,
        )

    def pair_sum(first, second, behind=None):
        given = swap(low(dot_left(blocks_of(first, 1 - core), second)))
        if behind is not None:
            given = after(given, behind)
        return low(dot_left(blocks_of(first, core), second) + wide(given))

    def swap(value):
        return lax.ppermute(value, "seq", [(i, i ^ 1) for i in range(count)])

    def after(value, other):
        return lax.optimization_barrier((value, other))[0]

    mem_rows = memory.shape[1]
    sharers = PAGE_TOK // mem_rows
    row_segs = segment_ids[0]
    row_pages = page_order[0]
    gain_one, shift_one = wide(norm1_gain), wide(norm1_bias)
    gain_two, shift_two = wide(norm2_gain), wide(norm2_bias)
    gain_three, shift_three = wide(norm3_gain), wide(norm3_bias)

    starts = jnp.sum(row_segs[None, :] < jnp.arange(PAGES)[:, None], axis=1, dtype=jnp.int32)
    big_page = row_segs[length // 2]
    big_start = jnp.sum(row_segs < big_page, dtype=jnp.int32)
    own_page = lax.dynamic_index_in_dim(row_pages, me // sharers, 0, keepdims=False)
    slot = jnp.arange(SLOTS)
    in_front = (slot < big_start)[:, None]
    slot_segs = jnp.where(slot < big_start, row_segs[:SLOTS], row_segs[length - SLOTS :])
    slot_mine = (slot_segs == own_page) & (slot * sharers // SLOTS == me % sharers)
    home_segs = lax.dynamic_slice_in_dim(row_segs, me * tokens, tokens, 0)
    active = jnp.concatenate((home_segs == big_page, slot_mine))[:, None]
    is_first, is_last = me == 0, me == count - 1

    def slots_of(front, back):
        return jnp.where(in_front, front, back)

    mem_own = memory[0]
    mem_page = mem_own
    if sharers > 1:
        groups = [[g * sharers + s for s in range(sharers)] for g in range(count // sharers)]
        mem_page = lax.all_gather(mem_own, "seq", axis=0, tiled=True, axis_index_groups=groups)
    mem_page = jnp.pad(mem_page, ((0, PAGE_PAD - PAGE_TOK), (0, 0)))
    gives_big = (own_page == big_page) & (me % sharers == 0)

    x_own = inputs[0]

    half = PAGE_PAD // 2
    masked_page = jnp.where(gives_big, mem_page, jnp.zeros_like(mem_page)).reshape(2, half, -1)
    pair_page = masked_page[core] + swap(masked_page[1 - core])
    at_end = jnp.where(core == 0, is_first, is_last)
    end_grad = jnp.where(core == 0, out_grad[0, :SLOTS], out_grad[0, tokens - SLOTS :])
    sent = jnp.concatenate((pair_page, jnp.where(at_end, end_grad, jnp.zeros_like(end_grad))))
    same_core = [[2 * chip + which for chip in range(count // 2)] for which in range(2)]
    bf = jnp.bfloat16
    lanes_ok = width % 128 == 0
    own_weight, own_bias = qkv_weight, wide(qv_bias)
    if not lanes_ok:
        own_weight = jnp.concatenate(
            [
                lax.dynamic_slice_in_dim(qkv_weight, part * features + me * width, width, 1)
                for part in range(3)
            ],
            axis=1,
        )
        own_bias = jnp.concatenate(
            [
                lax.dynamic_slice_in_dim(own_bias, part * features + me * width, width, 0)
                for part in range(2)
            ]
        )
    kv_shift = jnp.concatenate((jnp.zeros((features,), jnp.float32), wide(cross_v_bias)))
    normed_all, qkv, x_ends, kv_own = gather_rows(
        x_own,
        gain_one[None, :],
        shift_one[None, :],
        own_weight,
        own_bias[None, :],
        mem_page,
        cross_kv_weight,
        kv_shift[None, :],
        count,
        0,
    )
    mine = lax.psum(after(sent, x_ends), "seq", axis_index_groups=same_core)
    mixed, mixed_stats = self_forward(qkv, starts)
    chosen = slots_of(mixed[:SLOTS], mixed[length - SLOTS :])
    if lanes_ok:
        blocks_mixed, slots_mixed = exchange(
            (mixed, chosen),
            (
                jax.ShapeDtypeStruct((tokens, features), bf),
                jax.ShapeDtypeStruct((SLOTS, features), bf),
            ),
            (
                (1, 1, "seq", whole, columns_of(width)),
                (0, 0, "seq", rows_of(tokens), columns_of(width)),
            ),
            counts,
            1,
        )
    else:
        blocks_mixed, slots_mixed = exchange(
            (mixed, chosen),
            (
                jax.ShapeDtypeStruct((count, tokens, width), bf),
                jax.ShapeDtypeStruct((count, SLOTS, width), bf),
            ),
            ((1, 1, "seq", whole, lead), (0, 0, "seq", rows_of(tokens), lead)),
            counts,
            1,
        )
        blocks_mixed, slots_mixed = (
            blocks.transpose(1, 0, 2).reshape(blocks.shape[1], -1)
            for blocks in (blocks_mixed, slots_mixed)
        )
    mine = after(mine, slots_mixed)
    theirs = swap(mine)
    zeroth, first = jnp.where(core == 0, mine, theirs), jnp.where(core == 0, theirs, mine)
    mem_big = jnp.concatenate((zeroth[:half], first[:half]))
    front_grad, back_grad = zeroth[half:], first[half:]
    attended = jnp.concatenate((blocks_mixed, slots_mixed))
    resid = wide(
        jnp.concatenate((x_own, slots_of(x_ends[:SLOTS], x_ends[SLOTS:])))
    )
    resid_one = resid + dot_plain(attended, self_out_weight) + wide(self_out_bias)
    normed_two = low(norm_forward(resid_one, gain_two, shift_two))
    cross_queries = low(dot_plain(normed_two, cross_q_weight) + wide(cross_q_bias))
    kv_big = low(dot_plain(mem_big, cross_kv_weight) + kv_shift)
    cross_low, cross_stats = cross_forward(cross_queries, kv_big, kv_own)
    resid_two = resid_one + dot_plain(cross_low, cross_out_weight) + wide(cross_out_bias)
    normed_three = low(norm_forward(resid_two, gain_three, shift_three))
    pre_act = dot_plain(normed_three, fc1_weight) + wide(fc1_bias)
    hidden_act = low(gelu_exact(pre_act))
    final = low(resid_two + dot_plain(hidden_act, fc2_weight) + wide(fc2_bias))

    grad_out = jnp.concatenate((out_grad[0], slots_of(front_grad, back_grad)))
    grad_out = jnp.where(active, grad_out, jnp.zeros_like(grad_out))
    grad_act = dot_right(grad_out, fc2_weight)
    _, gelu_pull = jax.vjp(gelu_exact, pre_act)
    grad_pre = low(gelu_pull(grad_act)[0])
    grad_fc2_b = jnp.sum(wide(grad_out), axis=0)
    grad_fc2_w = pair_sum(hidden_act, grad_out, grad_pre)
    fc2_share = lax.psum_scatter(grad_fc2_w, "rows", scatter_dimension=1, tiled=True)
    grad_normed_three = dot_right(grad_pre, fc1_weight)
    grad_fc1_w = pair_sum(normed_three, grad_pre, grad_normed_three)
    fc1_share = lax.psum_scatter(grad_fc1_w, "rows", scatter_dimension=1, tiled=True)
    grad_fc1_b = jnp.sum(wide(grad_pre), axis=0)
    grad_two_norm, grad_gain_three, grad_shift_three = norm_backward(
        resid_two, gain_three, shift_three, grad_normed_three
    )
    grad_resid_two = wide(grad_out) + grad_two_norm
    grad_branch_two = low(grad_resid_two)
    grad_co_w = pair_sum(cross_low, grad_branch_two)
    grad_co_b = jnp.sum(wide(grad_branch_two), axis=0)
    grad_cross_low = low(dot_right(grad_branch_two, cross_out_weight))
    grad_cross_low = after(grad_cross_low, (grad_fc1_w, grad_fc2_w, grad_co_w))
    grad_cross_q, big_dk, big_dv, own_dk, own_dv, fc2_stack = cross_backward(
        cross_queries, kv_big, kv_own, cross_low, grad_cross_low, cross_stats, fc2_share, counts, 5
    )
    grad_cq_w = pair_sum(normed_two, grad_cross_q)
    grad_cq_b = jnp.sum(wide(grad_cross_q), axis=0)
    grad_one_norm, grad_gain_two, grad_shift_two = norm_backward(
        resid_one, gain_two, shift_two, dot_right(grad_cross_q, cross_q_weight)
    )
    grad_resid_one = grad_resid_two + grad_one_norm
    grad_branch_one = low(grad_resid_one)
    grad_o_w = pair_sum(attended, grad_branch_one)
    grad_o_b = jnp.sum(wide(grad_branch_one), axis=0)
    grad_attended = low(dot_right(grad_branch_one, self_out_weight))
    if lanes_ok:
        given, home_part, slot_part = (grad_attended,), (0, 0), (0, 1)

        def piece(first, size):
            def find(ref, index):
                return ref.at[
                    first : first + size, pl.ds(pl.multiple_of(index * width, width), width)
                ]

            return find

        pieces = piece(0, tokens), piece(tokens, SLOTS)
    else:
        by_device = grad_attended.reshape(-1, count, width).transpose(1, 0, 2)
        given, home_part, slot_part = (by_device[:, :tokens], by_device[:, tokens:]), (0, 0), (1, 1)
        pieces = lead, lead
    grad_mixed, slots_grad = exchange(
        given,
        (
            jax.ShapeDtypeStruct((length, width), bf),
            jax.ShapeDtypeStruct((count, SLOTS, width), bf),
        ),
        (
            home_part + ("seq", pieces[0], rows_of(tokens)),
            slot_part + ("seq", pieces[1], lead),
        ),
        counts,
        2,
    )
    dqkv, *stacks = self_backward(
        qkv,
        mixed,
        grad_mixed,
        slots_grad,
        jnp.concatenate((starts, big_start[None])),
        mixed_stats,
        (fc1_share, grad_co_w, grad_cq_w, grad_o_w),
        (("chip", "rows"),) + (("rows", "columns"),) * 3,
        counts,
        3,
    )

    slot_final = jnp.where(active[tokens:], final[tokens:], jnp.zeros_like(final[tokens:]))
    part_rows = PAGE_PAD // (count // 2)
    own_half = jnp.where(core == 0, big_dk, big_dv)
    own_half = own_half + swap(jnp.where(core == 0, big_dv, big_dk))
    part = lax.psum_scatter(
        after(own_half, (fc1_share, grad_mixed)), "seq", scatter_dimension=0, tiled=True, axis_index_groups=same_core
    )
    slot_half = jnp.where(core == 0, slot_final, low(grad_resid_one[tokens:]))
    slot_half = slot_half + swap(jnp.where(core == 0, low(grad_resid_one[tokens:]), slot_final))
    slot_half = lax.psum(after(slot_half, part), "seq", axis_index_groups=same_core)
    grad_ckv = jnp.concatenate((own_dk[:PAGE_TOK], own_dv[:PAGE_TOK]), axis=1)
    if sharers > 1:
        grad_ckv = lax.psum_scatter(
            grad_ckv, "seq", scatter_dimension=0, tiled=True, axis_index_groups=groups
        )
    part = after(part, dqkv)
    nothing = jnp.zeros_like(part)
    part_wide = jnp.concatenate(
        (jnp.where(core == 0, part, nothing), jnp.where(core == 0, nothing, part)), axis=1
    )
    part_memory = lax.dynamic_slice_in_dim(mem_big, me // 2 * part_rows, part_rows, 0)

    def ckv_terms(which):
        return dot_left(blocks_of(mem_own, which), grad_ckv) + dot_left(
            blocks_of(part_memory, which), part_wide
        )

    grad_ckv_w = low(ckv_terms(core) + wide(swap(low(ckv_terms(1 - core)))))
    grad_cv_b = jnp.sum(wide(grad_ckv[:, features:]), axis=0) + jnp.sum(
        wide(part_wide[:, features:]), axis=0
    )
    half_weight = lax.dynamic_slice_in_dim(cross_kv_weight, core * features, features, 1)
    part_grad = dot_right(part, half_weight)
    part_grad = part_grad.reshape(2, part_rows // 2, features)
    part_grad = low(part_grad[core] + swap(part_grad[1 - core]))
    memory_grad = dot_right(grad_ckv, cross_kv_weight)

    def at_home(own, returned):
        front = is_first & in_front
        back = is_last & ~in_front
        head = jnp.where(front, returned.astype(own.dtype), own[:SLOTS])
        tail = jnp.where(back, returned.astype(own.dtype), own[tokens - SLOTS :])
        return jnp.concatenate((head, own[SLOTS : tokens - SLOTS], tail))


    column_sums = jnp.sum(wide(dqkv), axis=0)

    def in_features(part):
        return lax.dynamic_update_slice_in_dim(
            jnp.zeros((features,), jnp.float32),
            column_sums[part * width : (part + 1) * width],
            me * width,
            0,
        )

    grad_qv_b = jnp.concatenate((in_features(0), in_features(2)))

    vectors = (
        grad_qv_b,
        grad_o_b,
        grad_gain_two,
        grad_shift_two,
        grad_cq_b,
        grad_cv_b,
        grad_co_b,
        grad_gain_three,
        grad_shift_three,
        grad_fc1_b,
        grad_fc2_b,
    )
    grad_in_norm, joined, places, sums = finish(
        dqkv,
        normed_all,
        x_own,
        gain_one[None, :],
        qkv_weight,
        part_grad,
        [vector[None, :] for vector in vectors],
        (fc2_stack, stacks[0]),
        stacks[1:],
        (grad_ckv_w,),
        counts,
        4,
    )
    big_grad, qkv_w, fc2_w, fc1_w, co_w, cq_w, o_w, ckv_w = sums
    if not lanes_ok:
        qkv_w = qkv_w.reshape(rows_count, count, -1, 3, width).transpose(0, 2, 3, 1, 4)
        qkv_w = qkv_w.reshape(-1, 3 * features)
    qkv_w, fc1_w, fc2_w, o_w, cq_w, co_w, ckv_w = widen(
        (qkv_w, fc1_w, fc2_w, o_w, cq_w, co_w, ckv_w)
    )
    joined = jnp.sum(joined, axis=0)
    slot_half = after(slot_half, joined)
    theirs = swap(slot_half)
    slot_final, slot_grad = (
        jnp.where(core == 0, slot_half, theirs),
        jnp.where(core == 0, theirs, slot_half),
    )
    layer_out = at_home(final[:tokens], slot_final)[None]
    input_grad = (at_home(grad_resid_one[:tokens], slot_grad) + grad_in_norm)[None]
    big_other = swap(big_grad)
    big_grad = jnp.stack(
        (jnp.where(core == 0, big_grad, big_other), jnp.where(core == 0, big_other, big_grad)), axis=1
    ).reshape(PAGE_PAD, features)
    big_grad = lax.dynamic_slice_in_dim(big_grad, me % sharers * mem_rows, mem_rows, 0)
    memory_grad = jnp.where(own_page == big_page, memory_grad + wide(big_grad), memory_grad)[None]
    pieces = [joined[row, lane : lane + size] for row, lane, size in places]
    g1, s1, qvb, ob, g2, s2, cqb, cvb, cob, g3, s3, f1b, f2b = pieces
    return (
        layer_out,
        input_grad,
        memory_grad,
        g1,
        s1,
        qkv_w,
        qvb,
        o_w,
        ob,
        g2,
        s2,
        cq_w,
        cqb,
        ckv_w,
        cvb,
        co_w,
        cob,
        g3,
        s3,
        fc1_w,
        f1b,
        fc2_w,
        f2b,
    )


def solution(mesh):
    split = P("rows", "seq", None)
    in_specs = (split, split, split, P("rows", None), P("rows", None)) + (P(),) * 20
    vector, matrix = P("seq"), P("seq", None)
    out_specs = (split, split, split) + (
        vector,
        vector,
        matrix,
        vector,
        matrix,
        vector,
        vector,
        vector,
        matrix,
        vector,
        matrix,
        vector,
        matrix,
        vector,
        vector,
        vector,
        matrix,
        vector,
        matrix,
        vector,
    )
    return jax.shard_map(body, mesh=mesh, in_specs=in_specs, out_specs=out_specs, check_vma=False)
```
